256 devices in a mesh: dp: 64 (over z, y, core), mp: 4 (over x).
Axes of the slice: x: 4, y: 4, z: 8, core: 2. Of those that a mesh axis runs over, the one named last changes fastest.
Arguments:
- tokens: bfloat16 [128, 6656], P('dp', 'mp'), may hold values from -6 to 6
- grad_out: bfloat16 [128, 6656], P('dp', 'mp'), may hold values from -1.5 to 1.5
- gate_src: bfloat16 [10240, 6656], P(('dp', 'mp')), may hold values from -0.078125 to 0.078125
- up_src: bfloat16 [10240, 6656], P(('dp', 'mp')), may hold values from -0.078125 to 0.078125
- down_src: bfloat16 [10240, 6656], P(('dp', 'mp')), may hold values from -0.25 to 0.25
- unit_map: int32 [15360], P(('dp', 'mp')), may hold values from 0 to 10239, as said below
- copy_flag: int32 [15360], P(('dp', 'mp')), may hold values from 0 to 1, as said below
Outputs:
- layer_out: bfloat16 [128, 6656], P('dp', 'mp')
- grad_tokens: bfloat16 [128, 6656], P('dp', 'mp')
- grad_gate: bfloat16 [15360, 6656], P(('dp', 'mp'))
- grad_up: bfloat16 [15360, 6656], P(('dp', 'mp'))
- grad_down: bfloat16 [15360, 6656], P(('dp', 'mp'))
The draws below stay inside these ranges and needn't reach their ends.
Inputs may be any that keep to these rules, and one draw needn't show every extreme that they name: `unit_map`: the widened unit j lies on the device of flat index j // 60 along dp+mp, and its source unit lies on a device with the same mp index. Every source unit is the source of one or two widened units. For every pair of devices, at most 3 widened units of the one have their source on the other; every device takes exactly 3 from some device and gives exactly 3 to some device. `copy_flag`: A source unit with one widened unit gives it flag 1; of a source's two widened units at least one has flag 1.
All inputs are finite; a program needn't handle non-finite values.
Results may differ from the reference program's by a relative error of at most 0.0049.
Values may be sent and summed in bfloat16 or wider, within the bound.
A program may use at most 128 MiB of HBM per device.

```python
import jax
import jax.numpy as jnp
from jax import lax

D = 6656
FS = 10240
TOKENS = 128
FW = 15360
FS_DEV = 40
FW_DEV = 60
QUANT = 1
N_DP = 64
N_MP = 4


def mapping_tables(key):
    unit_map = jnp.zeros((FW,), jnp.int32)
    copy_flag = jnp.zeros((FW,), jnp.int32)
    members = FW_DEV // QUANT
    for group in range(N_MP):
        group_key = jax.random.fold_in(key, 7000 + group)
        scores = jax.random.permutation(jax.random.fold_in(group_key, 1), 3 * N_DP).astype(jnp.int32)
        cell = jnp.arange(3 * N_DP, dtype=jnp.int32)
        offset = cell % N_DP
        layer = cell // N_DP
        first = scores[0] % N_DP
        scores = jnp.where(offset == first, layer - 3, scores)
        scores = jnp.where((offset == 1) & (layer == 0), -10, scores)
        scores = jnp.where((offset == N_DP // 2) & (layer == 0), -9, scores)
        scores = jnp.where((offset == N_DP - 1) & (layer == 0), -8, scores)
        order = jnp.argsort(scores)
        chosen = jnp.zeros((3 * N_DP,), jnp.int32).at[order[:members]].set(1)
        multiple = chosen.reshape(3, N_DP).sum(0)
        devices = jnp.arange(N_DP, dtype=jnp.int32)
        counts = QUANT * multiple[(devices[None, :] - devices[:, None]) % N_DP]
        before = jnp.cumsum(counts, axis=1) - counts

        def owner_lists(owner):
            owner_key = jax.random.fold_in(group_key, 100 + owner)
            extra = jax.random.permutation(jax.random.fold_in(owner_key, 1), FS_DEV)[:FS_DEV // 2].astype(jnp.int32)
            local = jnp.concatenate([jnp.arange(FS_DEV, dtype=jnp.int32), extra])
            coins = jax.random.randint(jax.random.fold_in(owner_key, 2), (FS_DEV // 2,), 0, 2).astype(jnp.int32)
            flags = jnp.concatenate([jnp.ones((FS_DEV,), jnp.int32), coins])
            shuffle = jax.random.permutation(jax.random.fold_in(owner_key, 3), FW_DEV)
            return (local[shuffle], flags[shuffle])
        owner_local, owner_flags = jax.vmap(owner_lists)(devices)

        def dest_shuffle(dest):
            return jax.random.permutation(jax.random.fold_in(group_key, 5000 + dest), FW_DEV).astype(jnp.int32)
        shuffles = jax.vmap(dest_shuffle)(devices)
        column = counts.T
        ends = jnp.cumsum(column, axis=1)
        starts = ends - column
        slot = jnp.arange(FW_DEV, dtype=jnp.int32)
        target = jnp.sum((slot[None, :, None] >= ends[:, None, :]).astype(jnp.int32), axis=2)
        position = slot[None, :] - jnp.take_along_axis(starts, target, axis=1)
        place = jnp.take_along_axis(before.T, target, axis=1) + position
        unit_local = shuffles[target, place]
        widened = (target * N_MP + group) * FW_DEV + unit_local
        source = (devices[:, None] * N_MP + group) * FS_DEV + owner_local
        unit_map = unit_map.at[widened.reshape(-1)].set(source.reshape(-1))
        copy_flag = copy_flag.at[widened.reshape(-1)].set(owner_flags.reshape(-1))
    return (unit_map, copy_flag)


def draw_unit_map(key, part):
    return mapping_tables(jax.random.fold_in(key, 11))[0]


def draw_copy_flag(key, part):
    return mapping_tables(jax.random.fold_in(key, 11))[1]


def draw_tokens(key, part):
    noise = jax.random.normal(jax.random.fold_in(key, 21), (TOKENS, D), jnp.float32)
    values = noise
    return jnp.clip(values, -6.0, 6.0).astype(jnp.bfloat16)


def draw_grad_out(key, part):
    noise = jax.random.normal(jax.random.fold_in(key, 31), (TOKENS, D), jnp.float32)
    values = 0.25 * noise
    return jnp.clip(values, -1.5, 1.5).astype(jnp.bfloat16)


def raised(values, key, source, target, parts, factor):
    owner, partner = [(jnp.arange(values.shape[dim]) // (values.shape[dim] // parts)).reshape([-1 if axis == dim else 1 for axis in range(values.ndim)]) for dim in (source, target)]
    chosen = jax.random.permutation(key, parts)[partner]
    strong = (owner == chosen) | (owner == (partner + parts // 2) % parts)
    return jnp.where(strong, factor * values, values)


def block_scale(stream_key, shape, shards, least, top_value):
    loudness, own = 1.0, jax.random.fold_in(stream_key, 6)
    for dim, parts in shards:
        draws = jnp.exp(jax.random.uniform(jax.random.fold_in(own, dim), (parts,), jnp.float32, least / len(shards), top_value / len(shards)))
        loudness = loudness * jnp.repeat(draws, shape[dim] // parts).reshape([-1 if axis == dim else 1 for axis in range(len(shape))])
    return loudness


def scatter_about(key, extent, width, limit, split=(), kind=jnp.bfloat16):
    factor_of = block_scale(key, extent, split, -0.22, 0.18) if split else 1.0
    drawn = jax.random.normal(key, extent, jnp.float32) * width * factor_of
    return jnp.minimum(jnp.maximum(drawn, -limit), limit).astype(kind)


def heavy_noise(own_key, shape, scale, bound, cuts, heavy, held_as=jnp.bfloat16):
    array = scale * jax.random.normal(own_key, shape, jnp.float32)
    if cuts:
        array = array * block_scale(own_key, shape, cuts, -0.22, 0.18)
    return jnp.clip(raised(array, jax.random.fold_in(own_key, 3), *heavy), -bound, bound).astype(held_as)


def setup_inputs(seed: int = 0) -> dict:
    splits = jax.random.split(jax.random.key(seed), 8)
    tokens = draw_tokens(jax.random.fold_in(splits[7], 71), 0)
    grad_out = draw_grad_out(jax.random.fold_in(splits[7], 71), 0)
    gate_src = scatter_about(splits[2], (FS, D), D ** -0.5, 0.078125, ((0, 256),))
    up_src = scatter_about(splits[3], (FS, D), D ** -0.5, 0.078125, ((0, 256),))
    down_src = heavy_noise(splits[4], (FS, D), FS ** -0.5, 0.25, ((0, 256),), (0, 1, 256, 6.0))
    unit_map = draw_unit_map(jax.random.fold_in(splits[7], 71), 0)
    copy_flag = draw_copy_flag(jax.random.fold_in(splits[7], 71), 0)
    return {"tokens": tokens, "grad_out": grad_out, "gate_src": gate_src, "up_src": up_src, "down_src": down_src, "unit_map": unit_map, "copy_flag": copy_flag}


def reference(tokens, grad_out, gate_src, up_src, down_src, unit_map, copy_flag):
    flags = copy_flag.astype(jnp.float32)
    share = jax.ops.segment_sum(flags, unit_map, num_segments=FS)
    scale = flags / share[unit_map]
    dims = (((1,), (1,)), ((), ()))
    pre_gate = lax.dot_general(tokens, gate_src, dims, preferred_element_type=jnp.float32)
    pre_up = lax.dot_general(tokens, up_src, dims, preferred_element_type=jnp.float32)
    sigma = jax.nn.sigmoid(pre_gate)
    active = pre_gate * sigma
    hidden = (active * pre_up).astype(jnp.bfloat16)
    layer_out = jnp.dot(hidden, down_src, preferred_element_type=jnp.float32).astype(jnp.bfloat16)
    grad_hidden = lax.dot_general(grad_out, down_src, dims, preferred_element_type=jnp.float32)
    grad_pre_gate = (grad_hidden * pre_up * (sigma + active * (1.0 - sigma))).astype(jnp.bfloat16)
    grad_pre_up = (grad_hidden * active).astype(jnp.bfloat16)
    grad_tokens = jnp.dot(grad_pre_gate, gate_src, preferred_element_type=jnp.float32)
    grad_tokens = grad_tokens + jnp.dot(grad_pre_up, up_src, preferred_element_type=jnp.float32)
    tdims = (((0,), (0,)), ((), ()))
    gate_rows = lax.dot_general(grad_pre_gate, tokens, tdims, preferred_element_type=jnp.float32).astype(jnp.bfloat16)
    up_rows = lax.dot_general(grad_pre_up, tokens, tdims, preferred_element_type=jnp.float32).astype(jnp.bfloat16)
    down_rows = lax.dot_general(hidden, grad_out, tdims, preferred_element_type=jnp.float32).astype(jnp.bfloat16)
    scale_bf = scale.astype(jnp.bfloat16)[:, None]
    grad_gate = gate_rows[unit_map] * scale_bf
    grad_up = up_rows[unit_map] * scale_bf
    grad_down = down_rows[unit_map]
    return layer_out, grad_tokens.astype(jnp.bfloat16), grad_gate, grad_up, grad_down
```

```python
import functools

import jax
import jax.numpy as jnp
from jax import lax
from jax.experimental import pallas as pl
from jax.experimental.pallas import tpu as pltpu
from jax.sharding import PartitionSpec as P

MESH = pl.DeviceIdType.MESH
BF = jnp.bfloat16
F32 = jnp.float32
I32 = jnp.int32

CORES = 2
CHIPS_Y = 4
SLOTS = 3
LANES = 128
ROWS = 16


def _mod(v, n):
    return lax.rem(v + n, n)


class Geometry:
    def __init__(self, n_dp, n_mp, tokens_dev, cols, src, wide):
        self.Y = CHIPS_Y
        self.YC = CHIPS_Y * CORES
        self.Z = n_dp // self.YC
        self.X = n_mp
        self.dp = n_dp
        self.t = tokens_dev
        self.T = n_dp * tokens_dev
        self.G = self.YC * tokens_dev
        self.cols = cols
        tiles = cols // LANES
        self.a = (tiles // 2) * LANES
        self.b = cols - self.a
        self.D = cols * n_mp
        self.src = src
        self.R = -(-src // 16) * 16
        self.wide = wide
        self.W8 = -(-wide // 8) * 8
        self.long = self.Z // 2
        self.short = self.Z - 1 - self.long


def kernel(g, *refs):
    (tok, gro, gate_h, up_h, down_h, umap, flag, o_out, o_in, gg_h, gu_h, gd_h) = refs[:12]
    (
        s1_src, s1_rcv, asm, codes, own_code,
        buf_a, buf_b,
        w_gate, w_up, w_down, ws,
        lf, lb, lt,
        ss, sel, msg, r1, r2,
        sib_a, sib_b, rcv_a, rcv_b, pa, pb,
        ring_sl, ring_rl, ring_ss, ring_rs, ax_s, ax_r,
        bx_s, bx_r, bz_s, bz_r, sum_b,
        fin_s, fin_r,
        g_gate, g_up, g_down,
        w_sem, o_sem,
        s1_ss, s1_rs, cz_ss, cz_rs, ga_xs, ga_xr, ga_zs, ga_zr, gb_zs, gb_zr, gb_xs, gb_xr,
        sa_s, sa_r, sb_s, sb_r,
        m1_s, m1_r, m2_s, m2_r,
        ra_s, ra_r, rb_s, rb_r,
        rl_s, rl_r, rs_s, rs_r, axx_s, axx_r, bxx_s, bxx_r, bzz_s, bzz_r, f_s, f_r,
    ) = refs[12:]
    X, Y, Z, YC = g.X, g.Y, g.Z, g.YC
    dp = lax.axis_index("dp")
    x = lax.axis_index("mp")
    z = lax.div(dp, YC)
    yc = lax.rem(dp, YC)
    y = lax.div(yc, CORES)
    c = lax.rem(yc, CORES)
    other = 1 - c
    step = 1 - 2 * c

    def at_z(zz):
        return (zz * YC + yc, x)

    def at_x(xx):
        return (dp, xx)

    def at_yc(k):
        return (z * YC + k, x)

    sibling = at_yc(y * CORES + other)
    yc_peers = []
    for dy in range(Y):
        for dc in range(CORES):
            if dy or dc:
                py = _mod(y + dy, Y)
                pc = _mod(c + dc, CORES)
                qy = _mod(y - dy, Y)
                yc_peers.append((dy * CORES + dc, py * CORES + pc, pc, qy * CORES + pc))

    sent = []

    def copy(src, dst, s_sem, r_sem, device):
        return pltpu.make_async_remote_copy(
            src_ref=src, dst_ref=dst, send_sem=s_sem, recv_sem=r_sem,
            device_id=device, device_id_type=MESH,
        )

    def send(src, dst, s_sem, r_sem, device):
        op = copy(src, dst, s_sem, r_sem, device)
        op.start()
        sent.append(op)

    def arrive(dst, s_sem, r_sem, device):
        copy(dst, dst, s_sem, r_sem, device).wait_recv()

    bar = pltpu.get_barrier_semaphore()
    for k in range(1, X):
        pl.semaphore_signal(bar, inc=1, device_id=at_x(_mod(x + k, X)), device_id_type=MESH)
    for k in range(1, Z):
        pl.semaphore_signal(bar, inc=1, device_id=at_z(_mod(z + k, Z)), device_id_type=MESH)
    for _, peer, _, _ in yc_peers:
        pl.semaphore_signal(bar, inc=1, device_id=at_yc(peer), device_id_type=MESH)

    loads = [
        pltpu.make_async_copy(h, v, w_sem.at[i])
        for i, (h, v) in enumerate(((gate_h, w_gate), (up_h, w_up), (down_h, w_down)))
    ]
    for op in loads:
        op.start()

    code = umap[...] * 2 + flag[...]
    own_code[...] = jnp.full(own_code.shape, -1, I32)
    own_code[:, 0:g.wide] = code
    code_row = own_code[...]
    s1_src[0, :, 0:g.cols] = tok[...].astype(F32)
    s1_src[1, :, 0:g.cols] = gro[...].astype(F32)
    for k in range(2):
        s1_src[k, :, g.cols:g.cols + LANES] = jnp.broadcast_to(code_row.astype(F32), (g.t, LANES))
    s1_rcv[yc] = s1_src[c]

    pl.semaphore_wait(bar, (X - 1) + (Z - 1) + len(yc_peers))

    for i, peer, pc, _ in yc_peers:
        send(s1_src.at[pc], s1_rcv.at[yc], s1_ss.at[i], s1_rs.at[i], at_yc(peer))
    for i, _, _, origin in yc_peers:
        arrive(s1_rcv.at[origin], s1_ss.at[i], s1_rs.at[i], sibling)
    for k in range(YC):
        asm[k * g.t:(k + 1) * g.t, :] = s1_rcv[k, :, 0:g.cols]
        codes[z, k:k + 1, :] = s1_rcv[k, 0:1, g.cols:g.cols + LANES]
    block = asm[...].astype(BF)
    buf_a[c, z, x] = block[:, 0:g.a]
    buf_b[c, x, z] = block[:, g.a:g.cols]

    for k in range(1, X):
        send(buf_a.at[c, z, x], buf_a.at[c, z, x], ga_xs.at[k - 1], ga_xr.at[k - 1], at_x(_mod(x + k, X)))
    for k in range(1, Z):
        send(buf_b.at[c, x, z], buf_b.at[c, x, z], gb_zs.at[k - 1], gb_zr.at[k - 1], at_z(_mod(z + k, Z)))
    for k in range(1, Z):
        send(codes.at[z], codes.at[z], cz_ss.at[k - 1], cz_rs.at[k - 1], at_z(_mod(z + k, Z)))

    for op in loads:
        op.wait()
    ws[0, g.R:2 * g.R, :] = jnp.zeros((g.R, g.D), BF)
    if g.R > g.src:
        pad = jnp.zeros((16, g.D), BF)
        ws[0, g.R - 16:g.R, :] = pad
        ws[1, g.R - 16:g.R, :] = pad
        ws[1, 2 * g.R - 16:2 * g.R, :] = pad
    ws[0, 0:g.src, :] = w_down[...]
    ws[1, 0:g.src, :] = w_gate[...]
    ws[1, g.R:g.R + g.src, :] = w_up[...]

    for k in range(1, X):
        arrive(buf_a.at[c, z, _mod(x - k, X)], ga_xs.at[k - 1], ga_xr.at[k - 1], sibling)

    def ring_gather(hop):
        if hop < g.long:
            b = _mod(z - hop * step, Z)
            send(buf_a.at[c, b], buf_a.at[c, b], ga_zs.at[hop], ga_zr.at[hop], at_z(_mod(z + step, Z)))
        if hop < g.short:
            b = _mod(z + hop * step, Z)
            i = g.long + hop
            send(buf_a.at[c, b], buf_a.at[c, b], ga_zs.at[i], ga_zr.at[i], at_z(_mod(z - step, Z)))

    def share_a(b, i):
        send(buf_a.at[c, b], buf_a.at[c, b], sa_s.at[i], sa_r.at[i], sibling)

    ring_gather(0)
    share_a(z, 0)
    for k in range(1, Z):
        arrive(buf_b.at[c, x, _mod(z - k, Z)], gb_zs.at[k - 1], gb_zr.at[k - 1], sibling)
    for k in range(1, X):
        send(buf_b.at[c, x], buf_b.at[c, x], gb_xs.at[k - 1], gb_xr.at[k - 1], at_x(_mod(x + k, X)))
    send(buf_b.at[c, x], buf_b.at[c, x], sb_s.at[0], sb_r.at[0], sibling)
    for hop in range(1, g.long + 1):
        b = _mod(z - hop * step, Z)
        arrive(buf_a.at[c, b], ga_zs.at[hop - 1], ga_zr.at[hop - 1], sibling)
        b2 = _mod(z + hop * step, Z)
        if hop <= g.short:
            arrive(buf_a.at[c, b2], ga_zs.at[g.long + hop - 1], ga_zr.at[g.long + hop - 1], sibling)
        ring_gather(hop)
        share_a(b, hop)
        if hop <= g.short:
            share_a(b2, g.long + hop)

        if hop == 1:
            for k in range(1, Z):
                arrive(codes.at[_mod(z - k, Z)], cz_ss.at[k - 1], cz_rs.at[k - 1], sibling)
            routing(g, codes, ss, sel, dp * X + x)
    for k in range(1, X):
        xx = _mod(x - k, X)
        arrive(buf_b.at[c, xx], gb_xs.at[k - 1], gb_xr.at[k - 1], sibling)
        send(buf_b.at[c, xx], buf_b.at[c, xx], sb_s.at[k], sb_r.at[k], sibling)

    for k in range(g.long + 1):
        arrive(buf_a.at[other, _mod(z + k * step, Z)], sa_s.at[k], sa_r.at[k], sibling)
    for k in range(1, g.short + 1):
        arrive(buf_a.at[other, _mod(z - k * step, Z)], sa_s.at[g.long + k], sa_r.at[g.long + k], sibling)
    for k in range(X):
        arrive(buf_b.at[other, _mod(x - k, X)], sb_s.at[k], sb_r.at[k], sibling)

    nt = (((1,), (1,)), ((), ()))

    def rows_a(array, xx):
        return buf_a[array, :, xx].reshape(g.T, g.a)

    def rows_b(array, xx):
        return buf_b[array, xx].reshape(g.T, g.b)

    pre = jnp.zeros((2 * g.R, g.T), F32)
    gh = jnp.zeros((g.R, g.T), F32)
    for xx in range(X):
        lo, mid, hi = xx * g.cols, xx * g.cols + g.a, (xx + 1) * g.cols
        pre += lax.dot_general(ws[1, :, lo:mid], rows_a(0, xx), nt, preferred_element_type=F32)
        pre += lax.dot_general(ws[1, :, mid:hi], rows_b(0, xx), nt, preferred_element_type=F32)
        gh += lax.dot_general(ws[0, 0:g.R, lo:mid], rows_a(1, xx), nt, preferred_element_type=F32)
        gh += lax.dot_general(ws[0, 0:g.R, mid:hi], rows_b(1, xx), nt, preferred_element_type=F32)
    pre_gate = pre[0:g.src]
    pre_up = pre[g.R:g.R + g.src]
    gh = gh[0:g.src]
    sigma = jax.nn.sigmoid(pre_gate)
    active = pre_gate * sigma
    lf[...] = jnp.zeros(lf.shape, F32)
    lf[0, 0:g.src, :] = active * pre_up
    lf[1, 0:g.src, :] = gh * pre_up * (sigma + active * (1.0 - sigma))
    lf[1, g.R:g.R + g.src, :] = gh * active
    for k in range(2):
        lb[k * LANES:(k + 1) * LANES, :] = lf[k].astype(BF)
        lt[k] = lf[k].T.astype(BF)

    def partial(array, lo, hi):
        return jnp.dot(lt[array][:, 0:2 * g.R], ws[array, :, lo:hi], preferred_element_type=F32)

    for xx in range(X):
        lo = xx * g.cols
        sib_a[xx] = partial(other, lo, lo + g.a).astype(BF).reshape(Z, g.G, g.a)
        send(sib_a.at[xx], rcv_a.at[xx], ra_s.at[xx], ra_r.at[xx], sibling)
    for xx in range(X):
        lo = xx * g.cols
        sib_b[xx] = partial(other, lo + g.a, lo + g.cols).astype(BF).reshape(Z, g.G, g.b)
        send(sib_b.at[xx], rcv_b.at[xx], rb_s.at[xx], rb_r.at[xx], sibling)
    for xx in range(X):
        lo = xx * g.cols
        pa[xx] = partial(c, lo, lo + g.a).reshape(Z, g.G, g.a)
    for xx in range(X):
        arrive(rcv_a.at[xx], ra_s.at[xx], ra_r.at[xx], sibling)

    def own_a(b):
        return pa[:, b] + rcv_a[:, b].astype(F32)

    def ring_reduce(hop):
        if hop < g.long:
            v = own_a(_mod(z + (g.long - hop) * step, Z))
            if hop:
                arrive(ring_rl.at[hop - 1], rl_s.at[hop - 1], rl_r.at[hop - 1], sibling)
                v = v + ring_rl[hop - 1].astype(F32)
            ring_sl[hop] = v.astype(BF)
            send(ring_sl.at[hop], ring_rl.at[hop], rl_s.at[hop], rl_r.at[hop], at_z(_mod(z + step, Z)))
        if hop < g.short:
            v = own_a(_mod(z - (g.short - hop) * step, Z))
            if hop:
                arrive(ring_rs.at[hop - 1], rs_s.at[hop - 1], rs_r.at[hop - 1], sibling)
                v = v + ring_rs[hop - 1].astype(F32)
            ring_ss[hop] = v.astype(BF)
            send(ring_ss.at[hop], ring_rs.at[hop], rs_s.at[hop], rs_r.at[hop], at_z(_mod(z - step, Z)))

    ring_reduce(0)

    picked = jnp.dot(sel[...], lb[...], preferred_element_type=F32).astype(BF)
    msg[...] = picked.reshape(Z, YC, ROWS, g.T)
    r1[z] = msg[z]
    for k in range(1, Z):
        zz = _mod(z + k, Z)
        send(msg.at[zz], r1.at[z], m1_s.at[k - 1], m1_r.at[k - 1], at_z(zz))

    for k in range(X):
        xx = _mod(x + k + 1, X)
        lo = pl.multiple_of(xx * g.cols + g.a, LANES)
        v = jnp.dot(lt[c][:, 0:2 * g.R], ws[c, :, pl.ds(lo, g.b)], preferred_element_type=F32)
        arrive(rcv_b.at[xx], rb_s.at[xx], rb_r.at[xx], sibling)
        v = v.reshape(Z, g.G, g.b) + rcv_b[xx].astype(F32)
        if k < X - 1:
            bx_s[k] = v.astype(BF)
            send(bx_s.at[k], bx_r.at[k], bxx_s.at[k], bxx_r.at[k], at_x(xx))
        else:
            pb[...] = v

    for hop in range(1, g.long):
        ring_reduce(hop)

    for k in range(1, Z):
        arrive(r1.at[_mod(z - k, Z)], m1_s.at[k - 1], m1_r.at[k - 1], sibling)
    r2[yc] = r1[:, yc]
    for i, peer, _, _ in yc_peers:
        send(r1.at[:, peer], r2.at[yc], m2_s.at[i], m2_r.at[i], at_yc(peer))

    for k in range(X - 1):
        arrive(bx_r.at[k], bxx_s.at[k], bxx_r.at[k], sibling)
    total_b = pb[...]
    for k in range(X - 1):
        total_b = total_b + bx_r[k].astype(F32)
    sum_b[...] = total_b
    bz_s[...] = total_b.astype(BF)
    for k in range(1, Z):
        zz = _mod(z + k, Z)
        send(bz_s.at[zz], bz_r.at[k - 1], bzz_s.at[k - 1], bzz_r.at[k - 1], at_z(zz))

    v = own_a(z)
    if g.long:
        arrive(ring_rl.at[g.long - 1], rl_s.at[g.long - 1], rl_r.at[g.long - 1], sibling)
        v = v + ring_rl[g.long - 1].astype(F32)
    if g.short:
        arrive(ring_rs.at[g.short - 1], rs_s.at[g.short - 1], rs_r.at[g.short - 1], sibling)
        v = v + ring_rs[g.short - 1].astype(F32)
    pa[:, z] = v
    ax_s[...] = v.astype(BF)
    for k in range(1, X):
        xx = _mod(x + k, X)
        send(ax_s.at[xx], ax_r.at[k - 1], axx_s.at[k - 1], axx_r.at[k - 1], at_x(xx))

    for i, _, _, origin in yc_peers:
        arrive(r2.at[origin], m2_s.at[i], m2_r.at[i], sibling)
    wide = widened(g, own_code[...], r2)
    g_rows = jnp.concatenate([wide[1], wide[2]], axis=0)
    for xx in range(X):
        for lo, width, rows in (
            (xx * g.cols, g.a, rows_a),
            (xx * g.cols + g.a, g.b, rows_b),
        ):
            both = jnp.dot(g_rows, rows(0, xx), preferred_element_type=F32).astype(BF)
            g_gate[:, lo:lo + width] = both[0:g.wide]
            g_up[:, lo:lo + width] = both[g.W8:g.W8 + g.wide]
            down = jnp.dot(wide[0], rows(1, xx), preferred_element_type=F32).astype(BF)
            g_down[:, lo:lo + width] = down[0:g.wide]
    stores = [
        pltpu.make_async_copy(v, h, o_sem.at[i])
        for i, (v, h) in enumerate(((g_gate, gg_h), (g_up, gu_h), (g_down, gd_h)))
    ]
    for op in stores:
        op.start()

    va = pa[x, z]
    for k in range(1, X):
        arrive(ax_r.at[k - 1], axx_s.at[k - 1], axx_r.at[k - 1], sibling)
        va = va + ax_r[k - 1].astype(F32)
    vb = sum_b[z]
    for k in range(1, Z):
        arrive(bz_r.at[k - 1], bzz_s.at[k - 1], bzz_r.at[k - 1], sibling)
        vb = vb + bz_r[k - 1].astype(F32)
    for k in range(YC):
        fin_s[k, :, 0:g.a] = va[k * g.t:(k + 1) * g.t]
        fin_s[k, :, g.a:g.cols] = vb[k * g.t:(k + 1) * g.t]
    fin_r[yc] = fin_s[yc]
    for i, peer, _, _ in yc_peers:
        send(fin_s.at[peer], fin_r.at[yc], f_s.at[i], f_r.at[i], at_yc(peer))
    for i, _, _, origin in yc_peers:
        arrive(fin_r.at[origin], f_s.at[i], f_r.at[i], sibling)
    for k, out in enumerate((o_out, o_in)):
        total = fin_r[k]
        for yy in range(1, Y):
            total = total + fin_r[yy * CORES + k]
        out[...] = total.astype(BF)

    for op in stores:
        op.wait()
    for op in sent:
        op.wait_send()


def routing(g, codes, ss, sel, flat):
    n, Z, YC = g.dp, g.Z, g.YC
    c = codes[...].reshape(n, LANES).astype(I32)
    local = (c >> 1) - flat * g.src
    owned = (local >= 0) & (local < g.src)
    loc = local.astype(F32)
    flg = (c & 1).astype(F32)
    ownf = jnp.where(owned, 1.0, 0.0)
    before = lax.broadcasted_iota(I32, (LANES, LANES), 0) < lax.broadcasted_iota(I32, (LANES, LANES), 1)
    rank = jnp.dot(ownf.astype(BF), jnp.where(before, 1.0, 0.0).astype(BF), preferred_element_type=F32)
    lane = lax.broadcasted_iota(I32, (n, LANES), 1).astype(F32)
    wide_lane = lax.broadcasted_iota(I32, (n, 2 * LANES), 1).astype(F32)
    picks = []
    share = jnp.zeros((1, LANES), F32)
    for k in range(SLOTS):
        chosen = jnp.where(rank == float(k), ownf, 0.0)
        idx = jnp.sum(chosen * loc, axis=1, keepdims=True)
        has = jnp.sum(chosen, axis=1, keepdims=True)
        fl = jnp.sum(chosen * flg, axis=1, keepdims=True)
        one = jnp.where(lane == idx, has, 0.0)
        share = share + jnp.sum(one * fl, axis=0, keepdims=True)
        picks.append((idx, has, fl, one))
    for k, (idx, has, fl, one) in enumerate(picks):
        total = jnp.sum(one * share, axis=1, keepdims=True)
        scale = jnp.where(has > 0.0, fl / jnp.where(has > 0.0, total, 1.0), 0.0)
        for kind, (offset, factor) in enumerate(
            ((0.0, has), (float(LANES), scale), (float(LANES + g.R), scale))
        ):
            q = k * 3 + kind
            ss[q * n:(q + 1) * n, :] = jnp.where(wide_lane == idx + offset, factor, 0.0).astype(BF)
    q = 3 * SLOTS
    row = lax.broadcasted_iota(I32, (n * ROWS, q * n), 0)
    col = lax.broadcasted_iota(I32, (n * ROWS, q * n), 1)
    spread = jnp.where(col == (row & (ROWS - 1)) * n + (row >> 4), 1.0, 0.0).astype(BF)
    sel[...] = jnp.dot(spread, ss[...], preferred_element_type=F32).astype(BF)


def widened(g, code_row, r2):
    src = (code_row >> 1).astype(F32)
    owner = jnp.floor((src + 0.5) * (1.0 / (g.src * g.X)))
    zz = jnp.floor((owner + 0.5) * (1.0 / g.YC))
    first = ((owner - zz * g.YC) * g.Z + zz) * ROWS
    sub = lax.broadcasted_iota(I32, (LANES, LANES), 0)
    lane = lax.broadcasted_iota(I32, (LANES, LANES), 1)
    owners = jnp.broadcast_to(owner, (LANES, LANES))
    own_col = jnp.sum(jnp.where(sub == lane, owners, 0.0), axis=1, keepdims=True)
    first_col = jnp.sum(
        jnp.where(sub == lane, jnp.broadcast_to(first, (LANES, LANES)), 0.0), axis=1, keepdims=True
    )
    earlier = jnp.sum(
        jnp.where((owners == own_col) & (lane < sub), 1.0, 0.0), axis=1, keepdims=True
    )
    target = (first_col + 3.0 * earlier)[0:g.W8]
    n = g.dp * ROWS
    pos = lax.broadcasted_iota(I32, (g.W8, n), 1).astype(F32)
    columns = r2[...].reshape(n, g.T)
    return [
        jnp.dot(
            jnp.where(pos == target + float(kind), 1.0, 0.0).astype(BF),
            columns, preferred_element_type=F32,
        ).astype(BF)
        for kind in range(3)
    ]


def per_device(tokens, grad_out, gate_src, up_src, down_src, unit_map, copy_flag):
    g = Geometry(
        lax.axis_size("dp"), lax.axis_size("mp"), tokens.shape[0], tokens.shape[1],
        gate_src.shape[0], unit_map.shape[0],
    )
    X, Z, YC = g.X, g.Z, g.YC
    V = pltpu.VMEM
    dma = pltpu.SemaphoreType.DMA

    def pair(n):
        return [dma((max(n, 1),)), dma((max(n, 1),))]

    scratch = [
        V((2, g.t, g.cols + LANES), F32), V((YC, g.t, g.cols + LANES), F32), V((g.G, g.cols), F32),
        V((Z, YC, LANES), F32), V((1, LANES), I32),
        V((2, Z, X, g.G, g.a), BF), V((2, X, Z, g.G, g.b), BF),
        V(gate_src.shape, BF), V(gate_src.shape, BF), V(gate_src.shape, BF), V((2, 2 * g.R, g.D), BF),
        V((2, LANES, g.T), F32), V((2 * LANES, g.T), BF), V((2, g.T, LANES), BF),
        V((3 * SLOTS * g.dp, 2 * LANES), BF), V((g.dp * ROWS, 2 * LANES), BF),
        V((Z, YC, ROWS, g.T), BF), V((Z, YC, ROWS, g.T), BF), V((YC, Z, ROWS, g.T), BF),
        V((X, Z, g.G, g.a), BF), V((X, Z, g.G, g.b), BF), V((X, Z, g.G, g.a), BF), V((X, Z, g.G, g.b), BF),
        V((X, Z, g.G, g.a), F32), V((Z, g.G, g.b), F32),
        V((g.long, X, g.G, g.a), BF), V((g.long, X, g.G, g.a), BF),
        V((max(g.short, 1), X, g.G, g.a), BF), V((max(g.short, 1), X, g.G, g.a), BF),
        V((X, g.G, g.a), BF), V((X - 1, g.G, g.a), BF),
        V((X - 1, Z, g.G, g.b), BF), V((X - 1, Z, g.G, g.b), BF),
        V((Z, g.G, g.b), BF), V((Z - 1, g.G, g.b), BF), V((Z, g.G, g.b), F32),
        V((YC, g.t, g.cols), F32), V((YC, g.t, g.cols), F32),
        V((g.wide, g.D), BF), V((g.wide, g.D), BF), V((g.wide, g.D), BF),
        dma((3,)), dma((3,)),
    ]
    counts = [YC, Z - 1, X - 1, Z - 1, Z - 1, X - 1, Z, X, Z - 1, YC, X, X, g.long, g.short, X - 1, X - 1, Z - 1, YC]
    for n in counts:
        scratch += pair(n)
    vm = pl.BlockSpec(memory_space=pltpu.VMEM)
    anyw = pl.BlockSpec(memory_space=pl.ANY)
    wide_shape = jax.ShapeDtypeStruct((g.wide, g.D), BF)
    tok_shape = jax.ShapeDtypeStruct(tokens.shape, BF)
    macs = 6 * g.T * g.src * g.D + 3 * g.T * g.wide * g.D
    return pl.pallas_call(
        functools.partial(kernel, g),
        out_shape=(tok_shape, tok_shape, wide_shape, wide_shape, wide_shape),
        in_specs=[vm, vm, anyw, anyw, anyw, vm, vm],
        out_specs=(vm, vm, anyw, anyw, anyw),
        scratch_shapes=scratch,
        compiler_params=pltpu.CompilerParams(
            collective_id=0, has_side_effects=True, vmem_limit_bytes=56 * 1024 * 1024
        ),
        cost_estimate=pl.CostEstimate(
            flops=2 * macs, bytes_accessed=3 * 2 * g.D * (g.src + g.wide), transcendentals=g.T * g.src
        ),
        name="widened_layer",
    )(
        tokens, grad_out, gate_src, up_src, down_src,
        unit_map.reshape(1, -1), copy_flag.reshape(1, -1),
    )


def solution(mesh):
    in_specs = (
        P("dp", "mp"),
        P("dp", "mp"),
        P(("dp", "mp"), None),
        P(("dp", "mp"), None),
        P(("dp", "mp"), None),
        P(("dp", "mp")),
        P(("dp", "mp")),
    )
    out_specs = (
        P("dp", "mp"),
        P("dp", "mp"),
        P(("dp", "mp"), None),
        P(("dp", "mp"), None),
        P(("dp", "mp"), None),
    )
    return jax.shard_map(
        per_device, mesh=mesh, in_specs=in_specs, out_specs=out_specs, check_vma=False
    )
```

```python
import functools

import jax
import jax.numpy as jnp
from jax import lax
from jax.experimental import pallas as pl
from jax.experimental.pallas import tpu as pltpu
from jax.sharding import PartitionSpec as P

MESH = pl.DeviceIdType.MESH
BF = jnp.bfloat16
F32 = jnp.float32
I32 = jnp.int32

CORES = 2
CHIPS_Y = 4
SLOTS = 3
LANES = 128


def _mod(v, n):
    return lax.rem(v + n, n)


class Geometry:
    def __init__(self, n_dp, n_mp, tokens_dev, cols, src, wide):
        self.Y = CHIPS_Y
        self.YC = CHIPS_Y * CORES
        self.Z = n_dp // self.YC
        self.X = n_mp
        self.dp = n_dp
        self.t = tokens_dev
        self.T = n_dp * tokens_dev
        self.G = self.YC * tokens_dev
        self.cols = cols
        tiles = cols // LANES
        self.a = (tiles // 2) * LANES
        self.b = cols - self.a
        self.D = cols * n_mp
        self.src = src
        self.R = -(-src // 16) * 16
        self.wide = wide
        self.W8 = -(-wide // 8) * 8
        self.long = self.Z // 2
        self.short = self.Z - 1 - self.long
        self.M = -(-(self.YC * 3 * SLOTS) // 16) * 16


def kernel(g, *refs):
    (tok, gro, gate_h, up_h, down_h, umap, flag, o_out, o_in, gg_h, gu_h, gd_h) = refs[:12]
    (
        s1_src, s1_rcv, asm, codes, own_code,
        buf_a, buf_b,
        w_gate, w_up, w_down, ws,
        lf, lb, lt,
        ss, spread, regroup, sel, msg, r1, m2, r2,
        sib_a, sib_b, rcv_a, rcv_b, pa, pb,
        ring_sl, ring_rl, ring_ss, ring_rs, ax_s, ax_r,
        b1_s, b1_r, b2_s, b2_r, bd_s, bd_r, bz_s, bz_r,
        fin_s, fin_r,
        g_gate, g_up, g_down,
        w_sem, o_sem,
        s1_ss, s1_rs, cz_ss, cz_rs, ga_xs, ga_xr, ga_zs, ga_zr, gb_zs, gb_zr, gb_xs, gb_xr,
        sa_s, sa_r, sb_s, sb_r,
        m1_s, m1_r, m2_s, m2_r,
        ra_s, ra_r, rb_s, rb_r,
        rz_s, rz_r, axx_s, axx_r, bxx_s, bxx_r, bzz_s, bzz_r, f_s, f_r,
    ) = refs[12:]
    X, Y, Z, YC = g.X, g.Y, g.Z, g.YC
    dp = lax.axis_index("dp")
    x = lax.axis_index("mp")
    z = lax.div(dp, YC)
    yc = lax.rem(dp, YC)
    y = lax.div(yc, CORES)
    c = lax.rem(yc, CORES)
    other = 1 - c
    step = 1 - 2 * c

    def at_z(zz):
        return (zz * YC + yc, x)

    def at_x(xx):
        return (dp, xx)

    def at_yc(k):
        return (z * YC + k, x)

    sibling = at_yc(y * CORES + other)
    yc_peers = []
    for dy in range(Y):
        for dc in range(CORES):
            if dy or dc:
                py = _mod(y + dy, Y)
                pc = _mod(c + dc, CORES)
                qy = _mod(y - dy, Y)
                yc_peers.append((dy * CORES + dc, py * CORES + pc, pc, qy * CORES + pc))

    sent = []

    def copy(src, dst, s_sem, r_sem, device):
        return pltpu.make_async_remote_copy(
            src_ref=src, dst_ref=dst, send_sem=s_sem, recv_sem=r_sem,
            device_id=device, device_id_type=MESH,
        )

    def send(src, dst, s_sem, r_sem, device):
        op = copy(src, dst, s_sem, r_sem, device)
        op.start()
        sent.append(op)

    def arrive(dst, s_sem, r_sem, device):
        copy(dst, dst, s_sem, r_sem, device).wait_recv()

    bar = pltpu.get_barrier_semaphore()
    for k in range(1, X):
        pl.semaphore_signal(bar, inc=1, device_id=at_x(_mod(x + k, X)), device_id_type=MESH)
    for k in range(1, Z):
        pl.semaphore_signal(bar, inc=1, device_id=at_z(_mod(z + k, Z)), device_id_type=MESH)
    for _, peer, _, _ in yc_peers:
        pl.semaphore_signal(bar, inc=1, device_id=at_yc(peer), device_id_type=MESH)

    loads = [
        pltpu.make_async_copy(h, v, w_sem.at[i])
        for i, (h, v) in enumerate(((gate_h, w_gate), (up_h, w_up), (down_h, w_down)))
    ]
    for op in loads:
        op.start()

    code = umap[...] * 2 + flag[...]
    own_code[...] = jnp.full(own_code.shape, -1, I32)
    own_code[:, 0:g.wide] = code
    code_row = own_code[...]
    s1_src[0, :, 0:g.cols] = tok[...].astype(F32)
    s1_src[1, :, 0:g.cols] = gro[...].astype(F32)
    for k in range(2):
        s1_src[k, :, g.cols:g.cols + LANES] = jnp.broadcast_to(code_row.astype(F32), (g.t, LANES))
    s1_rcv[yc] = s1_src[c]
    static_matrices(g, spread, regroup)

    pl.semaphore_wait(bar, (X - 1) + (Z - 1) + len(yc_peers))

    for i, peer, pc, _ in yc_peers:
        send(s1_src.at[pc], s1_rcv.at[yc], s1_ss.at[i], s1_rs.at[i], at_yc(peer))
    for i, _, _, origin in yc_peers:
        arrive(s1_rcv.at[origin], s1_ss.at[i], s1_rs.at[i], sibling)
    for k in range(YC):
        asm[k * g.t:(k + 1) * g.t, :] = s1_rcv[k, :, 0:g.cols]
        codes[z, k:k + 1, :] = s1_rcv[k, 0:1, g.cols:g.cols + LANES]
    block = asm[...].astype(BF)
    buf_a[c, z, x] = block[:, 0:g.a]
    buf_b[c, x, z] = block[:, g.a:g.cols]

    right, left = at_z(_mod(z + step, Z)), at_z(_mod(z - step, Z))
    a_cols = [x] + [_mod(x - k, X) for k in range(1, X)]

    def slots_at(hop):
        out = [(hop, _mod(z - hop * step, Z))]
        if 1 <= hop <= g.short:
            out.append((g.long + hop, _mod(z + hop * step, Z)))
        return out

    def a_forward(hop, j):
        if hop < g.long:
            ref = buf_a.at[c, _mod(z - hop * step, Z), a_cols[j]]
            i = hop * X + j
            send(ref, ref, ga_zs.at[i], ga_zr.at[i], right)
        if hop < g.short:
            ref = buf_a.at[c, _mod(z + hop * step, Z), a_cols[j]]
            i = (g.long + hop) * X + j
            send(ref, ref, ga_zs.at[i], ga_zr.at[i], left)

    def a_arrive(hop, j):
        i = (hop - 1) * X + j
        arrive(buf_a.at[c, _mod(z - hop * step, Z), a_cols[j]], ga_zs.at[i], ga_zr.at[i], sibling)
        if hop <= g.short:
            i = (g.long + hop - 1) * X + j
            arrive(buf_a.at[c, _mod(z + hop * step, Z), a_cols[j]], ga_zs.at[i], ga_zr.at[i], sibling)

    def b_forward(hop):
        if hop < g.long:
            ref = buf_b.at[c, x, _mod(z - hop * step, Z)]
            send(ref, ref, gb_zs.at[hop], gb_zr.at[hop], right)
        if hop < g.short:
            ref = buf_b.at[c, x, _mod(z + hop * step, Z)]
            i = g.long + hop
            send(ref, ref, gb_zs.at[i], gb_zr.at[i], left)

    def b_arrive(hop):
        arrive(buf_b.at[c, x, _mod(z - hop * step, Z)], gb_zs.at[hop - 1], gb_zr.at[hop - 1], sibling)
        if hop <= g.short:
            i = g.long + hop - 1
            arrive(buf_b.at[c, x, _mod(z + hop * step, Z)], gb_zs.at[i], gb_zr.at[i], sibling)

    x_up, x_down, x_far = _mod(x + 1, X), _mod(x - 1, X), _mod(x + 2, X)

    def b_across(i, b):
        ref = buf_b.at[c, x, b]
        send(ref, ref, gb_xs.at[3 * i], gb_xr.at[3 * i], at_x(x_up))
        send(ref, ref, gb_xs.at[3 * i + 1], gb_xr.at[3 * i + 1], at_x(x_down))

    def b_pass_on(i, b):
        arrive(buf_b.at[c, x_down, b], gb_xs.at[3 * i], gb_xr.at[3 * i], sibling)
        arrive(buf_b.at[c, x_up, b], gb_xs.at[3 * i + 1], gb_xr.at[3 * i + 1], sibling)
        way = 1 - 2 * lax.rem(b, 2)
        ref = buf_b.at[c, _mod(x - way, X), b]
        send(ref, ref, gb_xs.at[3 * i + 2], gb_xr.at[3 * i + 2], at_x(_mod(x + way, X)))

    def b_share(i, b):
        arrive(buf_b.at[c, x_far, b], gb_xs.at[3 * i + 2], gb_xr.at[3 * i + 2], sibling)
        ref = buf_b.at[c, :, b]
        send(ref, ref, sb_s.at[i], sb_r.at[i], sibling)

    def a_share(i, b):
        ref = buf_a.at[c, b]
        send(ref, ref, sa_s.at[i], sa_r.at[i], sibling)

    b_forward(0)
    for k in range(1, X):
        ref = buf_a.at[c, z, x]
        send(ref, ref, ga_xs.at[k - 1], ga_xr.at[k - 1], at_x(_mod(x + k, X)))
    a_forward(0, 0)
    b_across(0, z)
    for k in range(1, Z):
        send(codes.at[z], codes.at[z], cz_ss.at[k - 1], cz_rs.at[k - 1], at_z(_mod(z + k, Z)))

    for op in loads:
        op.wait()
    ws[0, g.R:2 * g.R, :] = jnp.zeros((g.R, g.D), BF)
    if g.R > g.src:
        pad = jnp.zeros((16, g.D), BF)
        ws[0, g.R - 16:g.R, :] = pad
        ws[1, g.R - 16:g.R, :] = pad
        ws[1, 2 * g.R - 16:2 * g.R, :] = pad
    ws[0, 0:g.src, :] = w_down[...]
    ws[1, 0:g.src, :] = w_gate[...]
    ws[1, g.R:g.R + g.src, :] = w_up[...]

    for k in (1, X - 1, *range(2, X - 1)):
        arrive(buf_a.at[c, z, _mod(x - k, X)], ga_xs.at[k - 1], ga_xr.at[k - 1], sibling)
        a_forward(0, k)
    a_share(0, z)
    for hop in range(1, g.long + 1):
        b_arrive(hop)
        b_forward(hop)
        for i, b in slots_at(hop):
            b_across(i, b)
        for i, b in slots_at(hop - 1):
            b_pass_on(i, b)
        for j in (0, 1, X - 1, *range(2, X - 1)):
            a_arrive(hop, j)
            a_forward(hop, j)
        for i, b in slots_at(hop):
            a_share(i, b)
        for i, b in slots_at(hop - 1):
            b_share(i, b)
        if hop == 1:
            for k in range(1, Z):
                arrive(codes.at[_mod(z - k, Z)], cz_ss.at[k - 1], cz_rs.at[k - 1], sibling)
            routing(g, codes, ss, spread, sel, dp * X + x)
    for i, b in slots_at(g.long):
        b_pass_on(i, b)
    for i, b in slots_at(g.long):
        b_share(i, b)

    for i in range(Z):
        hop = i if i <= g.long else g.long - i
        b = _mod(z + hop * step, Z)
        arrive(buf_a.at[other, b], sa_s.at[i], sa_r.at[i], sibling)
        arrive(buf_b.at[other, :, b], sb_s.at[i], sb_r.at[i], sibling)

    nt = (((1,), (1,)), ((), ()))

    def rows_a(array, xx):
        return buf_a[array, :, xx].reshape(g.T, g.a)

    def rows_b(array, xx):
        return buf_b[array, xx].reshape(g.T, g.b)

    pre = jnp.zeros((2 * g.R, g.T), F32)
    gh = jnp.zeros((g.R, g.T), F32)
    for xx in range(X):
        lo, mid, hi = xx * g.cols, xx * g.cols + g.a, (xx + 1) * g.cols
        pre += lax.dot_general(ws[1, :, lo:mid], rows_a(0, xx), nt, preferred_element_type=F32)
        pre += lax.dot_general(ws[1, :, mid:hi], rows_b(0, xx), nt, preferred_element_type=F32)
        gh += lax.dot_general(ws[0, 0:g.R, lo:mid], rows_a(1, xx), nt, preferred_element_type=F32)
        gh += lax.dot_general(ws[0, 0:g.R, mid:hi], rows_b(1, xx), nt, preferred_element_type=F32)
    pre_gate = pre[0:g.src]
    pre_up = pre[g.R:g.R + g.src]
    gh = gh[0:g.src]
    sigma = jax.nn.sigmoid(pre_gate)
    active = pre_gate * sigma
    lf[...] = jnp.zeros(lf.shape, F32)
    lf[0, 0:g.src, :] = active * pre_up
    lf[1, 0:g.src, :] = gh * pre_up * (sigma + active * (1.0 - sigma))
    lf[1, g.R:g.R + g.src, :] = gh * active
    for k in range(2):
        lb[k * LANES:(k + 1) * LANES, :] = lf[k].astype(BF)
        lt[k] = lf[k].T.astype(BF)

    def partial(array, lo, hi):
        return jnp.dot(lt[array][:, 0:2 * g.R], ws[array, :, lo:hi], preferred_element_type=F32)

    def partial_b(array, xx):
        lo = pl.multiple_of(xx * g.cols + g.a, LANES)
        v = jnp.dot(lt[array][:, 0:2 * g.R], ws[array, :, pl.ds(lo, g.b)], preferred_element_type=F32)
        return v.reshape(Z, g.G, g.b)

    def own_a(b, xx):
        return pa[xx, b] + rcv_a[xx, b].astype(F32)

    def reduce_a(hop, xx):
        if hop < g.long:
            v = own_a(_mod(z + (g.long - hop) * step, Z), xx)
            if hop:
                i = (hop - 1) * X + xx
                arrive(ring_rl.at[hop - 1, xx], rz_s.at[i], rz_r.at[i], sibling)
                v = v + ring_rl[hop - 1, xx].astype(F32)
            ring_sl[hop, xx] = v.astype(BF)
            i = hop * X + xx
            send(ring_sl.at[hop, xx], ring_rl.at[hop, xx], rz_s.at[i], rz_r.at[i], right)
        if hop < g.short:
            v = own_a(_mod(z - (g.short - hop) * step, Z), xx)
            if hop:
                i = (g.long + hop - 1) * X + xx
                arrive(ring_rs.at[hop - 1, xx], rz_s.at[i], rz_r.at[i], sibling)
                v = v + ring_rs[hop - 1, xx].astype(F32)
            ring_ss[hop, xx] = v.astype(BF)
            i = (g.long + hop) * X + xx
            send(ring_ss.at[hop, xx], ring_rs.at[hop, xx], rz_s.at[i], rz_r.at[i], left)

    b_long = [(h, _mod(z + (g.long - h) * step, Z)) for h in range(g.long)]
    b_short = [(g.long + h, _mod(z - (g.short - h) * step, Z)) for h in range(g.short)]
    b_own = (Z - 1, z)
    b_order = []
    for h in range(g.long):
        b_order.append(b_long[h])
        if h < g.short:
            b_order.append(b_short[h])
    b_order.append(b_own)

    def way_of(b):
        return 1 - 2 * lax.rem(b, 2)

    def b_first(i, b):
        b1_s[i] = pb[x_far, b].astype(BF)
        send(b1_s.at[i], b1_r.at[i], bxx_s.at[3 * i], bxx_r.at[3 * i], at_x(_mod(x + way_of(b), X)))

    def b_direct(i, b):
        to = _mod(x - way_of(b), X)
        bd_s[i] = pb[to, b].astype(BF)
        send(bd_s.at[i], bd_r.at[i], bxx_s.at[3 * i + 1], bxx_r.at[3 * i + 1], at_x(to))

    def b_second(i, b):
        to = _mod(x + way_of(b), X)
        arrive(b1_r.at[i], bxx_s.at[3 * i], bxx_r.at[3 * i], sibling)
        b2_s[i] = (pb[to, b] + b1_r[i].astype(F32)).astype(BF)
        send(b2_s.at[i], b2_r.at[i], bxx_s.at[3 * i + 2], bxx_r.at[3 * i + 2], at_x(to))

    def b_sum(i, b):
        arrive(bd_r.at[i], bxx_s.at[3 * i + 1], bxx_r.at[3 * i + 1], sibling)
        arrive(b2_r.at[i], bxx_s.at[3 * i + 2], bxx_r.at[3 * i + 2], sibling)
        return pb[x, b] + bd_r[i].astype(F32) + b2_r[i].astype(F32)

    def reduce_b(hop):
        for chain, to, n in ((b_long, right, g.long), (b_short, left, g.short)):
            if hop < n:
                i, b = chain[hop]
                v = b_sum(i, b)
                if hop:
                    arrive(bz_r.at[i - 1], bzz_s.at[i - 1], bzz_r.at[i - 1], sibling)
                    v = v + bz_r[i - 1].astype(F32)
                bz_s[i] = v.astype(BF)
                send(bz_s.at[i], bz_r.at[i], bzz_s.at[i], bzz_r.at[i], to)

    for xx in range(X):
        lo = xx * g.cols
        sib_a[xx] = partial(other, lo, lo + g.a).astype(BF).reshape(Z, g.G, g.a)
        send(sib_a.at[xx], rcv_a.at[xx], ra_s.at[xx], ra_r.at[xx], sibling)
    for k in range(X):
        xx = _mod(x + (2, 1, X - 1, 0)[k], X)
        sib_b[k] = partial_b(other, xx).astype(BF)
        send(sib_b.at[k], rcv_b.at[k], rb_s.at[k], rb_r.at[k], sibling)
    for xx in range(X):
        lo = xx * g.cols
        pa[xx] = partial(c, lo, lo + g.a).reshape(Z, g.G, g.a)
        arrive(rcv_a.at[xx], ra_s.at[xx], ra_r.at[xx], sibling)
        reduce_a(0, xx)
    for k in range(X):
        xx = _mod(x + (2, 1, X - 1, 0)[k], X)
        v = partial_b(c, xx)
        arrive(rcv_b.at[k], rb_s.at[k], rb_r.at[k], sibling)
        pb[xx] = v + rcv_b[k].astype(F32)
        if k == 0:
            for i, b in b_order:
                b_first(i, b)
        if k == 2:
            for i, b in b_order:
                b_direct(i, b)

    picked = jnp.dot(sel[...], lb[...], preferred_element_type=F32).astype(BF)
    msg[...] = picked.reshape(Z, g.M, g.T)
    r1[z] = msg[z]

    for i, b in b_order[0:Z // 2]:
        b_second(i, b)
    for xx in range(X):
        reduce_a(1, xx)
    for k in range(1, Z):
        zz = _mod(z + k, Z)
        send(msg.at[zz], r1.at[z], m1_s.at[k - 1], m1_r.at[k - 1], at_z(zz))
    for i, b in b_order[Z // 2:]:
        b_second(i, b)
    reduce_b(0)
    for xx in range(X):
        reduce_a(2, xx)
    reduce_b(1)
    for xx in range(X):
        reduce_a(3, xx)
    for k in range(1, Z):
        arrive(r1.at[_mod(z - k, Z)], m1_s.at[k - 1], m1_r.at[k - 1], sibling)
    m2[...] = jnp.dot(
        regroup[...], r1[...].reshape(Z * g.M, g.T), preferred_element_type=F32
    ).astype(BF).reshape(YC, g.M, g.T)
    r2[yc] = m2[yc]
    for i, peer, _, _ in yc_peers:
        send(m2.at[peer], r2.at[yc], m2_s.at[i], m2_r.at[i], at_yc(peer))
    reduce_b(2)
    reduce_b(3)

    for xx in range(X):
        v = own_a(z, xx)
        i = (g.long - 1) * X + xx
        arrive(ring_rl.at[g.long - 1, xx], rz_s.at[i], rz_r.at[i], sibling)
        v = v + ring_rl[g.long - 1, xx].astype(F32)
        i = (g.long + g.short - 1) * X + xx
        arrive(ring_rs.at[g.short - 1, xx], rz_s.at[i], rz_r.at[i], sibling)
        v = v + ring_rs[g.short - 1, xx].astype(F32)
        pa[xx, z] = v
        ax_s[xx] = v.astype(BF)
    for k in range(1, X):
        xx = _mod(x + k, X)
        send(ax_s.at[xx], ax_r.at[k - 1], axx_s.at[k - 1], axx_r.at[k - 1], at_x(xx))

    for i, _, _, origin in yc_peers:
        arrive(r2.at[origin], m2_s.at[i], m2_r.at[i], sibling)
    wide = widened(g, own_code[...], r2)
    g_rows = jnp.concatenate([wide[1], wide[2]], axis=0)
    for xx in range(X):
        for lo, width, rows in (
            (xx * g.cols, g.a, rows_a),
            (xx * g.cols + g.a, g.b, rows_b),
        ):
            both = jnp.dot(g_rows, rows(0, xx), preferred_element_type=F32).astype(BF)
            g_gate[:, lo:lo + width] = both[0:g.wide]
            g_up[:, lo:lo + width] = both[g.W8:g.W8 + g.wide]
            down = jnp.dot(wide[0], rows(1, xx), preferred_element_type=F32).astype(BF)
            g_down[:, lo:lo + width] = down[0:g.wide]
    stores = [
        pltpu.make_async_copy(v, h, o_sem.at[i])
        for i, (v, h) in enumerate(((g_gate, gg_h), (g_up, gu_h), (g_down, gd_h)))
    ]
    for op in stores:
        op.start()

    va = pa[x, z]
    for k in range(1, X):
        arrive(ax_r.at[k - 1], axx_s.at[k - 1], axx_r.at[k - 1], sibling)
        va = va + ax_r[k - 1].astype(F32)
    vb = b_sum(*b_own)
    for i in (g.long - 1, g.long + g.short - 1):
        arrive(bz_r.at[i], bzz_s.at[i], bzz_r.at[i], sibling)
        vb = vb + bz_r[i].astype(F32)
    for k in range(YC):
        fin_s[k, :, 0:g.a] = va[k * g.t:(k + 1) * g.t]
        fin_s[k, :, g.a:g.cols] = vb[k * g.t:(k + 1) * g.t]
    fin_r[yc] = fin_s[yc]
    for i, peer, _, _ in yc_peers:
        send(fin_s.at[peer], fin_r.at[yc], f_s.at[i], f_r.at[i], at_yc(peer))
    for i, _, _, origin in yc_peers:
        arrive(fin_r.at[origin], f_s.at[i], f_r.at[i], sibling)
    for k, out in enumerate((o_out, o_in)):
        total = fin_r[k]
        for yy in range(1, Y):
            total = total + fin_r[yy * CORES + k]
        out[...] = total.astype(BF)

    for op in stores:
        op.wait()
    for op in sent:
        op.wait_send()


def routing(g, codes, ss, spread, sel, flat):
    n, Z, YC = g.dp, g.Z, g.YC
    c = codes[...].reshape(n, LANES).astype(I32)
    local = (c >> 1) - flat * g.src
    owned = (local >= 0) & (local < g.src)
    loc = local.astype(F32)
    flg = (c & 1).astype(F32)
    ownf = jnp.where(owned, 1.0, 0.0)
    before = lax.broadcasted_iota(I32, (LANES, LANES), 0) < lax.broadcasted_iota(I32, (LANES, LANES), 1)
    rank = jnp.dot(ownf.astype(BF), jnp.where(before, 1.0, 0.0).astype(BF), preferred_element_type=F32)
    lane = lax.broadcasted_iota(I32, (n, LANES), 1).astype(F32)
    wide_lane = lax.broadcasted_iota(I32, (n, 2 * LANES), 1).astype(F32)
    picks = []
    share = jnp.zeros((1, LANES), F32)
    for k in range(SLOTS):
        chosen = jnp.where(rank == float(k), ownf, 0.0)
        idx = jnp.sum(chosen * loc, axis=1, keepdims=True)
        has = jnp.sum(chosen, axis=1, keepdims=True)
        fl = jnp.sum(chosen * flg, axis=1, keepdims=True)
        one = jnp.where(lane == idx, has, 0.0)
        share = share + jnp.sum(one * fl, axis=0, keepdims=True)
        picks.append((idx, has, fl, one))
    for k, (idx, has, fl, one) in enumerate(picks):
        total = jnp.sum(one * share, axis=1, keepdims=True)
        scale = jnp.where(has > 0.0, fl / jnp.where(has > 0.0, total, 1.0), 0.0)
        for kind, (offset, factor) in enumerate(
            ((0.0, has), (float(LANES), scale), (float(LANES + g.R), scale))
        ):
            q = k * 3 + kind
            ss[q * n:(q + 1) * n, :] = jnp.where(wide_lane == idx + offset, factor, 0.0).astype(BF)
    sel[...] = jnp.dot(spread[...], ss[...], preferred_element_type=F32).astype(BF)


def static_matrices(g, spread, regroup):
    per = 3 * SLOTS
    n, rows = g.dp, g.Z * g.M

    def parts(groups):
        row = lax.broadcasted_iota(I32, (rows, 1), 0).astype(F32)
        block = jnp.floor((row + 0.5) * (1.0 / g.M))
        rest = row - block * g.M
        inner = jnp.floor((rest + 0.5) * (1.0 / per))
        return block, inner, rest - inner * per, rest < float(groups * per)

    block, inner, q, valid = parts(g.YC)
    want = jnp.where(valid, q * n + block * g.YC + inner, -1.0)
    col = lax.broadcasted_iota(I32, (rows, per * n), 1).astype(F32)
    spread[...] = jnp.where(col == want, 1.0, 0.0).astype(BF)
    want = jnp.where(valid, inner * g.M + block * per + q, -1.0)
    col = lax.broadcasted_iota(I32, (rows, rows), 1).astype(F32)
    regroup[...] = jnp.where(col == want, 1.0, 0.0).astype(BF)


def widened(g, code_row, r2):
    src = (code_row >> 1).astype(F32)
    owner = jnp.floor((src + 0.5) * (1.0 / (g.src * g.X)))
    zz = jnp.floor((owner + 0.5) * (1.0 / g.YC))
    first = (owner - zz * g.YC) * g.M + zz * (3.0 * SLOTS)
    sub = lax.broadcasted_iota(I32, (LANES, LANES), 0)
    lane = lax.broadcasted_iota(I32, (LANES, LANES), 1)
    owners = jnp.broadcast_to(owner, (LANES, LANES))
    own_col = jnp.sum(jnp.where(sub == lane, owners, 0.0), axis=1, keepdims=True)
    first_col = jnp.sum(
        jnp.where(sub == lane, jnp.broadcast_to(first, (LANES, LANES)), 0.0), axis=1, keepdims=True
    )
    earlier = jnp.sum(
        jnp.where((owners == own_col) & (lane < sub), 1.0, 0.0), axis=1, keepdims=True
    )
    target = (first_col + 3.0 * earlier)[0:g.W8]
    n = g.YC * g.M
    pos = lax.broadcasted_iota(I32, (g.W8, n), 1).astype(F32)
    columns = r2[...].reshape(n, g.T)
    return [
        jnp.dot(
            jnp.where(pos == target + float(kind), 1.0, 0.0).astype(BF),
            columns, preferred_element_type=F32,
        ).astype(BF)
        for kind in range(3)
    ]


def hand_over(n, *refs):
    sem = refs[2 * n]
    ops = [pltpu.make_async_copy(refs[i], refs[n + i], sem.at[i]) for i in range(n)]
    for op in ops:
        op.start()
    for op in ops:
        op.wait()


def per_device(tokens, grad_out, gate_src, up_src, down_src, unit_map, copy_flag):
    g = Geometry(
        lax.axis_size("dp"), lax.axis_size("mp"), tokens.shape[0], tokens.shape[1],
        gate_src.shape[0], unit_map.shape[0],
    )
    X, Z, YC = g.X, g.Z, g.YC
    V = pltpu.VMEM
    dma = pltpu.SemaphoreType.DMA

    def pair(n):
        return [dma((max(n, 1),)), dma((max(n, 1),))]

    scratch = [
        V((2, g.t, g.cols + LANES), F32), V((YC, g.t, g.cols + LANES), F32), V((g.G, g.cols), F32),
        V((Z, YC, LANES), F32), V((1, LANES), I32),
        V((2, Z, X, g.G, g.a), BF), V((2, X, Z, g.G, g.b), BF),
        V(gate_src.shape, BF), V(gate_src.shape, BF), V(gate_src.shape, BF), V((2, 2 * g.R, g.D), BF),
        V((2, LANES, g.T), F32), V((2 * LANES, g.T), BF), V((2, g.T, LANES), BF),
        V((3 * SLOTS * g.dp, 2 * LANES), BF), V((Z * g.M, 3 * SLOTS * g.dp), BF), V((Z * g.M, Z * g.M), BF),
        V((Z * g.M, 2 * LANES), BF),
        V((Z, g.M, g.T), BF), V((Z, g.M, g.T), BF), V((YC, g.M, g.T), BF), V((YC, g.M, g.T), BF),
        V((X, Z, g.G, g.a), BF), V((X, Z, g.G, g.b), BF), V((X, Z, g.G, g.a), BF), V((X, Z, g.G, g.b), BF),
        V((X, Z, g.G, g.a), F32), V((X, Z, g.G, g.b), F32),
        V((g.long, X, g.G, g.a), BF), V((g.long, X, g.G, g.a), BF),
        V((g.short, X, g.G, g.a), BF), V((g.short, X, g.G, g.a), BF),
        V((X, g.G, g.a), BF), V((X - 1, g.G, g.a), BF),
        *[V((Z, g.G, g.b), BF) for _ in range(6)],
        V((Z - 1, g.G, g.b), BF), V((Z - 1, g.G, g.b), BF),
        V((YC, g.t, g.cols), F32), V((YC, g.t, g.cols), F32),
        V((g.wide, g.D), BF), V((g.wide, g.D), BF), V((g.wide, g.D), BF),
        dma((3,)), dma((3,)),
    ]
    counts = [
        YC, Z - 1, X - 1, (Z - 1) * X, Z - 1, 3 * Z, Z, Z, Z - 1, YC, X, X,
        (Z - 1) * X, X - 1, 3 * Z, Z - 1, YC,
    ]
    for n in counts:
        scratch += pair(n)
    vm = pl.BlockSpec(memory_space=pltpu.VMEM)
    anyw = pl.BlockSpec(memory_space=pl.ANY)
    wide_shape = jax.ShapeDtypeStruct((g.wide, g.D), BF)
    tok_shape = jax.ShapeDtypeStruct(tokens.shape, BF)
    macs = 6 * g.T * g.src * g.D + 3 * g.T * g.wide * g.D
    results = pl.pallas_call(
        functools.partial(kernel, g),
        out_shape=(tok_shape, tok_shape, wide_shape, wide_shape, wide_shape),
        in_specs=[vm, vm, anyw, anyw, anyw, vm, vm],
        out_specs=(vm, vm, anyw, anyw, anyw),
        scratch_shapes=scratch,
        compiler_params=pltpu.CompilerParams(
            collective_id=0, has_side_effects=True, vmem_limit_bytes=56 * 1024 * 1024
        ),
        cost_estimate=pl.CostEstimate(
            flops=2 * macs, bytes_accessed=3 * 2 * g.D * (g.src + g.wide), transcendentals=g.T * g.src
        ),
        name="widened_layer",
    )(
        tokens, grad_out, gate_src, up_src, down_src,
        unit_map.reshape(1, -1), copy_flag.reshape(1, -1),
    )
    return pl.pallas_call(
        functools.partial(hand_over, len(results)),
        out_shape=tuple(jax.ShapeDtypeStruct(r.shape, r.dtype) for r in results),
        in_specs=[anyw] * len(results),
        out_specs=(anyw,) * len(results),
        scratch_shapes=[dma((len(results),))],
        cost_estimate=pl.CostEstimate(flops=0, bytes_accessed=12 * g.wide * g.D, transcendentals=0),
        name="hand_over",
    )(*results)


def solution(mesh):
    in_specs = (
        P("dp", "mp"),
        P("dp", "mp"),
        P(("dp", "mp"), None),
        P(("dp", "mp"), None),
        P(("dp", "mp"), None),
        P(("dp", "mp")),
        P(("dp", "mp")),
    )
    out_specs = (
        P("dp", "mp"),
        P("dp", "mp"),
        P(("dp", "mp"), None),
        P(("dp", "mp"), None),
        P(("dp", "mp"), None),
    )
    return jax.shard_map(
        per_device, mesh=mesh, in_specs=in_specs, out_specs=out_specs, check_vma=False
    )
```

```python
import functools

import jax
import jax.numpy as jnp
from jax import lax
from jax.experimental import pallas as pl
from jax.experimental.pallas import tpu as pltpu
from jax.sharding import PartitionSpec as P

MESH = pl.DeviceIdType.MESH
BF = jnp.bfloat16
F32 = jnp.float32
I32 = jnp.int32

CORES = 2
CHIPS_Y = 4
SLOTS = 3
LANES = 128


def _mod(v, n):
    return lax.rem(v + n, n)


class Geometry:
    def __init__(self, n_dp, n_mp, tokens_dev, cols, src, wide):
        self.Y = CHIPS_Y
        self.YC = CHIPS_Y * CORES
        self.Z = n_dp // self.YC
        self.X = n_mp
        self.dp = n_dp
        self.t = tokens_dev
        self.T = n_dp * tokens_dev
        self.G = self.YC * tokens_dev
        self.cols = cols
        tiles = cols // LANES
        self.a = (tiles // 2) * LANES
        self.b = cols - self.a
        self.D = cols * n_mp
        self.src = src
        self.R = -(-src // 16) * 16
        self.wide = wide
        self.W8 = -(-wide // 8) * 8
        self.long = self.Z // 2
        self.short = self.Z - 1 - self.long
        self.M = -(-(self.YC * 3 * SLOTS) // 16) * 16


def kernel(g, *refs):
    (tok, gro, gate_h, up_h, down_h, umap, flag, o_out, o_in, gg_h, gu_h, gd_h) = refs[:12]
    (
        s1_src, s1_rcv, asm, codes, own_code,
        buf_a, buf_b,
        w_gate, w_up, w_down, ws,
        lf, lb, lt,
        ss, spread, regroup, sel, msg, r1, m2, r2,
        sib_a, sib_b, rcv_a, rcv_b, pa, pb,
        ring_sl, ring_rl, ring_ss, ring_rs, ax_s, ax_r,
        b1_s, b1_r, b2_s, b2_r, bd_s, bd_r, bz_s, bz_r,
        fin_s, fin_r,
        g_gate, g_up, g_down,
        w_sem, o_sem,
        s1_ss, s1_rs, cz_ss, cz_rs, ga_xs, ga_xr, ga_zs, ga_zr, gb_zs, gb_zr, gb_xs, gb_xr,
        sa_s, sa_r, sb_s, sb_r,
        m1_s, m1_r, m2_s, m2_r,
        ra_s, ra_r, rb_s, rb_r,
        rz_s, rz_r, axx_s, axx_r, bxx_s, bxx_r, bzz_s, bzz_r, f_s, f_r,
    ) = refs[12:]
    X, Y, Z, YC = g.X, g.Y, g.Z, g.YC
    dp = lax.axis_index("dp")
    x = lax.axis_index("mp")
    z = lax.div(dp, YC)
    yc = lax.rem(dp, YC)
    y = lax.div(yc, CORES)
    c = lax.rem(yc, CORES)
    other = 1 - c
    step = 1 - 2 * c

    def at_z(zz):
        return (zz * YC + yc, x)

    def at_x(xx):
        return (dp, xx)

    def at_yc(k):
        return (z * YC + k, x)

    sibling = at_yc(y * CORES + other)
    yc_peers = []
    for dy in range(Y):
        for dc in range(CORES):
            if dy or dc:
                py = _mod(y + dy, Y)
                pc = _mod(c + dc, CORES)
                qy = _mod(y - dy, Y)
                yc_peers.append((dy * CORES + dc, py * CORES + pc, pc, qy * CORES + pc))

    sent = []

    def copy(src, dst, s_sem, r_sem, device):
        return pltpu.make_async_remote_copy(
            src_ref=src, dst_ref=dst, send_sem=s_sem, recv_sem=r_sem,
            device_id=device, device_id_type=MESH,
        )

    def send(src, dst, s_sem, r_sem, device):
        op = copy(src, dst, s_sem, r_sem, device)
        op.start()
        sent.append(op)

    def arrive(dst, s_sem, r_sem, device):
        copy(dst, dst, s_sem, r_sem, device).wait_recv()

    bar = pltpu.get_barrier_semaphore()
    for k in range(1, X):
        pl.semaphore_signal(bar, inc=1, device_id=at_x(_mod(x + k, X)), device_id_type=MESH)
    for k in range(1, Z):
        pl.semaphore_signal(bar, inc=1, device_id=at_z(_mod(z + k, Z)), device_id_type=MESH)
    for _, peer, _, _ in yc_peers:
        pl.semaphore_signal(bar, inc=1, device_id=at_yc(peer), device_id_type=MESH)

    loads = [
        pltpu.make_async_copy(h, v, w_sem.at[i])
        for i, (h, v) in enumerate(((gate_h, w_gate), (up_h, w_up), (down_h, w_down)))
    ]
    for op in loads:
        op.start()

    code = umap[...] * 2 + flag[...]
    own_code[...] = jnp.full(own_code.shape, -1, I32)
    own_code[:, 0:g.wide] = code
    code_row = own_code[...]
    s1_src[0, :, 0:g.cols] = tok[...].astype(F32)
    s1_src[1, :, 0:g.cols] = gro[...].astype(F32)
    for k in range(2):
        s1_src[k, :, g.cols:g.cols + LANES] = jnp.broadcast_to(code_row.astype(F32), (g.t, LANES))
    s1_rcv[yc] = s1_src[c]

    pl.semaphore_wait(bar, (X - 1) + (Z - 1) + len(yc_peers))

    for i, peer, pc, _ in yc_peers:
        send(s1_src.at[pc], s1_rcv.at[yc], s1_ss.at[i], s1_rs.at[i], at_yc(peer))
    for i, _, _, origin in yc_peers:
        arrive(s1_rcv.at[origin], s1_ss.at[i], s1_rs.at[i], sibling)
    for k in range(YC):
        asm[k * g.t:(k + 1) * g.t, :] = s1_rcv[k, :, 0:g.cols]
        codes[z, k:k + 1, :] = s1_rcv[k, 0:1, g.cols:g.cols + LANES]
    block = asm[...].astype(BF)
    buf_a[c, z, x] = block[:, 0:g.a]
    buf_b[c, x, z] = block[:, g.a:g.cols]

    right, left = at_z(_mod(z + step, Z)), at_z(_mod(z - step, Z))
    a_cols = [x] + [_mod(x - k, X) for k in range(1, X)]

    def slots_at(hop):
        out = [(hop, _mod(z - hop * step, Z))]
        if 1 <= hop <= g.short:
            out.append((g.long + hop, _mod(z + hop * step, Z)))
        return out

    def a_forward(hop, j):
        if hop < g.long:
            ref = buf_a.at[c, _mod(z - hop * step, Z), a_cols[j]]
            i = hop * X + j
            send(ref, ref, ga_zs.at[i], ga_zr.at[i], right)
        if hop < g.short:
            ref = buf_a.at[c, _mod(z + hop * step, Z), a_cols[j]]
            i = (g.long + hop) * X + j
            send(ref, ref, ga_zs.at[i], ga_zr.at[i], left)

    def a_arrive(hop, j):
        i = (hop - 1) * X + j
        arrive(buf_a.at[c, _mod(z - hop * step, Z), a_cols[j]], ga_zs.at[i], ga_zr.at[i], sibling)
        if hop <= g.short:
            i = (g.long + hop - 1) * X + j
            arrive(buf_a.at[c, _mod(z + hop * step, Z), a_cols[j]], ga_zs.at[i], ga_zr.at[i], sibling)

    def b_forward(hop):
        if hop < g.long:
            ref = buf_b.at[c, x, _mod(z - hop * step, Z)]
            send(ref, ref, gb_zs.at[hop], gb_zr.at[hop], right)
        if hop < g.short:
            ref = buf_b.at[c, x, _mod(z + hop * step, Z)]
            i = g.long + hop
            send(ref, ref, gb_zs.at[i], gb_zr.at[i], left)

    def b_arrive(hop):
        arrive(buf_b.at[c, x, _mod(z - hop * step, Z)], gb_zs.at[hop - 1], gb_zr.at[hop - 1], sibling)
        if hop <= g.short:
            i = g.long + hop - 1
            arrive(buf_b.at[c, x, _mod(z + hop * step, Z)], gb_zs.at[i], gb_zr.at[i], sibling)

    x_up, x_down, x_far = _mod(x + 1, X), _mod(x - 1, X), _mod(x + 2, X)

    def b_across(i, b, last=False):
        ref = buf_b.at[c, x, b]
        if last:
            send(ref, ref, gb_xs.at[3 * i + 2], gb_xr.at[3 * i + 2], at_x(x_far))
        send(ref, ref, gb_xs.at[3 * i], gb_xr.at[3 * i], at_x(x_up))
        send(ref, ref, gb_xs.at[3 * i + 1], gb_xr.at[3 * i + 1], at_x(x_down))

    def b_beside(i, b):
        arrive(buf_b.at[c, x_down, b], gb_xs.at[3 * i], gb_xr.at[3 * i], sibling)
        arrive(buf_b.at[c, x_up, b], gb_xs.at[3 * i + 1], gb_xr.at[3 * i + 1], sibling)

    def b_pass_on(i, b):
        b_beside(i, b)
        way = 1 - 2 * lax.rem(b, 2)
        ref = buf_b.at[c, _mod(x - way, X), b]
        send(ref, ref, gb_xs.at[3 * i + 2], gb_xr.at[3 * i + 2], at_x(_mod(x + way, X)))

    def b_share(i, b):
        arrive(buf_b.at[c, x_far, b], gb_xs.at[3 * i + 2], gb_xr.at[3 * i + 2], sibling)
        ref = buf_b.at[c, :, b]
        send(ref, ref, sb_s.at[i], sb_r.at[i], sibling)

    def a_share(i, b):
        ref = buf_a.at[c, b]
        send(ref, ref, sa_s.at[i], sa_r.at[i], sibling)

    b_forward(0)
    for k in range(1, X):
        ref = buf_a.at[c, z, x]
        send(ref, ref, ga_xs.at[k - 1], ga_xr.at[k - 1], at_x(_mod(x + k, X)))
    a_forward(0, 0)
    b_across(0, z)
    for k in range(1, Z):
        send(codes.at[z], codes.at[z], cz_ss.at[k - 1], cz_rs.at[k - 1], at_z(_mod(z + k, Z)))

    for op in loads:
        op.wait()
    ws[0, g.R:2 * g.R, :] = jnp.zeros((g.R, g.D), BF)
    if g.R > g.src:
        pad = jnp.zeros((16, g.D), BF)
        ws[0, g.R - 16:g.R, :] = pad
        ws[1, g.R - 16:g.R, :] = pad
        ws[1, 2 * g.R - 16:2 * g.R, :] = pad
    ws[0, 0:g.src, :] = w_down[...]
    ws[1, 0:g.src, :] = w_gate[...]
    ws[1, g.R:g.R + g.src, :] = w_up[...]
    spread_rows(g, spread)

    for k in (1, X - 1, *range(2, X - 1)):
        arrive(buf_a.at[c, z, _mod(x - k, X)], ga_xs.at[k - 1], ga_xr.at[k - 1], sibling)
        a_forward(0, k)
    a_share(0, z)
    for hop in range(1, g.long + 1):
        b_arrive(hop)
        b_forward(hop)
        for i, b in slots_at(hop):
            b_across(i, b, last=hop == g.long)
        for j in (0, 1, X - 1, *range(2, X - 1)):
            a_arrive(hop, j)
            a_forward(hop, j)
        for i, b in slots_at(hop - 1):
            b_pass_on(i, b)
        for i, b in slots_at(hop):
            a_share(i, b)
        if hop > 1:
            for i, b in slots_at(hop - 2):
                b_share(i, b)
    for k in range(1, Z):
        arrive(codes.at[_mod(z - k, Z)], cz_ss.at[k - 1], cz_rs.at[k - 1], sibling)
    routing(g, codes, ss, dp * X + x)
    for i, b in slots_at(g.long):
        b_beside(i, b)
    for hop in (g.long - 1, g.long):
        for i, b in slots_at(hop):
            b_share(i, b)
    sel[...] = jnp.dot(spread[...], ss[...], preferred_element_type=F32).astype(BF)
    regroup_rows(g, regroup)

    for i in range(Z):
        hop = i if i <= g.long else g.long - i
        b = _mod(z + hop * step, Z)
        arrive(buf_a.at[other, b], sa_s.at[i], sa_r.at[i], sibling)
        arrive(buf_b.at[other, :, b], sb_s.at[i], sb_r.at[i], sibling)

    nt = (((1,), (1,)), ((), ()))

    def rows_a(array, xx):
        return buf_a[array, :, xx].reshape(g.T, g.a)

    def rows_b(array, xx):
        return buf_b[array, xx].reshape(g.T, g.b)

    pre = jnp.zeros((2 * g.R, g.T), F32)
    gh = jnp.zeros((g.R, g.T), F32)
    for xx in range(X):
        lo, mid, hi = xx * g.cols, xx * g.cols + g.a, (xx + 1) * g.cols
        pre += lax.dot_general(ws[1, :, lo:mid], rows_a(0, xx), nt, preferred_element_type=F32)
        pre += lax.dot_general(ws[1, :, mid:hi], rows_b(0, xx), nt, preferred_element_type=F32)
        gh += lax.dot_general(ws[0, 0:g.R, lo:mid], rows_a(1, xx), nt, preferred_element_type=F32)
        gh += lax.dot_general(ws[0, 0:g.R, mid:hi], rows_b(1, xx), nt, preferred_element_type=F32)
    pre_gate = pre[0:g.src]
    pre_up = pre[g.R:g.R + g.src]
    gh = gh[0:g.src]
    sigma = jax.nn.sigmoid(pre_gate)
    active = pre_gate * sigma
    lf[...] = jnp.zeros(lf.shape, F32)
    lf[0, 0:g.src, :] = active * pre_up
    lf[1, 0:g.src, :] = gh * pre_up * (sigma + active * (1.0 - sigma))
    lf[1, g.R:g.R + g.src, :] = gh * active
    for k in range(2):
        lb[k * LANES:(k + 1) * LANES, :] = lf[k].astype(BF)
        lt[k] = lf[k].T.astype(BF)

    def partial(array, lo, hi):
        return jnp.dot(lt[array][:, 0:2 * g.R], ws[array, :, lo:hi], preferred_element_type=F32)

    def partial_b(array, xx):
        lo = pl.multiple_of(xx * g.cols + g.a, LANES)
        v = jnp.dot(lt[array][:, 0:2 * g.R], ws[array, :, pl.ds(lo, g.b)], preferred_element_type=F32)
        return v.reshape(Z, g.G, g.b)

    def own_a(b, xx):
        return pa[xx, b] + rcv_a[xx, b].astype(F32)

    def reduce_a(hop, xx):
        if hop < g.long:
            v = own_a(_mod(z + (g.long - hop) * step, Z), xx)
            if hop:
                i = (hop - 1) * X + xx
                arrive(ring_rl.at[hop - 1, xx], rz_s.at[i], rz_r.at[i], sibling)
                v = v + ring_rl[hop - 1, xx].astype(F32)
            ring_sl[hop, xx] = v.astype(BF)
            i = hop * X + xx
            send(ring_sl.at[hop, xx], ring_rl.at[hop, xx], rz_s.at[i], rz_r.at[i], right)
        if hop < g.short:
            v = own_a(_mod(z - (g.short - hop) * step, Z), xx)
            if hop:
                i = (g.long + hop - 1) * X + xx
                arrive(ring_rs.at[hop - 1, xx], rz_s.at[i], rz_r.at[i], sibling)
                v = v + ring_rs[hop - 1, xx].astype(F32)
            ring_ss[hop, xx] = v.astype(BF)
            i = (g.long + hop) * X + xx
            send(ring_ss.at[hop, xx], ring_rs.at[hop, xx], rz_s.at[i], rz_r.at[i], left)

    b_long = [(h, _mod(z + (g.long - h) * step, Z)) for h in range(g.long)]
    b_short = [(g.long + h, _mod(z - (g.short - h) * step, Z)) for h in range(g.short)]
    b_own = (Z - 1, z)
    b_order = []
    for h in range(g.long):
        b_order.append(b_long[h])
        if h < g.short:
            b_order.append(b_short[h])
    b_order.append(b_own)

    def way_of(b):
        return 1 - 2 * lax.rem(b, 2)

    def b_first(i, b):
        b1_s[i] = pb[x_far, b].astype(BF)
        send(b1_s.at[i], b1_r.at[i], bxx_s.at[3 * i], bxx_r.at[3 * i], at_x(_mod(x + way_of(b), X)))

    def b_direct(i, b):
        to = _mod(x - way_of(b), X)
        bd_s[i] = pb[to, b].astype(BF)
        send(bd_s.at[i], bd_r.at[i], bxx_s.at[3 * i + 1], bxx_r.at[3 * i + 1], at_x(to))

    def b_second(i, b):
        to = _mod(x + way_of(b), X)
        arrive(b1_r.at[i], bxx_s.at[3 * i], bxx_r.at[3 * i], sibling)
        b2_s[i] = (pb[to, b] + b1_r[i].astype(F32)).astype(BF)
        send(b2_s.at[i], b2_r.at[i], bxx_s.at[3 * i + 2], bxx_r.at[3 * i + 2], at_x(to))

    def b_sum(i, b):
        arrive(bd_r.at[i], bxx_s.at[3 * i + 1], bxx_r.at[3 * i + 1], sibling)
        arrive(b2_r.at[i], bxx_s.at[3 * i + 2], bxx_r.at[3 * i + 2], sibling)
        return pb[x, b] + bd_r[i].astype(F32) + b2_r[i].astype(F32)

    def reduce_b(hop):
        for chain, to, n in ((b_long, right, g.long), (b_short, left, g.short)):
            if hop < n:
                i, b = chain[hop]
                v = b_sum(i, b)
                if hop:
                    arrive(bz_r.at[i - 1], bzz_s.at[i - 1], bzz_r.at[i - 1], sibling)
                    v = v + bz_r[i - 1].astype(F32)
                bz_s[i] = v.astype(BF)
                send(bz_s.at[i], bz_r.at[i], bzz_s.at[i], bzz_r.at[i], to)

    order = [x_far, x_up, x_down, x]
    for k, xx in enumerate(order):
        sib_b[k] = partial_b(other, xx).astype(BF)
        send(sib_b.at[k], rcv_b.at[k], rb_s.at[k], rb_r.at[k], sibling)
    for xx in range(X):
        lo = xx * g.cols
        sib_a[xx] = partial(other, lo, lo + g.a).astype(BF).reshape(Z, g.G, g.a)
        send(sib_a.at[xx], rcv_a.at[xx], ra_s.at[xx], ra_r.at[xx], sibling)

    def chip_b(k):
        v = partial_b(c, order[k])
        arrive(rcv_b.at[k], rb_s.at[k], rb_r.at[k], sibling)
        pb[order[k]] = v + rcv_b[k].astype(F32)

    chip_b(0)
    for i, b in b_order:
        b_first(i, b)
    chip_b(1)
    chip_b(2)
    for i, b in b_order:
        b_direct(i, b)
    for xx in range(X):
        lo = xx * g.cols
        pa[xx] = partial(c, lo, lo + g.a).reshape(Z, g.G, g.a)
        arrive(rcv_a.at[xx], ra_s.at[xx], ra_r.at[xx], sibling)
        reduce_a(0, xx)
    for i, b in b_order:
        b_second(i, b)
    chip_b(3)
    for xx in range(X):
        reduce_a(1, xx)
    reduce_b(0)

    picked = jnp.dot(sel[...], lb[...], preferred_element_type=F32).astype(BF)
    msg[...] = picked.reshape(Z, g.M, g.T)
    r1[z] = msg[z]
    for xx in range(X):
        reduce_a(2, xx)
    reduce_b(1)
    for k in range(1, Z):
        zz = _mod(z + k, Z)
        send(msg.at[zz], r1.at[z], m1_s.at[k - 1], m1_r.at[k - 1], at_z(zz))
    for xx in range(X):
        reduce_a(3, xx)
    reduce_b(2)
    for xx in range(X):
        v = own_a(z, xx)
        i = (g.long - 1) * X + xx
        arrive(ring_rl.at[g.long - 1, xx], rz_s.at[i], rz_r.at[i], sibling)
        v = v + ring_rl[g.long - 1, xx].astype(F32)
        i = (g.long + g.short - 1) * X + xx
        arrive(ring_rs.at[g.short - 1, xx], rz_s.at[i], rz_r.at[i], sibling)
        v = v + ring_rs[g.short - 1, xx].astype(F32)
        pa[xx, z] = v
        ax_s[xx] = v.astype(BF)
    for k in range(1, X):
        xx = _mod(x + k, X)
        send(ax_s.at[xx], ax_r.at[k - 1], axx_s.at[k - 1], axx_r.at[k - 1], at_x(xx))
    reduce_b(3)
    for k in range(1, Z):
        arrive(r1.at[_mod(z - k, Z)], m1_s.at[k - 1], m1_r.at[k - 1], sibling)
    m2[...] = jnp.dot(
        regroup[...], r1[...].reshape(Z * g.M, g.T), preferred_element_type=F32
    ).astype(BF).reshape(YC, g.M, g.T)
    r2[yc] = m2[yc]
    for i, peer, _, _ in yc_peers:
        send(m2.at[peer], r2.at[yc], m2_s.at[i], m2_r.at[i], at_yc(peer))

    va = pa[x, z]
    for k in range(1, X):
        arrive(ax_r.at[k - 1], axx_s.at[k - 1], axx_r.at[k - 1], sibling)
        va = va + ax_r[k - 1].astype(F32)
    vb = b_sum(*b_own)
    for i in (g.long - 1, g.long + g.short - 1):
        arrive(bz_r.at[i], bzz_s.at[i], bzz_r.at[i], sibling)
        vb = vb + bz_r[i].astype(F32)
    for k in range(YC):
        fin_s[k, :, 0:g.a] = va[k * g.t:(k + 1) * g.t]
        fin_s[k, :, g.a:g.cols] = vb[k * g.t:(k + 1) * g.t]
    fin_r[yc] = fin_s[yc]
    for i, peer, _, _ in yc_peers:
        send(fin_s.at[peer], fin_r.at[yc], f_s.at[i], f_r.at[i], at_yc(peer))

    for i, _, _, origin in yc_peers:
        arrive(r2.at[origin], m2_s.at[i], m2_r.at[i], sibling)
    wide = widened(g, own_code[...], r2)
    g_rows = jnp.concatenate([wide[1], wide[2]], axis=0)
    for xx in range(X):
        for lo, width, rows in (
            (xx * g.cols, g.a, rows_a),
            (xx * g.cols + g.a, g.b, rows_b),
        ):
            both = jnp.dot(g_rows, rows(0, xx), preferred_element_type=F32).astype(BF)
            g_gate[:, lo:lo + width] = both[0:g.wide]
            g_up[:, lo:lo + width] = both[g.W8:g.W8 + g.wide]
            down = jnp.dot(wide[0], rows(1, xx), preferred_element_type=F32).astype(BF)
            g_down[:, lo:lo + width] = down[0:g.wide]
    stores = [
        pltpu.make_async_copy(v, h, o_sem.at[i])
        for i, (v, h) in enumerate(((g_gate, gg_h), (g_up, gu_h), (g_down, gd_h)))
    ]
    for op in stores:
        op.start()

    for i, _, _, origin in yc_peers:
        arrive(fin_r.at[origin], f_s.at[i], f_r.at[i], sibling)
    for k, out in enumerate((o_out, o_in)):
        total = fin_r[k]
        for yy in range(1, Y):
            total = total + fin_r[yy * CORES + k]
        out[...] = total.astype(BF)

    for op in stores:
        op.wait()
    for op in sent:
        op.wait_send()


def routing(g, codes, ss, flat):
    n, Z, YC = g.dp, g.Z, g.YC
    c = codes[...].reshape(n, LANES).astype(I32)
    local = (c >> 1) - flat * g.src
    owned = (local >= 0) & (local < g.src)
    loc = local.astype(F32)
    flg = (c & 1).astype(F32)
    ownf = jnp.where(owned, 1.0, 0.0)
    before = lax.broadcasted_iota(I32, (LANES, LANES), 0) < lax.broadcasted_iota(I32, (LANES, LANES), 1)
    rank = jnp.dot(ownf.astype(BF), jnp.where(before, 1.0, 0.0).astype(BF), preferred_element_type=F32)
    lane = lax.broadcasted_iota(I32, (n, LANES), 1).astype(F32)
    wide_lane = lax.broadcasted_iota(I32, (n, 2 * LANES), 1).astype(F32)
    picks = []
    share = jnp.zeros((1, LANES), F32)
    for k in range(SLOTS):
        chosen = jnp.where(rank == float(k), ownf, 0.0)
        idx = jnp.sum(chosen * loc, axis=1, keepdims=True)
        has = jnp.sum(chosen, axis=1, keepdims=True)
        fl = jnp.sum(chosen * flg, axis=1, keepdims=True)
        one = jnp.where(lane == idx, has, 0.0)
        share = share + jnp.sum(one * fl, axis=0, keepdims=True)
        picks.append((idx, has, fl, one))
    for k, (idx, has, fl, one) in enumerate(picks):
        total = jnp.sum(one * share, axis=1, keepdims=True)
        scale = jnp.where(has > 0.0, fl / jnp.where(has > 0.0, total, 1.0), 0.0)
        for kind, (offset, factor) in enumerate(
            ((0.0, has), (float(LANES), scale), (float(LANES + g.R), scale))
        ):
            q = k * 3 + kind
            ss[q * n:(q + 1) * n, :] = jnp.where(wide_lane == idx + offset, factor, 0.0).astype(BF)


def row_parts(g, groups):
    per = 3 * SLOTS
    row = lax.broadcasted_iota(I32, (g.Z * g.M, 1), 0).astype(F32)
    block = jnp.floor((row + 0.5) * (1.0 / g.M))
    rest = row - block * g.M
    inner = jnp.floor((rest + 0.5) * (1.0 / per))
    return block, inner, rest - inner * per, rest < float(groups * per)


def spread_rows(g, spread):
    block, inner, q, valid = row_parts(g, g.YC)
    want = jnp.where(valid, q * g.dp + block * g.YC + inner, -1.0)
    col = lax.broadcasted_iota(I32, spread.shape, 1).astype(F32)
    spread[...] = jnp.where(col == want, 1.0, 0.0).astype(BF)


def regroup_rows(g, regroup):
    block, inner, q, valid = row_parts(g, g.Z)
    want = jnp.where(valid, inner * g.M + block * (3.0 * SLOTS) + q, -1.0)
    col = lax.broadcasted_iota(I32, regroup.shape, 1).astype(F32)
    regroup[...] = jnp.where(col == want, 1.0, 0.0).astype(BF)


def widened(g, code_row, r2):
    src = (code_row >> 1).astype(F32)
    owner = jnp.floor((src + 0.5) * (1.0 / (g.src * g.X)))
    zz = jnp.floor((owner + 0.5) * (1.0 / g.YC))
    first = (owner - zz * g.YC) * g.M + zz * (3.0 * SLOTS)
    sub = lax.broadcasted_iota(I32, (LANES, LANES), 0)
    lane = lax.broadcasted_iota(I32, (LANES, LANES), 1)
    owners = jnp.broadcast_to(owner, (LANES, LANES))
    own_col = jnp.sum(jnp.where(sub == lane, owners, 0.0), axis=1, keepdims=True)
    first_col = jnp.sum(
        jnp.where(sub == lane, jnp.broadcast_to(first, (LANES, LANES)), 0.0), axis=1, keepdims=True
    )
    earlier = jnp.sum(
        jnp.where((owners == own_col) & (lane < sub), 1.0, 0.0), axis=1, keepdims=True
    )
    target = (first_col + 3.0 * earlier)[0:g.W8]
    n = g.YC * g.M
    pos = lax.broadcasted_iota(I32, (g.W8, n), 1).astype(F32)
    columns = r2[...].reshape(n, g.T)
    return [
        jnp.dot(
            jnp.where(pos == target + float(kind), 1.0, 0.0).astype(BF),
            columns, preferred_element_type=F32,
        ).astype(BF)
        for kind in range(3)
    ]


PARTS = 4


def hand_over(n, *refs):
    ins, outs, bufs, (sem_in, sem_out) = refs[:n], refs[n:2 * n], refs[2 * n:3 * n], refs[3 * n:]
    steps = []
    for i in range(n):
        cols = ins[i].shape[1]
        width = cols // PARTS if cols % (PARTS * LANES) == 0 else cols
        for lo in range(0, cols, width):
            k, part = len(steps), (slice(None), pl.ds(lo, width))
            steps.append((
                pltpu.make_async_copy(ins[i].at[part], bufs[i].at[part], sem_in.at[k]),
                pltpu.make_async_copy(bufs[i].at[part], outs[i].at[part], sem_out.at[k]),
            ))
    for fetch, _ in steps:
        fetch.start()
    for fetch, store in steps:
        fetch.wait()
        store.start()
    for _, store in steps:
        store.wait()


def per_device(tokens, grad_out, gate_src, up_src, down_src, unit_map, copy_flag):
    g = Geometry(
        lax.axis_size("dp"), lax.axis_size("mp"), tokens.shape[0], tokens.shape[1],
        gate_src.shape[0], unit_map.shape[0],
    )
    X, Z, YC = g.X, g.Z, g.YC
    V = pltpu.VMEM
    dma = pltpu.SemaphoreType.DMA

    def pair(n):
        return [dma((max(n, 1),)), dma((max(n, 1),))]

    scratch = [
        V((2, g.t, g.cols + LANES), F32), V((YC, g.t, g.cols + LANES), F32), V((g.G, g.cols), F32),
        V((Z, YC, LANES), F32), V((1, LANES), I32),
        V((2, Z, X, g.G, g.a), BF), V((2, X, Z, g.G, g.b), BF),
        V(gate_src.shape, BF), V(gate_src.shape, BF), V(gate_src.shape, BF), V((2, 2 * g.R, g.D), BF),
        V((2, LANES, g.T), F32), V((2 * LANES, g.T), BF), V((2, g.T, LANES), BF),
        V((3 * SLOTS * g.dp, 2 * LANES), BF), V((Z * g.M, 3 * SLOTS * g.dp), BF), V((Z * g.M, Z * g.M), BF),
        V((Z * g.M, 2 * LANES), BF),
        V((Z, g.M, g.T), BF), V((Z, g.M, g.T), BF), V((YC, g.M, g.T), BF), V((YC, g.M, g.T), BF),
        V((X, Z, g.G, g.a), BF), V((X, Z, g.G, g.b), BF), V((X, Z, g.G, g.a), BF), V((X, Z, g.G, g.b), BF),
        V((X, Z, g.G, g.a), F32), V((X, Z, g.G, g.b), F32),
        V((g.long, X, g.G, g.a), BF), V((g.long, X, g.G, g.a), BF),
        V((g.short, X, g.G, g.a), BF), V((g.short, X, g.G, g.a), BF),
        V((X, g.G, g.a), BF), V((X - 1, g.G, g.a), BF),
        *[V((Z, g.G, g.b), BF) for _ in range(6)],
        V((Z - 1, g.G, g.b), BF), V((Z - 1, g.G, g.b), BF),
        V((YC, g.t, g.cols), F32), V((YC, g.t, g.cols), F32),
        V((g.wide, g.D), BF), V((g.wide, g.D), BF), V((g.wide, g.D), BF),
        dma((3,)), dma((3,)),
    ]
    counts = [
        YC, Z - 1, X - 1, (Z - 1) * X, Z - 1, 3 * Z, Z, Z, Z - 1, YC, X, X,
        (Z - 1) * X, X - 1, 3 * Z, Z - 1, YC,
    ]
    for n in counts:
        scratch += pair(n)
    vm = pl.BlockSpec(memory_space=pltpu.VMEM)
    anyw = pl.BlockSpec(memory_space=pl.ANY)
    wide_shape = jax.ShapeDtypeStruct((g.wide, g.D), BF)
    tok_shape = jax.ShapeDtypeStruct(tokens.shape, BF)
    macs = 6 * g.T * g.src * g.D + 3 * g.T * g.wide * g.D
    results = pl.pallas_call(
        functools.partial(kernel, g),
        out_shape=(tok_shape, tok_shape, wide_shape, wide_shape, wide_shape),
        in_specs=[vm, vm, anyw, anyw, anyw, vm, vm],
        out_specs=(vm, vm, anyw, anyw, anyw),
        scratch_shapes=scratch,
        compiler_params=pltpu.CompilerParams(
            collective_id=0, has_side_effects=True, vmem_limit_bytes=56 * 1024 * 1024
        ),
        cost_estimate=pl.CostEstimate(
            flops=2 * macs, bytes_accessed=3 * 2 * g.D * (g.src + g.wide), transcendentals=g.T * g.src
        ),
        name="widened_layer",
    )(
        tokens, grad_out, gate_src, up_src, down_src,
        unit_map.reshape(1, -1), copy_flag.reshape(1, -1),
    )
    return pl.pallas_call(
        functools.partial(hand_over, len(results)),
        out_shape=tuple(jax.ShapeDtypeStruct(r.shape, r.dtype) for r in results),
        in_specs=[anyw] * len(results),
        out_specs=(anyw,) * len(results),
        scratch_shapes=[V(r.shape, r.dtype) for r in results] + [dma((len(results) * PARTS,))] * 2,
        cost_estimate=pl.CostEstimate(flops=0, bytes_accessed=12 * g.wide * g.D, transcendentals=0),
        name="hand_over",
    )(*results)


def solution(mesh):
    in_specs = (
        P("dp", "mp"),
        P("dp", "mp"),
        P(("dp", "mp"), None),
        P(("dp", "mp"), None),
        P(("dp", "mp"), None),
        P(("dp", "mp")),
        P(("dp", "mp")),
    )
    out_specs = (
        P("dp", "mp"),
        P("dp", "mp"),
        P(("dp", "mp"), None),
        P(("dp", "mp"), None),
        P(("dp", "mp"), None),
    )
    return jax.shard_map(
        per_device, mesh=mesh, in_specs=in_specs, out_specs=out_specs, check_vma=False
    )
```

```python
import functools

import jax
import jax.numpy as jnp
from jax import lax
from jax.experimental import pallas as pl
from jax.experimental.pallas import tpu as pltpu
from jax.sharding import PartitionSpec as P

MESH = pl.DeviceIdType.MESH
BF = jnp.bfloat16
F32 = jnp.float32
I32 = jnp.int32

CORES = 2
CHIPS_Y = 4
SLOTS = 3
LANES = 128


def _mod(v, n):
    return lax.rem(v + n, n)


class Geometry:
    def __init__(self, n_dp, n_mp, tokens_dev, cols, src, wide):
        self.Y = CHIPS_Y
        self.YC = CHIPS_Y * CORES
        self.Z = n_dp // self.YC
        self.X = n_mp
        self.dp = n_dp
        self.t = tokens_dev
        self.T = n_dp * tokens_dev
        self.G = self.YC * tokens_dev
        self.cols = cols
        tiles = cols // LANES
        self.a = (tiles // 2) * LANES
        self.b = cols - self.a
        self.D = cols * n_mp
        self.src = src
        self.R = -(-src // 16) * 16
        self.wide = wide
        self.W8 = -(-wide // 8) * 8
        self.long = self.Z // 2
        self.short = self.Z - 1 - self.long
        self.M = -(-(self.YC * 3 * SLOTS) // 16) * 16


def kernel(g, *refs):
    (tok, gro, gate_h, up_h, down_h, umap, flag, o_out, o_in, gg_h, gu_h, gd_h) = refs[:12]
    (
        s1_src, s1_rcv, asm, codes, own_code,
        buf_a, buf_b,
        w_own, w_out, ws,
        pre_s, pre_r, lf, lb, lt,
        ss, spread, regroup, sel, msg, r1, m2, r2,
        pa, pb,
        ring_sl, ring_rl, ring_ss, ring_rs, ax_s, ax_r,
        b1_s, b1_r, b2_s, b2_r, bd_s, bd_r, bz_s, bz_r,
        fin_s, fin_r,
        g_gate, g_up, g_down,
        w_sem, o_sem,
        s1_ss, s1_rs, cz_ss, cz_rs, ga_xs, ga_xr, ga_zs, ga_zr, gb_zs, gb_zr, gb_xs, gb_xr,
        sa_s, sa_r, sb_s, sb_r,
        m1_s, m1_r, m2_s, m2_r,
        wx_s, wx_r, px_s, px_r,
        rz_s, rz_r, axx_s, axx_r, bxx_s, bxx_r, bzz_s, bzz_r, f_s, f_r,
    ) = refs[12:]
    X, Y, Z, YC = g.X, g.Y, g.Z, g.YC
    dp = lax.axis_index("dp")
    x = lax.axis_index("mp")
    z = lax.div(dp, YC)
    yc = lax.rem(dp, YC)
    y = lax.div(yc, CORES)
    c = lax.rem(yc, CORES)
    other = 1 - c
    step = 1 - 2 * c

    def at_z(zz):
        return (zz * YC + yc, x)

    def at_x(xx):
        return (dp, xx)

    def at_yc(k):
        return (z * YC + k, x)

    sibling = at_yc(y * CORES + other)
    yc_peers = []
    for dy in range(Y):
        for dc in range(CORES):
            if dy or dc:
                py = _mod(y + dy, Y)
                pc = _mod(c + dc, CORES)
                qy = _mod(y - dy, Y)
                yc_peers.append((dy * CORES + dc, py * CORES + pc, pc, qy * CORES + pc))

    sent = []

    def copy(src, dst, s_sem, r_sem, device):
        return pltpu.make_async_remote_copy(
            src_ref=src, dst_ref=dst, send_sem=s_sem, recv_sem=r_sem,
            device_id=device, device_id_type=MESH,
        )

    def send(src, dst, s_sem, r_sem, device):
        op = copy(src, dst, s_sem, r_sem, device)
        op.start()
        sent.append(op)

    def arrive(dst, s_sem, r_sem, device):
        copy(dst, dst, s_sem, r_sem, device).wait_recv()

    bar = pltpu.get_barrier_semaphore()
    for k in range(1, X):
        pl.semaphore_signal(bar, inc=1, device_id=at_x(_mod(x + k, X)), device_id_type=MESH)
    for k in range(1, Z):
        pl.semaphore_signal(bar, inc=1, device_id=at_z(_mod(z + k, Z)), device_id_type=MESH)
    for _, peer, _, _ in yc_peers:
        pl.semaphore_signal(bar, inc=1, device_id=at_yc(peer), device_id_type=MESH)

    loads = [
        pltpu.make_async_copy(h, w_own.at[i], w_sem.at[i])
        for i, h in enumerate((gate_h, up_h, down_h))
    ]
    for op in loads:
        op.start()

    code = umap[...] * 2 + flag[...]
    own_code[...] = jnp.full(own_code.shape, -1, I32)
    own_code[:, 0:g.wide] = code
    code_row = own_code[...]
    s1_src[0, :, 0:g.cols] = tok[...].astype(F32)
    s1_src[1, :, 0:g.cols] = gro[...].astype(F32)
    for k in range(2):
        s1_src[k, :, g.cols:g.cols + LANES] = jnp.broadcast_to(code_row.astype(F32), (g.t, LANES))
    s1_rcv[yc] = s1_src[c]

    pl.semaphore_wait(bar, (X - 1) + (Z - 1) + len(yc_peers))

    for i, peer, pc, _ in yc_peers:
        send(s1_src.at[pc], s1_rcv.at[yc], s1_ss.at[i], s1_rs.at[i], at_yc(peer))
    for i, _, _, origin in yc_peers:
        arrive(s1_rcv.at[origin], s1_ss.at[i], s1_rs.at[i], sibling)
    for k in range(YC):
        asm[k * g.t:(k + 1) * g.t, :] = s1_rcv[k, :, 0:g.cols]
        codes[z, k:k + 1, :] = s1_rcv[k, 0:1, g.cols:g.cols + LANES]
    block = asm[...].astype(BF)
    buf_a[c, z, x] = block[:, 0:g.a]
    buf_b[c, x, z] = block[:, g.a:g.cols]

    right, left = at_z(_mod(z + step, Z)), at_z(_mod(z - step, Z))
    a_cols = [x] + [_mod(x - k, X) for k in range(1, X)]

    def slots_at(hop):
        out = [(hop, _mod(z - hop * step, Z))]
        if 1 <= hop <= g.short:
            out.append((g.long + hop, _mod(z + hop * step, Z)))
        return out

    def a_forward(hop, j):
        if hop < g.long:
            ref = buf_a.at[c, _mod(z - hop * step, Z), a_cols[j]]
            i = hop * X + j
            send(ref, ref, ga_zs.at[i], ga_zr.at[i], right)
        if hop < g.short:
            ref = buf_a.at[c, _mod(z + hop * step, Z), a_cols[j]]
            i = (g.long + hop) * X + j
            send(ref, ref, ga_zs.at[i], ga_zr.at[i], left)

    def a_arrive(hop, j):
        i = (hop - 1) * X + j
        arrive(buf_a.at[c, _mod(z - hop * step, Z), a_cols[j]], ga_zs.at[i], ga_zr.at[i], sibling)
        if hop <= g.short:
            i = (g.long + hop - 1) * X + j
            arrive(buf_a.at[c, _mod(z + hop * step, Z), a_cols[j]], ga_zs.at[i], ga_zr.at[i], sibling)

    def b_forward(hop):
        if hop < g.long:
            ref = buf_b.at[c, x, _mod(z - hop * step, Z)]
            send(ref, ref, gb_zs.at[hop], gb_zr.at[hop], right)
        if hop < g.short:
            ref = buf_b.at[c, x, _mod(z + hop * step, Z)]
            i = g.long + hop
            send(ref, ref, gb_zs.at[i], gb_zr.at[i], left)

    def b_arrive(hop):
        arrive(buf_b.at[c, x, _mod(z - hop * step, Z)], gb_zs.at[hop - 1], gb_zr.at[hop - 1], sibling)
        if hop <= g.short:
            i = g.long + hop - 1
            arrive(buf_b.at[c, x, _mod(z + hop * step, Z)], gb_zs.at[i], gb_zr.at[i], sibling)

    x_up, x_down, x_far = _mod(x + 1, X), _mod(x - 1, X), _mod(x + 2, X)

    def b_across(i, b, last=False):
        ref = buf_b.at[c, x, b]
        if last:
            send(ref, ref, gb_xs.at[3 * i + 2], gb_xr.at[3 * i + 2], at_x(x_far))
        send(ref, ref, gb_xs.at[3 * i], gb_xr.at[3 * i], at_x(x_up))
        send(ref, ref, gb_xs.at[3 * i + 1], gb_xr.at[3 * i + 1], at_x(x_down))

    def b_beside(i, b):
        arrive(buf_b.at[c, x_down, b], gb_xs.at[3 * i], gb_xr.at[3 * i], sibling)
        arrive(buf_b.at[c, x_up, b], gb_xs.at[3 * i + 1], gb_xr.at[3 * i + 1], sibling)

    def b_pass_on(i, b):
        b_beside(i, b)
        way = 1 - 2 * lax.rem(b, 2)
        ref = buf_b.at[c, _mod(x - way, X), b]
        send(ref, ref, gb_xs.at[3 * i + 2], gb_xr.at[3 * i + 2], at_x(_mod(x + way, X)))

    def b_share(i, b):
        arrive(buf_b.at[c, x_far, b], gb_xs.at[3 * i + 2], gb_xr.at[3 * i + 2], sibling)
        ref = buf_b.at[c, :, b]
        send(ref, ref, sb_s.at[i], sb_r.at[i], sibling)

    def a_share(i, b):
        ref = buf_a.at[c, b]
        send(ref, ref, sa_s.at[i], sa_r.at[i], sibling)

    b_forward(0)
    for k in range(1, X):
        ref = buf_a.at[c, z, x]
        send(ref, ref, ga_xs.at[k - 1], ga_xr.at[k - 1], at_x(_mod(x + k, X)))
    a_forward(0, 0)
    b_across(0, z)
    for k in range(1, Z):
        send(codes.at[z], codes.at[z], cz_ss.at[k - 1], cz_rs.at[k - 1], at_z(_mod(z + k, Z)))

    for op in loads:
        op.wait()
    if g.R > g.src:
        pad = jnp.zeros((16, g.D), BF)
        w_out[0, g.R - 16:g.R, :] = pad
        w_out[1, g.R - 16:g.R, :] = pad
        ws[g.R - 16:g.R, :] = pad
        ws[3 * g.R - 16:3 * g.R, :] = pad
    w_out[0, 0:g.src, :] = w_own[2 * other]
    w_out[1, 0:g.src, :] = w_own[1]
    for k in range(2):
        rows = ws.at[pl.ds((2 * k + 1) * g.R, g.R)]
        send(w_out.at[k], rows, wx_s.at[k], wx_r.at[k], sibling)
    ws[0:g.src, :] = w_own[2 * c]
    ws[2 * g.R:2 * g.R + g.src, :] = w_own[1]
    spread_rows(g, spread)

    for k in (1, X - 1, *range(2, X - 1)):
        arrive(buf_a.at[c, z, _mod(x - k, X)], ga_xs.at[k - 1], ga_xr.at[k - 1], sibling)
        a_forward(0, k)
    a_share(0, z)
    for hop in range(1, g.long + 1):
        b_arrive(hop)
        b_forward(hop)
        for i, b in slots_at(hop):
            b_across(i, b, last=hop == g.long)
        for j in (0, 1, X - 1, *range(2, X - 1)):
            a_arrive(hop, j)
            a_forward(hop, j)
        for i, b in slots_at(hop - 1):
            b_pass_on(i, b)
        for i, b in slots_at(hop):
            a_share(i, b)
        if hop > 1:
            for i, b in slots_at(hop - 2):
                b_share(i, b)
    for k in range(1, Z):
        arrive(codes.at[_mod(z - k, Z)], cz_ss.at[k - 1], cz_rs.at[k - 1], sibling)
    routing(g, codes, ss, dp * X + x)
    for i, b in slots_at(g.long):
        b_beside(i, b)
    for hop in (g.long - 1, g.long):
        for i, b in slots_at(hop):
            b_share(i, b)
    sel[...] = jnp.dot(spread[...], ss[...], preferred_element_type=F32).astype(BF)
    regroup_rows(g, regroup)

    nt = (((1,), (1,)), ((), ()))

    def rows_a(array, xx):
        return buf_a[array, :, xx].reshape(g.T, g.a)

    def rows_b(array, xx):
        return buf_b[array, xx].reshape(g.T, g.b)

    for k in range(2):
        rows = ws.at[pl.ds((2 * k + 1) * g.R, g.R)]
        arrive(rows, wx_s.at[k], wx_r.at[k], sibling)
    pre = jnp.zeros((4 * g.R, g.T), F32)
    for xx in range(X):
        lo, mid, hi = xx * g.cols, xx * g.cols + g.a, (xx + 1) * g.cols
        pre += lax.dot_general(ws[:, lo:mid], rows_a(c, xx), nt, preferred_element_type=F32)
        pre += lax.dot_general(ws[:, mid:hi], rows_b(c, xx), nt, preferred_element_type=F32)
    pre_s[...] = pre
    send(pre_s, pre_r, px_s.at[0], px_r.at[0], sibling)
    arrive(pre_r, px_s.at[0], px_r.at[0], sibling)

    def turned(lo):
        return jnp.concatenate([pre_r[lo + g.R:lo + 2 * g.R], pre_r[lo:lo + g.R]], axis=0)

    first = c == 0
    pre_gate = jnp.where(first, pre_s[0:2 * g.R], turned(0))
    pre_up = jnp.where(first, pre_s[2 * g.R:4 * g.R], turned(2 * g.R))
    gh = jnp.where(first, turned(0), pre_s[0:2 * g.R])
    sigma = jax.nn.sigmoid(pre_gate)
    active = pre_gate * sigma
    hidden = active * pre_up
    d_gate = gh * pre_up * (sigma + active * (1.0 - sigma))
    d_up = gh * active
    lf[...] = jnp.zeros(lf.shape, F32)
    lf[0:2 * g.R, :] = jnp.where(first, d_gate, hidden)
    lf[2 * g.R:4 * g.R, :] = jnp.where(first, d_up, 0.0)
    for k in range(2):
        lt[:, k * LANES:(k + 1) * LANES] = lf[k * LANES:(k + 1) * LANES, :].T.astype(BF)
    lf[...] = jnp.zeros(lf.shape, F32)
    lf[0:g.R, :] = hidden[0:g.R]
    lf[LANES:LANES + g.R, :] = d_gate[0:g.R]
    lf[LANES + g.R:LANES + 2 * g.R, :] = d_up[0:g.R]
    lb[...] = lf[...].astype(BF)

    def partial(lo, width):
        return jnp.dot(lt[:, 0:4 * g.R], ws[:, pl.ds(lo, width)], preferred_element_type=F32)

    def own_a(b, xx):
        return pa[xx, b]

    def reduce_a(hop, xx):
        if hop < g.long:
            v = own_a(_mod(z + (g.long - hop) * step, Z), xx)
            if hop:
                i = (hop - 1) * X + xx
                arrive(ring_rl.at[hop - 1, xx], rz_s.at[i], rz_r.at[i], sibling)
                v = v + ring_rl[hop - 1, xx].astype(F32)
            ring_sl[hop, xx] = v.astype(BF)
            i = hop * X + xx
            send(ring_sl.at[hop, xx], ring_rl.at[hop, xx], rz_s.at[i], rz_r.at[i], right)
        if hop < g.short:
            v = own_a(_mod(z - (g.short - hop) * step, Z), xx)
            if hop:
                i = (g.long + hop - 1) * X + xx
                arrive(ring_rs.at[hop - 1, xx], rz_s.at[i], rz_r.at[i], sibling)
                v = v + ring_rs[hop - 1, xx].astype(F32)
            ring_ss[hop, xx] = v.astype(BF)
            i = (g.long + hop) * X + xx
            send(ring_ss.at[hop, xx], ring_rs.at[hop, xx], rz_s.at[i], rz_r.at[i], left)

    b_long = [(h, _mod(z + (g.long - h) * step, Z)) for h in range(g.long)]
    b_short = [(g.long + h, _mod(z - (g.short - h) * step, Z)) for h in range(g.short)]
    b_own = (Z - 1, z)
    b_order = []
    for h in range(g.long):
        b_order.append(b_long[h])
        if h < g.short:
            b_order.append(b_short[h])
    b_order.append(b_own)

    def way_of(b):
        return 1 - 2 * lax.rem(b, 2)

    def b_first(i, b):
        b1_s[i] = pb[x_far, b].astype(BF)
        send(b1_s.at[i], b1_r.at[i], bxx_s.at[3 * i], bxx_r.at[3 * i], at_x(_mod(x + way_of(b), X)))

    def b_direct(i, b):
        to = _mod(x - way_of(b), X)
        bd_s[i] = pb[to, b].astype(BF)
        send(bd_s.at[i], bd_r.at[i], bxx_s.at[3 * i + 1], bxx_r.at[3 * i + 1], at_x(to))

    def b_second(i, b):
        to = _mod(x + way_of(b), X)
        arrive(b1_r.at[i], bxx_s.at[3 * i], bxx_r.at[3 * i], sibling)
        b2_s[i] = (pb[to, b] + b1_r[i].astype(F32)).astype(BF)
        send(b2_s.at[i], b2_r.at[i], bxx_s.at[3 * i + 2], bxx_r.at[3 * i + 2], at_x(to))

    def b_sum(i, b):
        arrive(bd_r.at[i], bxx_s.at[3 * i + 1], bxx_r.at[3 * i + 1], sibling)
        arrive(b2_r.at[i], bxx_s.at[3 * i + 2], bxx_r.at[3 * i + 2], sibling)
        return pb[x, b] + bd_r[i].astype(F32) + b2_r[i].astype(F32)

    def reduce_b(hop):
        for chain, to, n in ((b_long, right, g.long), (b_short, left, g.short)):
            if hop < n:
                i, b = chain[hop]
                v = b_sum(i, b)
                if hop:
                    arrive(bz_r.at[i - 1], bzz_s.at[i - 1], bzz_r.at[i - 1], sibling)
                    v = v + bz_r[i - 1].astype(F32)
                bz_s[i] = v.astype(BF)
                send(bz_s.at[i], bz_r.at[i], bzz_s.at[i], bzz_r.at[i], to)

    order = [x_far, x_up, x_down, x]

    def chip_b(k):
        lo = pl.multiple_of(order[k] * g.cols + g.a, LANES)
        pb[order[k]] = partial(lo, g.b).reshape(Z, g.G, g.b)

    chip_b(0)
    for i, b in b_order:
        b_first(i, b)
    chip_b(1)
    chip_b(2)
    for i, b in b_order:
        b_direct(i, b)
    for xx in range(X):
        pa[xx] = partial(xx * g.cols, g.a).reshape(Z, g.G, g.a)
        reduce_a(0, xx)
    for i, b in b_order:
        b_second(i, b)
    chip_b(3)
    for xx in range(X):
        reduce_a(1, xx)
    reduce_b(0)

    picked = jnp.dot(sel[...], lb[...], preferred_element_type=F32).astype(BF)
    msg[...] = picked.reshape(Z, g.M, g.T)
    r1[z] = msg[z]
    for xx in range(X):
        reduce_a(2, xx)
    reduce_b(1)
    for k in range(1, Z):
        zz = _mod(z + k, Z)
        send(msg.at[zz], r1.at[z], m1_s.at[k - 1], m1_r.at[k - 1], at_z(zz))
    for xx in range(X):
        reduce_a(3, xx)
    reduce_b(2)
    for xx in range(X):
        v = own_a(z, xx)
        i = (g.long - 1) * X + xx
        arrive(ring_rl.at[g.long - 1, xx], rz_s.at[i], rz_r.at[i], sibling)
        v = v + ring_rl[g.long - 1, xx].astype(F32)
        i = (g.long + g.short - 1) * X + xx
        arrive(ring_rs.at[g.short - 1, xx], rz_s.at[i], rz_r.at[i], sibling)
        v = v + ring_rs[g.short - 1, xx].astype(F32)
        pa[xx, z] = v
        ax_s[xx] = v.astype(BF)
    for k in range(1, X):
        xx = _mod(x + k, X)
        send(ax_s.at[xx], ax_r.at[k - 1], axx_s.at[k - 1], axx_r.at[k - 1], at_x(xx))
    reduce_b(3)
    for k in range(1, Z):
        arrive(r1.at[_mod(z - k, Z)], m1_s.at[k - 1], m1_r.at[k - 1], sibling)
    m2[...] = jnp.dot(
        regroup[...], r1[...].reshape(Z * g.M, g.T), preferred_element_type=F32
    ).astype(BF).reshape(YC, g.M, g.T)
    r2[yc] = m2[yc]
    for i, peer, _, _ in yc_peers:
        send(m2.at[peer], r2.at[yc], m2_s.at[i], m2_r.at[i], at_yc(peer))

    va = pa[x, z]
    for k in range(1, X):
        arrive(ax_r.at[k - 1], axx_s.at[k - 1], axx_r.at[k - 1], sibling)
        va = va + ax_r[k - 1].astype(F32)
    vb = b_sum(*b_own)
    for i in (g.long - 1, g.long + g.short - 1):
        arrive(bz_r.at[i], bzz_s.at[i], bzz_r.at[i], sibling)
        vb = vb + bz_r[i].astype(F32)
    for k in range(YC):
        fin_s[k, :, 0:g.a] = va[k * g.t:(k + 1) * g.t]
        fin_s[k, :, g.a:g.cols] = vb[k * g.t:(k + 1) * g.t]
    fin_r[yc] = fin_s[yc]
    for i, peer, _, _ in yc_peers:
        send(fin_s.at[peer], fin_r.at[yc], f_s.at[i], f_r.at[i], at_yc(peer))

    for i in range(Z):
        hop = i if i <= g.long else g.long - i
        b = _mod(z + hop * step, Z)
        arrive(buf_a.at[other, b], sa_s.at[i], sa_r.at[i], sibling)
        arrive(buf_b.at[other, :, b], sb_s.at[i], sb_r.at[i], sibling)

    for i, _, _, origin in yc_peers:
        arrive(r2.at[origin], m2_s.at[i], m2_r.at[i], sibling)
    wide = widened(g, own_code[...], r2)
    g_rows = jnp.concatenate([wide[1], wide[2]], axis=0)
    for xx in range(X):
        for lo, width, rows in (
            (xx * g.cols, g.a, rows_a),
            (xx * g.cols + g.a, g.b, rows_b),
        ):
            both = jnp.dot(g_rows, rows(0, xx), preferred_element_type=F32).astype(BF)
            g_gate[:, lo:lo + width] = both[0:g.wide]
            g_up[:, lo:lo + width] = both[g.W8:g.W8 + g.wide]
            down = jnp.dot(wide[0], rows(1, xx), preferred_element_type=F32).astype(BF)
            g_down[:, lo:lo + width] = down[0:g.wide]
    stores = [
        pltpu.make_async_copy(v, h, o_sem.at[i])
        for i, (v, h) in enumerate(((g_gate, gg_h), (g_up, gu_h), (g_down, gd_h)))
    ]
    for op in stores:
        op.start()

    for op in sent:
        op.wait_send()
    for i, _, _, origin in yc_peers:
        arrive(fin_r.at[origin], f_s.at[i], f_r.at[i], sibling)
    for k, out in enumerate((o_in, o_out)):
        total = fin_r[k]
        for yy in range(1, Y):
            total = total + fin_r[yy * CORES + k]
        out[...] = total.astype(BF)

    for op in stores:
        op.wait()


def routing(g, codes, ss, flat):
    n, Z, YC = g.dp, g.Z, g.YC
    c = codes[...].reshape(n, LANES).astype(I32)
    local = (c >> 1) - flat * g.src
    owned = (local >= 0) & (local < g.src)
    loc = local.astype(F32)
    flg = (c & 1).astype(F32)
    ownf = jnp.where(owned, 1.0, 0.0)
    before = lax.broadcasted_iota(I32, (LANES, LANES), 0) < lax.broadcasted_iota(I32, (LANES, LANES), 1)
    rank = jnp.dot(ownf.astype(BF), jnp.where(before, 1.0, 0.0).astype(BF), preferred_element_type=F32)
    lane = lax.broadcasted_iota(I32, (n, LANES), 1).astype(F32)
    wide_lane = lax.broadcasted_iota(I32, (n, 2 * LANES), 1).astype(F32)
    picks = []
    share = jnp.zeros((1, LANES), F32)
    for k in range(SLOTS):
        chosen = jnp.where(rank == float(k), ownf, 0.0)
        idx = jnp.sum(chosen * loc, axis=1, keepdims=True)
        has = jnp.sum(chosen, axis=1, keepdims=True)
        fl = jnp.sum(chosen * flg, axis=1, keepdims=True)
        one = jnp.where(lane == idx, has, 0.0)
        share = share + jnp.sum(one * fl, axis=0, keepdims=True)
        picks.append((idx, has, fl, one))
    for k, (idx, has, fl, one) in enumerate(picks):
        total = jnp.sum(one * share, axis=1, keepdims=True)
        scale = jnp.where(has > 0.0, fl / jnp.where(has > 0.0, total, 1.0), 0.0)
        for kind, (offset, factor) in enumerate(
            ((0.0, has), (float(LANES), scale), (float(LANES + g.R), scale))
        ):
            q = k * 3 + kind
            ss[q * n:(q + 1) * n, :] = jnp.where(wide_lane == idx + offset, factor, 0.0).astype(BF)


def row_parts(g, groups):
    per = 3 * SLOTS
    row = lax.broadcasted_iota(I32, (g.Z * g.M, 1), 0).astype(F32)
    block = jnp.floor((row + 0.5) * (1.0 / g.M))
    rest = row - block * g.M
    inner = jnp.floor((rest + 0.5) * (1.0 / per))
    return block, inner, rest - inner * per, rest < float(groups * per)


def spread_rows(g, spread):
    block, inner, q, valid = row_parts(g, g.YC)
    want = jnp.where(valid, q * g.dp + block * g.YC + inner, -1.0)
    col = lax.broadcasted_iota(I32, spread.shape, 1).astype(F32)
    spread[...] = jnp.where(col == want, 1.0, 0.0).astype(BF)


def regroup_rows(g, regroup):
    block, inner, q, valid = row_parts(g, g.Z)
    want = jnp.where(valid, inner * g.M + block * (3.0 * SLOTS) + q, -1.0)
    col = lax.broadcasted_iota(I32, regroup.shape, 1).astype(F32)
    regroup[...] = jnp.where(col == want, 1.0, 0.0).astype(BF)


def widened(g, code_row, r2):
    src = (code_row >> 1).astype(F32)
    owner = jnp.floor((src + 0.5) * (1.0 / (g.src * g.X)))
    zz = jnp.floor((owner + 0.5) * (1.0 / g.YC))
    first = (owner - zz * g.YC) * g.M + zz * (3.0 * SLOTS)
    sub = lax.broadcasted_iota(I32, (LANES, LANES), 0)
    lane = lax.broadcasted_iota(I32, (LANES, LANES), 1)
    owners = jnp.broadcast_to(owner, (LANES, LANES))
    own_col = jnp.sum(jnp.where(sub == lane, owners, 0.0), axis=1, keepdims=True)
    first_col = jnp.sum(
        jnp.where(sub == lane, jnp.broadcast_to(first, (LANES, LANES)), 0.0), axis=1, keepdims=True
    )
    earlier = jnp.sum(
        jnp.where((owners == own_col) & (lane < sub), 1.0, 0.0), axis=1, keepdims=True
    )
    target = (first_col + 3.0 * earlier)[0:g.W8]
    n = g.YC * g.M
    pos = lax.broadcasted_iota(I32, (g.W8, n), 1).astype(F32)
    columns = r2[...].reshape(n, g.T)
    return [
        jnp.dot(
            jnp.where(pos == target + float(kind), 1.0, 0.0).astype(BF),
            columns, preferred_element_type=F32,
        ).astype(BF)
        for kind in range(3)
    ]


PARTS = 4


def hand_over(n, *refs):
    ins, outs, bufs, (sem_in, sem_out) = refs[:n], refs[n:2 * n], refs[2 * n:3 * n], refs[3 * n:]
    steps = []
    for i in range(n):
        cols = ins[i].shape[1]
        width = cols // PARTS if cols % (PARTS * LANES) == 0 else cols
        for lo in range(0, cols, width):
            k, part = len(steps), (slice(None), pl.ds(lo, width))
            steps.append((
                pltpu.make_async_copy(ins[i].at[part], bufs[i].at[part], sem_in.at[k]),
                pltpu.make_async_copy(bufs[i].at[part], outs[i].at[part], sem_out.at[k]),
            ))
    for fetch, _ in steps:
        fetch.start()
    for fetch, store in steps:
        fetch.wait()
        store.start()
    for _, store in steps:
        store.wait()


def per_device(tokens, grad_out, gate_src, up_src, down_src, unit_map, copy_flag):
    g = Geometry(
        lax.axis_size("dp"), lax.axis_size("mp"), tokens.shape[0], tokens.shape[1],
        gate_src.shape[0], unit_map.shape[0],
    )
    X, Z, YC = g.X, g.Z, g.YC
    V = pltpu.VMEM
    dma = pltpu.SemaphoreType.DMA

    def pair(n):
        return [dma((max(n, 1),)), dma((max(n, 1),))]

    scratch = [
        V((2, g.t, g.cols + LANES), F32), V((YC, g.t, g.cols + LANES), F32), V((g.G, g.cols), F32),
        V((Z, YC, LANES), F32), V((1, LANES), I32),
        V((2, Z, X, g.G, g.a), BF), V((2, X, Z, g.G, g.b), BF),
        V((3, *gate_src.shape), BF), V((2, g.R, g.D), BF), V((4 * g.R, g.D), BF),
        V((4 * g.R, g.T), F32), V((4 * g.R, g.T), F32),
        V((2 * LANES, g.T), F32), V((2 * LANES, g.T), BF), V((g.T, 2 * LANES), BF),
        V((3 * SLOTS * g.dp, 2 * LANES), BF), V((Z * g.M, 3 * SLOTS * g.dp), BF), V((Z * g.M, Z * g.M), BF),
        V((Z * g.M, 2 * LANES), BF),
        V((Z, g.M, g.T), BF), V((Z, g.M, g.T), BF), V((YC, g.M, g.T), BF), V((YC, g.M, g.T), BF),
        V((X, Z, g.G, g.a), F32), V((X, Z, g.G, g.b), F32),
        V((g.long, X, g.G, g.a), BF), V((g.long, X, g.G, g.a), BF),
        V((g.short, X, g.G, g.a), BF), V((g.short, X, g.G, g.a), BF),
        V((X, g.G, g.a), BF), V((X - 1, g.G, g.a), BF),
        *[V((Z, g.G, g.b), BF) for _ in range(6)],
        V((Z - 1, g.G, g.b), BF), V((Z - 1, g.G, g.b), BF),
        V((YC, g.t, g.cols), F32), V((YC, g.t, g.cols), F32),
        V((g.wide, g.D), BF), V((g.wide, g.D), BF), V((g.wide, g.D), BF),
        dma((3,)), dma((3,)),
    ]
    counts = [
        YC, Z - 1, X - 1, (Z - 1) * X, Z - 1, 3 * Z, Z, Z, Z - 1, YC, 2, 1,
        (Z - 1) * X, X - 1, 3 * Z, Z - 1, YC,
    ]
    for n in counts:
        scratch += pair(n)
    vm = pl.BlockSpec(memory_space=pltpu.VMEM)
    anyw = pl.BlockSpec(memory_space=pl.ANY)
    wide_shape = jax.ShapeDtypeStruct((g.wide, g.D), BF)
    tok_shape = jax.ShapeDtypeStruct(tokens.shape, BF)
    macs = 6 * g.T * g.src * g.D + 3 * g.T * g.wide * g.D
    results = pl.pallas_call(
        functools.partial(kernel, g),
        out_shape=(tok_shape, tok_shape, wide_shape, wide_shape, wide_shape),
        in_specs=[vm, vm, anyw, anyw, anyw, vm, vm],
        out_specs=(vm, vm, anyw, anyw, anyw),
        scratch_shapes=scratch,
        compiler_params=pltpu.CompilerParams(
            collective_id=0, has_side_effects=True, vmem_limit_bytes=56 * 1024 * 1024
        ),
        cost_estimate=pl.CostEstimate(
            flops=2 * macs, bytes_accessed=3 * 2 * g.D * (g.src + g.wide), transcendentals=g.T * g.src
        ),
        name="widened_layer",
    )(
        tokens, grad_out, gate_src, up_src, down_src,
        unit_map.reshape(1, -1), copy_flag.reshape(1, -1),
    )
    return pl.pallas_call(
        functools.partial(hand_over, len(results)),
        out_shape=tuple(jax.ShapeDtypeStruct(r.shape, r.dtype) for r in results),
        in_specs=[anyw] * len(results),
        out_specs=(anyw,) * len(results),
        scratch_shapes=[V(r.shape, r.dtype) for r in results] + [dma((len(results) * PARTS,))] * 2,
        cost_estimate=pl.CostEstimate(flops=0, bytes_accessed=12 * g.wide * g.D, transcendentals=0),
        name="hand_over",
    )(*results)


def solution(mesh):
    in_specs = (
        P("dp", "mp"),
        P("dp", "mp"),
        P(("dp", "mp"), None),
        P(("dp", "mp"), None),
        P(("dp", "mp"), None),
        P(("dp", "mp")),
        P(("dp", "mp")),
    )
    out_specs = (
        P("dp", "mp"),
        P("dp", "mp"),
        P(("dp", "mp"), None),
        P(("dp", "mp"), None),
        P(("dp", "mp"), None),
    )
    return jax.shard_map(
        per_device, mesh=mesh, in_specs=in_specs, out_specs=out_specs, check_vma=False
    )
```

```python
import functools

import jax
import jax.numpy as jnp
from jax import lax
from jax.experimental import pallas as pl
from jax.experimental.pallas import tpu as pltpu
from jax.sharding import PartitionSpec as P

MESH = pl.DeviceIdType.MESH
BF = jnp.bfloat16
F32 = jnp.float32
I32 = jnp.int32

CORES = 2
CHIPS_Y = 4
SLOTS = 3
LANES = 128


def _mod(v, n):
    return lax.rem(v + n, n)


class Geometry:
    def __init__(self, n_dp, n_mp, tokens_dev, cols, src, wide):
        self.Y = CHIPS_Y
        self.YC = CHIPS_Y * CORES
        self.Z = n_dp // self.YC
        self.X = n_mp
        self.dp = n_dp
        self.t = tokens_dev
        self.T = n_dp * tokens_dev
        self.G = self.YC * tokens_dev
        self.cols = cols
        tiles = cols // LANES
        self.a = (tiles // 2) * LANES
        self.b = cols - self.a
        self.ra = (tiles // 2 + 1) * LANES
        self.rb = cols - self.ra
        self.D = cols * n_mp
        self.src = src
        self.R = -(-src // 16) * 16
        self.wide = wide
        self.W8 = -(-wide // 8) * 8
        self.long = self.Z // 2
        self.short = self.Z - 1 - self.long
        self.M = -(-(self.YC * 3 * SLOTS) // 16) * 16


def kernel(g, *refs):
    (tok, gro, gate_h, up_h, down_h, umap, flag, o_out, o_in, gg_h, gu_h, gd_h) = refs[:12]
    (
        s1_src, s1_rcv, asm, codes, own_code,
        buf_a, buf_b,
        w_own, w_out, ws,
        pre_s, pre_r, lf, lb, lt,
        ss, spread, regroup, sel, msg, r1, m2, r2,
        pa, pb,
        ring_sl, ring_rl, ring_ss, ring_rs, ax_s, ax_r,
        b1_s, b1_r, b2_s, b2_r, bd_s, bd_r, bz_s, bz_r,
        fin_s, fin_r,
        g_gate, g_up, g_down,
        w_sem, o_sem,
        s1_ss, s1_rs, cz_ss, cz_rs, ga_xs, ga_xr, ga_zs, ga_zr, gb_zs, gb_zr, gb_xs, gb_xr,
        sa_s, sa_r, sb_s, sb_r,
        m1_s, m1_r, m2_s, m2_r,
        wx_s, wx_r, px_s, px_r,
        rz_s, rz_r, axx_s, axx_r, bxx_s, bxx_r, bzz_s, bzz_r, f_s, f_r,
    ) = refs[12:]
    X, Y, Z, YC = g.X, g.Y, g.Z, g.YC
    dp = lax.axis_index("dp")
    x = lax.axis_index("mp")
    z = lax.div(dp, YC)
    yc = lax.rem(dp, YC)
    y = lax.div(yc, CORES)
    c = lax.rem(yc, CORES)
    other = 1 - c
    step = 1 - 2 * c

    def at_z(zz):
        return (zz * YC + yc, x)

    def at_x(xx):
        return (dp, xx)

    def at_yc(k):
        return (z * YC + k, x)

    sibling = at_yc(y * CORES + other)
    yc_peers = []
    for dy in range(Y):
        for dc in range(CORES):
            if dy or dc:
                py = _mod(y + dy, Y)
                pc = _mod(c + dc, CORES)
                qy = _mod(y - dy, Y)
                yc_peers.append((dy * CORES + dc, py * CORES + pc, pc, qy * CORES + pc))

    sent = []

    def copy(src, dst, s_sem, r_sem, device):
        return pltpu.make_async_remote_copy(
            src_ref=src, dst_ref=dst, send_sem=s_sem, recv_sem=r_sem,
            device_id=device, device_id_type=MESH,
        )

    def send(src, dst, s_sem, r_sem, device):
        op = copy(src, dst, s_sem, r_sem, device)
        op.start()
        sent.append(op)

    def arrive(dst, s_sem, r_sem, device):
        copy(dst, dst, s_sem, r_sem, device).wait_recv()

    bar = pltpu.get_barrier_semaphore()
    for k in range(1, X):
        pl.semaphore_signal(bar, inc=1, device_id=at_x(_mod(x + k, X)), device_id_type=MESH)
    for k in range(1, Z):
        pl.semaphore_signal(bar, inc=1, device_id=at_z(_mod(z + k, Z)), device_id_type=MESH)
    for _, peer, _, _ in yc_peers:
        pl.semaphore_signal(bar, inc=1, device_id=at_yc(peer), device_id_type=MESH)

    loads = [
        pltpu.make_async_copy(h, w_own.at[i], w_sem.at[i])
        for i, h in enumerate((gate_h, up_h, down_h))
    ]
    for op in loads:
        op.start()

    code = umap[...] * 2 + flag[...]
    own_code[...] = jnp.full(own_code.shape, -1, I32)
    own_code[:, 0:g.wide] = code
    code_row = own_code[...]
    s1_src[0, :, 0:g.cols] = tok[...].astype(F32)
    s1_src[1, :, 0:g.cols] = gro[...].astype(F32)
    for k in range(2):
        s1_src[k, :, g.cols:g.cols + LANES] = jnp.broadcast_to(code_row.astype(F32), (g.t, LANES))
    s1_rcv[yc] = s1_src[c]

    pl.semaphore_wait(bar, (X - 1) + (Z - 1) + len(yc_peers))

    for i, peer, pc, _ in yc_peers:
        send(s1_src.at[pc], s1_rcv.at[yc], s1_ss.at[i], s1_rs.at[i], at_yc(peer))
    for i, _, _, origin in yc_peers:
        arrive(s1_rcv.at[origin], s1_ss.at[i], s1_rs.at[i], sibling)
    for k in range(YC):
        asm[k * g.t:(k + 1) * g.t, :] = s1_rcv[k, :, 0:g.cols]
        codes[z, k:k + 1, :] = s1_rcv[k, 0:1, g.cols:g.cols + LANES]
    block = asm[...].astype(BF)
    buf_a[c, z, x] = block[:, 0:g.a]
    buf_b[c, x, z] = block[:, g.a:g.cols]

    right, left = at_z(_mod(z + step, Z)), at_z(_mod(z - step, Z))
    a_cols = [x] + [_mod(x - k, X) for k in range(1, X)]

    def slots_at(hop):
        out = [(hop, _mod(z - hop * step, Z))]
        if 1 <= hop <= g.short:
            out.append((g.long + hop, _mod(z + hop * step, Z)))
        return out

    def a_forward(hop, j):
        if hop < g.long:
            ref = buf_a.at[c, _mod(z - hop * step, Z), a_cols[j]]
            i = hop * X + j
            send(ref, ref, ga_zs.at[i], ga_zr.at[i], right)
        if hop < g.short:
            ref = buf_a.at[c, _mod(z + hop * step, Z), a_cols[j]]
            i = (g.long + hop) * X + j
            send(ref, ref, ga_zs.at[i], ga_zr.at[i], left)

    def a_arrive(hop, j):
        i = (hop - 1) * X + j
        arrive(buf_a.at[c, _mod(z - hop * step, Z), a_cols[j]], ga_zs.at[i], ga_zr.at[i], sibling)
        if hop <= g.short:
            i = (g.long + hop - 1) * X + j
            arrive(buf_a.at[c, _mod(z + hop * step, Z), a_cols[j]], ga_zs.at[i], ga_zr.at[i], sibling)

    def b_forward(hop):
        if hop < g.long:
            ref = buf_b.at[c, x, _mod(z - hop * step, Z)]
            send(ref, ref, gb_zs.at[hop], gb_zr.at[hop], right)
        if hop < g.short:
            ref = buf_b.at[c, x, _mod(z + hop * step, Z)]
            i = g.long + hop
            send(ref, ref, gb_zs.at[i], gb_zr.at[i], left)

    def b_arrive(hop):
        arrive(buf_b.at[c, x, _mod(z - hop * step, Z)], gb_zs.at[hop - 1], gb_zr.at[hop - 1], sibling)
        if hop <= g.short:
            i = g.long + hop - 1
            arrive(buf_b.at[c, x, _mod(z + hop * step, Z)], gb_zs.at[i], gb_zr.at[i], sibling)

    x_up, x_down, x_far = _mod(x + 1, X), _mod(x - 1, X), _mod(x + 2, X)

    def b_across(i, b, last=False):
        ref = buf_b.at[c, x, b]
        if last:
            send(ref, ref, gb_xs.at[3 * i + 2], gb_xr.at[3 * i + 2], at_x(x_far))
        send(ref, ref, gb_xs.at[3 * i], gb_xr.at[3 * i], at_x(x_up))
        send(ref, ref, gb_xs.at[3 * i + 1], gb_xr.at[3 * i + 1], at_x(x_down))

    def b_beside(i, b):
        arrive(buf_b.at[c, x_down, b], gb_xs.at[3 * i], gb_xr.at[3 * i], sibling)
        arrive(buf_b.at[c, x_up, b], gb_xs.at[3 * i + 1], gb_xr.at[3 * i + 1], sibling)

    def b_pass_on(i, b):
        b_beside(i, b)
        way = 1 - 2 * lax.rem(b, 2)
        ref = buf_b.at[c, _mod(x - way, X), b]
        send(ref, ref, gb_xs.at[3 * i + 2], gb_xr.at[3 * i + 2], at_x(_mod(x + way, X)))

    def b_share(i, b):
        arrive(buf_b.at[c, x_far, b], gb_xs.at[3 * i + 2], gb_xr.at[3 * i + 2], sibling)
        ref = buf_b.at[c, :, b]
        send(ref, ref, sb_s.at[i], sb_r.at[i], sibling)

    def a_share(i, b):
        ref = buf_a.at[c, b]
        send(ref, ref, sa_s.at[i], sa_r.at[i], sibling)

    b_forward(0)
    for k in range(1, X):
        ref = buf_a.at[c, z, x]
        send(ref, ref, ga_xs.at[k - 1], ga_xr.at[k - 1], at_x(_mod(x + k, X)))
    a_forward(0, 0)
    b_across(0, z)
    for k in range(1, Z):
        send(codes.at[z], codes.at[z], cz_ss.at[k - 1], cz_rs.at[k - 1], at_z(_mod(z + k, Z)))

    for op in loads:
        op.wait()
    if g.R > g.src:
        pad = jnp.zeros((16, g.D), BF)
        w_out[0, g.R - 16:g.R, :] = pad
        w_out[1, g.R - 16:g.R, :] = pad
        ws[g.R - 16:g.R, :] = pad
        ws[3 * g.R - 16:3 * g.R, :] = pad
    w_out[0, 0:g.src, :] = w_own[2 * other]
    w_out[1, 0:g.src, :] = w_own[1]
    for k in range(2):
        rows = ws.at[pl.ds((2 * k + 1) * g.R, g.R)]
        send(w_out.at[k], rows, wx_s.at[k], wx_r.at[k], sibling)
    ws[0:g.src, :] = w_own[2 * c]
    ws[2 * g.R:2 * g.R + g.src, :] = w_own[1]
    spread_rows(g, spread)

    for k in (1, X - 1, *range(2, X - 1)):
        arrive(buf_a.at[c, z, _mod(x - k, X)], ga_xs.at[k - 1], ga_xr.at[k - 1], sibling)
        a_forward(0, k)
    a_share(0, z)
    for hop in range(1, g.long + 1):
        b_arrive(hop)
        b_forward(hop)
        for i, b in slots_at(hop):
            b_across(i, b, last=hop == g.long)
        for j in (0, 1, X - 1, *range(2, X - 1)):
            a_arrive(hop, j)
            a_forward(hop, j)
        for i, b in slots_at(hop - 1):
            b_pass_on(i, b)
        for i, b in slots_at(hop):
            a_share(i, b)
        if hop > 1:
            for i, b in slots_at(hop - 2):
                b_share(i, b)
    for k in range(1, Z):
        arrive(codes.at[_mod(z - k, Z)], cz_ss.at[k - 1], cz_rs.at[k - 1], sibling)
    routing(g, codes, ss, dp * X + x)
    for i, b in slots_at(g.long):
        b_beside(i, b)
    for hop in (g.long - 1, g.long):
        for i, b in slots_at(hop):
            b_share(i, b)
    sel[...] = jnp.dot(spread[...], ss[...], preferred_element_type=F32).astype(BF)
    regroup_rows(g, regroup)

    nt = (((1,), (1,)), ((), ()))

    def rows_a(array, xx):
        return buf_a[array, :, xx].reshape(g.T, g.a)

    def rows_b(array, xx):
        return buf_b[array, xx].reshape(g.T, g.b)

    for k in range(2):
        rows = ws.at[pl.ds((2 * k + 1) * g.R, g.R)]
        arrive(rows, wx_s.at[k], wx_r.at[k], sibling)
    pre = jnp.zeros((4 * g.R, g.T), F32)
    for xx in range(X):
        lo, mid, hi = xx * g.cols, xx * g.cols + g.a, (xx + 1) * g.cols
        pre += lax.dot_general(ws[:, lo:mid], rows_a(c, xx), nt, preferred_element_type=F32)
        pre += lax.dot_general(ws[:, mid:hi], rows_b(c, xx), nt, preferred_element_type=F32)
    pre_s[...] = pre
    send(pre_s, pre_r, px_s.at[0], px_r.at[0], sibling)
    arrive(pre_r, px_s.at[0], px_r.at[0], sibling)

    def turned(lo):
        return jnp.concatenate([pre_r[lo + g.R:lo + 2 * g.R], pre_r[lo:lo + g.R]], axis=0)

    first = c == 0
    pre_gate = jnp.where(first, pre_s[0:2 * g.R], turned(0))
    pre_up = jnp.where(first, pre_s[2 * g.R:4 * g.R], turned(2 * g.R))
    gh = jnp.where(first, turned(0), pre_s[0:2 * g.R])
    sigma = jax.nn.sigmoid(pre_gate)
    active = pre_gate * sigma
    hidden = active * pre_up
    d_gate = gh * pre_up * (sigma + active * (1.0 - sigma))
    d_up = gh * active
    lf[...] = jnp.zeros(lf.shape, F32)
    lf[0:2 * g.R, :] = jnp.where(first, d_gate, hidden)
    lf[2 * g.R:4 * g.R, :] = jnp.where(first, d_up, 0.0)
    for k in range(2):
        lt[:, k * LANES:(k + 1) * LANES] = lf[k * LANES:(k + 1) * LANES, :].T.astype(BF)
    lf[...] = jnp.zeros(lf.shape, F32)
    lf[0:g.R, :] = hidden[0:g.R]
    lf[LANES:LANES + g.R, :] = d_gate[0:g.R]
    lf[LANES + g.R:LANES + 2 * g.R, :] = d_up[0:g.R]
    lb[...] = lf[...].astype(BF)

    def partial(lo, width):
        return jnp.dot(lt[:, 0:4 * g.R], ws[:, pl.ds(lo, width)], preferred_element_type=F32)

    def own_a(b, xx):
        return pa[xx, b]

    def reduce_a(hop, xx):
        if hop < g.long:
            v = own_a(_mod(z + (g.long - hop) * step, Z), xx)
            if hop:
                i = (hop - 1) * X + xx
                arrive(ring_rl.at[hop - 1, xx], rz_s.at[i], rz_r.at[i], sibling)
                v = v + ring_rl[hop - 1, xx].astype(F32)
            ring_sl[hop, xx] = v.astype(BF)
            i = hop * X + xx
            send(ring_sl.at[hop, xx], ring_rl.at[hop, xx], rz_s.at[i], rz_r.at[i], right)
        if hop < g.short:
            v = own_a(_mod(z - (g.short - hop) * step, Z), xx)
            if hop:
                i = (g.long + hop - 1) * X + xx
                arrive(ring_rs.at[hop - 1, xx], rz_s.at[i], rz_r.at[i], sibling)
                v = v + ring_rs[hop - 1, xx].astype(F32)
            ring_ss[hop, xx] = v.astype(BF)
            i = (g.long + hop) * X + xx
            send(ring_ss.at[hop, xx], ring_rs.at[hop, xx], rz_s.at[i], rz_r.at[i], left)

    b_long = [(h, _mod(z + (g.long - h) * step, Z)) for h in range(g.long)]
    b_short = [(g.long + h, _mod(z - (g.short - h) * step, Z)) for h in range(g.short)]
    b_own = (Z - 1, z)
    b_order = []
    for h in range(g.long):
        b_order.append(b_long[h])
        if h < g.short:
            b_order.append(b_short[h])
    b_order.append(b_own)

    def way_of(b):
        return 1 - 2 * lax.rem(b, 2)

    def b_first(i, b):
        b1_s[i] = pb[x_far, b].astype(BF)
        send(b1_s.at[i], b1_r.at[i], bxx_s.at[3 * i], bxx_r.at[3 * i], at_x(_mod(x + way_of(b), X)))

    def b_direct(i, b):
        to = _mod(x - way_of(b), X)
        bd_s[i] = pb[to, b].astype(BF)
        send(bd_s.at[i], bd_r.at[i], bxx_s.at[3 * i + 1], bxx_r.at[3 * i + 1], at_x(to))

    def b_second(i, b):
        to = _mod(x + way_of(b), X)
        arrive(b1_r.at[i], bxx_s.at[3 * i], bxx_r.at[3 * i], sibling)
        b2_s[i] = (pb[to, b] + b1_r[i].astype(F32)).astype(BF)
        send(b2_s.at[i], b2_r.at[i], bxx_s.at[3 * i + 2], bxx_r.at[3 * i + 2], at_x(to))

    def b_sum(i, b):
        arrive(bd_r.at[i], bxx_s.at[3 * i + 1], bxx_r.at[3 * i + 1], sibling)
        arrive(b2_r.at[i], bxx_s.at[3 * i + 2], bxx_r.at[3 * i + 2], sibling)
        return pb[x, b] + bd_r[i].astype(F32) + b2_r[i].astype(F32)

    def reduce_b(hop):
        for chain, to, n in ((b_long, right, g.long), (b_short, left, g.short)):
            if hop < n:
                i, b = chain[hop]
                v = b_sum(i, b)
                if hop:
                    arrive(bz_r.at[i - 1], bzz_s.at[i - 1], bzz_r.at[i - 1], sibling)
                    v = v + bz_r[i - 1].astype(F32)
                bz_s[i] = v.astype(BF)
                send(bz_s.at[i], bz_r.at[i], bzz_s.at[i], bzz_r.at[i], to)

    order = [x_far, x_up, x_down, x]

    def chip_b(k):
        lo = pl.multiple_of(order[k] * g.cols + g.ra, LANES)
        pb[order[k]] = partial(lo, g.rb).reshape(Z, g.G, g.rb)

    picked = jnp.dot(sel[...], lb[...], preferred_element_type=F32).astype(BF)
    msg[...] = picked.reshape(Z, g.M, g.T)
    r1[z] = msg[z]
    chip_b(0)
    for i, b in b_order:
        b_first(i, b)
    chip_b(1)
    chip_b(2)
    for i, b in b_order:
        b_direct(i, b)
    for xx in range(X):
        pa[xx] = partial(xx * g.cols, g.ra).reshape(Z, g.G, g.ra)
        reduce_a(0, xx)
    for k in range(1, Z):
        zz = _mod(z + k, Z)
        send(msg.at[zz], r1.at[z], m1_s.at[k - 1], m1_r.at[k - 1], at_z(zz))
    half = Z // 2
    for i, b in b_order[0:half]:
        b_second(i, b)
    for xx in range(X):
        reduce_a(1, xx)
    chip_b(3)
    for i, b in b_order[half:]:
        b_second(i, b)
    reduce_b(0)

    for xx in range(X):
        reduce_a(2, xx)
    reduce_b(1)
    for xx in range(X):
        reduce_a(3, xx)
    reduce_b(2)
    for k in range(1, Z):
        arrive(r1.at[_mod(z - k, Z)], m1_s.at[k - 1], m1_r.at[k - 1], sibling)
    m2[...] = jnp.dot(
        regroup[...], r1[...].reshape(Z * g.M, g.T), preferred_element_type=F32
    ).astype(BF).reshape(YC, g.M, g.T)
    r2[yc] = m2[yc]
    for i, peer, _, _ in yc_peers:
        send(m2.at[peer], r2.at[yc], m2_s.at[i], m2_r.at[i], at_yc(peer))

    for xx in range(X):
        v = own_a(z, xx)
        i = (g.long - 1) * X + xx
        arrive(ring_rl.at[g.long - 1, xx], rz_s.at[i], rz_r.at[i], sibling)
        v = v + ring_rl[g.long - 1, xx].astype(F32)
        i = (g.long + g.short - 1) * X + xx
        arrive(ring_rs.at[g.short - 1, xx], rz_s.at[i], rz_r.at[i], sibling)
        v = v + ring_rs[g.short - 1, xx].astype(F32)
        pa[xx, z] = v
        ax_s[xx] = v.astype(BF)
    for k in range(1, X):
        xx = _mod(x + k, X)
        send(ax_s.at[xx], ax_r.at[k - 1], axx_s.at[k - 1], axx_r.at[k - 1], at_x(xx))
    reduce_b(3)

    va = pa[x, z]
    for k in range(1, X):
        arrive(ax_r.at[k - 1], axx_s.at[k - 1], axx_r.at[k - 1], sibling)
        va = va + ax_r[k - 1].astype(F32)
    vb = b_sum(*b_own)
    for i in (g.long - 1, g.long + g.short - 1):
        arrive(bz_r.at[i], bzz_s.at[i], bzz_r.at[i], sibling)
        vb = vb + bz_r[i].astype(F32)
    for k in range(YC):
        fin_s[k, :, 0:g.ra] = va[k * g.t:(k + 1) * g.t]
        fin_s[k, :, g.ra:g.cols] = vb[k * g.t:(k + 1) * g.t]
    fin_r[yc] = fin_s[yc]
    for i, peer, _, _ in yc_peers:
        send(fin_s.at[peer], fin_r.at[yc], f_s.at[i], f_r.at[i], at_yc(peer))

    for i in range(Z):
        hop = i if i <= g.long else g.long - i
        b = _mod(z + hop * step, Z)
        arrive(buf_a.at[other, b], sa_s.at[i], sa_r.at[i], sibling)
        arrive(buf_b.at[other, :, b], sb_s.at[i], sb_r.at[i], sibling)

    for i, _, _, origin in yc_peers:
        arrive(r2.at[origin], m2_s.at[i], m2_r.at[i], sibling)
    wide = widened(g, own_code[...], r2)
    g_rows = jnp.concatenate([wide[1], wide[2]], axis=0)
    for xx in range(X):
        for lo, width, rows in (
            (xx * g.cols, g.a, rows_a),
            (xx * g.cols + g.a, g.b, rows_b),
        ):
            both = jnp.dot(g_rows, rows(0, xx), preferred_element_type=F32).astype(BF)
            g_gate[:, lo:lo + width] = both[0:g.wide]
            g_up[:, lo:lo + width] = both[g.W8:g.W8 + g.wide]
            down = jnp.dot(wide[0], rows(1, xx), preferred_element_type=F32).astype(BF)
            g_down[:, lo:lo + width] = down[0:g.wide]
    stores = [
        pltpu.make_async_copy(v, h, o_sem.at[i])
        for i, (v, h) in enumerate(((g_gate, gg_h), (g_up, gu_h), (g_down, gd_h)))
    ]
    for op in stores:
        op.start()

    for op in sent:
        op.wait_send()
    for i, _, _, origin in yc_peers:
        arrive(fin_r.at[origin], f_s.at[i], f_r.at[i], sibling)
    for k, out in enumerate((o_in, o_out)):
        total = fin_r[k]
        for yy in range(1, Y):
            total = total + fin_r[yy * CORES + k]
        out[...] = total.astype(BF)

    for op in stores:
        op.wait()


def routing(g, codes, ss, flat):
    n, Z, YC = g.dp, g.Z, g.YC
    c = codes[...].reshape(n, LANES).astype(I32)
    local = (c >> 1) - flat * g.src
    owned = (local >= 0) & (local < g.src)
    loc = local.astype(F32)
    flg = (c & 1).astype(F32)
    ownf = jnp.where(owned, 1.0, 0.0)
    before = lax.broadcasted_iota(I32, (LANES, LANES), 0) < lax.broadcasted_iota(I32, (LANES, LANES), 1)
    rank = jnp.dot(ownf.astype(BF), jnp.where(before, 1.0, 0.0).astype(BF), preferred_element_type=F32)
    lane = lax.broadcasted_iota(I32, (n, LANES), 1).astype(F32)
    wide_lane = lax.broadcasted_iota(I32, (n, 2 * LANES), 1).astype(F32)
    picks = []
    share = jnp.zeros((1, LANES), F32)
    for k in range(SLOTS):
        chosen = jnp.where(rank == float(k), ownf, 0.0)
        idx = jnp.sum(chosen * loc, axis=1, keepdims=True)
        has = jnp.sum(chosen, axis=1, keepdims=True)
        fl = jnp.sum(chosen * flg, axis=1, keepdims=True)
        one = jnp.where(lane == idx, has, 0.0)
        share = share + jnp.sum(one * fl, axis=0, keepdims=True)
        picks.append((idx, has, fl, one))
    for k, (idx, has, fl, one) in enumerate(picks):
        total = jnp.sum(one * share, axis=1, keepdims=True)
        scale = jnp.where(has > 0.0, fl / jnp.where(has > 0.0, total, 1.0), 0.0)
        for kind, (offset, factor) in enumerate(
            ((0.0, has), (float(LANES), scale), (float(LANES + g.R), scale))
        ):
            q = k * 3 + kind
            ss[q * n:(q + 1) * n, :] = jnp.where(wide_lane == idx + offset, factor, 0.0).astype(BF)


def row_parts(g, groups):
    per = 3 * SLOTS
    row = lax.broadcasted_iota(I32, (g.Z * g.M, 1), 0).astype(F32)
    block = jnp.floor((row + 0.5) * (1.0 / g.M))
    rest = row - block * g.M
    inner = jnp.floor((rest + 0.5) * (1.0 / per))
    return block, inner, rest - inner * per, rest < float(groups * per)


def spread_rows(g, spread):
    block, inner, q, valid = row_parts(g, g.YC)
    want = jnp.where(valid, q * g.dp + block * g.YC + inner, -1.0)
    col = lax.broadcasted_iota(I32, spread.shape, 1).astype(F32)
    spread[...] = jnp.where(col == want, 1.0, 0.0).astype(BF)


def regroup_rows(g, regroup):
    block, inner, q, valid = row_parts(g, g.Z)
    want = jnp.where(valid, inner * g.M + block * (3.0 * SLOTS) + q, -1.0)
    col = lax.broadcasted_iota(I32, regroup.shape, 1).astype(F32)
    regroup[...] = jnp.where(col == want, 1.0, 0.0).astype(BF)


def widened(g, code_row, r2):
    src = (code_row >> 1).astype(F32)
    owner = jnp.floor((src + 0.5) * (1.0 / (g.src * g.X)))
    zz = jnp.floor((owner + 0.5) * (1.0 / g.YC))
    first = (owner - zz * g.YC) * g.M + zz * (3.0 * SLOTS)
    sub = lax.broadcasted_iota(I32, (LANES, LANES), 0)
    lane = lax.broadcasted_iota(I32, (LANES, LANES), 1)
    owners = jnp.broadcast_to(owner, (LANES, LANES))
    own_col = jnp.sum(jnp.where(sub == lane, owners, 0.0), axis=1, keepdims=True)
    first_col = jnp.sum(
        jnp.where(sub == lane, jnp.broadcast_to(first, (LANES, LANES)), 0.0), axis=1, keepdims=True
    )
    earlier = jnp.sum(
        jnp.where((owners == own_col) & (lane < sub), 1.0, 0.0), axis=1, keepdims=True
    )
    target = (first_col + 3.0 * earlier)[0:g.W8]
    n = g.YC * g.M
    pos = lax.broadcasted_iota(I32, (g.W8, n), 1).astype(F32)
    columns = r2[...].reshape(n, g.T)
    return [
        jnp.dot(
            jnp.where(pos == target + float(kind), 1.0, 0.0).astype(BF),
            columns, preferred_element_type=F32,
        ).astype(BF)
        for kind in range(3)
    ]


PARTS = 4


def hand_over(n, *refs):
    ins, outs, bufs, (sem_in, sem_out) = refs[:n], refs[n:2 * n], refs[2 * n:3 * n], refs[3 * n:]
    steps = []
    for i in range(n):
        cols = ins[i].shape[1]
        width = cols // PARTS if cols % (PARTS * LANES) == 0 else cols
        for lo in range(0, cols, width):
            k, part = len(steps), (slice(None), pl.ds(lo, width))
            steps.append((
                pltpu.make_async_copy(ins[i].at[part], bufs[i].at[part], sem_in.at[k]),
                pltpu.make_async_copy(bufs[i].at[part], outs[i].at[part], sem_out.at[k]),
            ))
    for fetch, _ in steps:
        fetch.start()
    for fetch, store in steps:
        fetch.wait()
        store.start()
    for _, store in steps:
        store.wait()


def per_device(tokens, grad_out, gate_src, up_src, down_src, unit_map, copy_flag):
    g = Geometry(
        lax.axis_size("dp"), lax.axis_size("mp"), tokens.shape[0], tokens.shape[1],
        gate_src.shape[0], unit_map.shape[0],
    )
    X, Z, YC = g.X, g.Z, g.YC
    V = pltpu.VMEM
    dma = pltpu.SemaphoreType.DMA

    def pair(n):
        return [dma((max(n, 1),)), dma((max(n, 1),))]

    scratch = [
        V((2, g.t, g.cols + LANES), F32), V((YC, g.t, g.cols + LANES), F32), V((g.G, g.cols), F32),
        V((Z, YC, LANES), F32), V((1, LANES), I32),
        V((2, Z, X, g.G, g.a), BF), V((2, X, Z, g.G, g.b), BF),
        V((3, *gate_src.shape), BF), V((2, g.R, g.D), BF), V((4 * g.R, g.D), BF),
        V((4 * g.R, g.T), F32), V((4 * g.R, g.T), F32),
        V((2 * LANES, g.T), F32), V((2 * LANES, g.T), BF), V((g.T, 2 * LANES), BF),
        V((3 * SLOTS * g.dp, 2 * LANES), BF), V((Z * g.M, 3 * SLOTS * g.dp), BF), V((Z * g.M, Z * g.M), BF),
        V((Z * g.M, 2 * LANES), BF),
        V((Z, g.M, g.T), BF), V((Z, g.M, g.T), BF), V((YC, g.M, g.T), BF), V((YC, g.M, g.T), BF),
        V((X, Z, g.G, g.ra), F32), V((X, Z, g.G, g.rb), F32),
        V((g.long, X, g.G, g.ra), BF), V((g.long, X, g.G, g.ra), BF),
        V((g.short, X, g.G, g.ra), BF), V((g.short, X, g.G, g.ra), BF),
        V((X, g.G, g.ra), BF), V((X - 1, g.G, g.ra), BF),
        *[V((Z, g.G, g.rb), BF) for _ in range(6)],
        V((Z - 1, g.G, g.rb), BF), V((Z - 1, g.G, g.rb), BF),
        V((YC, g.t, g.cols), F32), V((YC, g.t, g.cols), F32),
        V((g.wide, g.D), BF), V((g.wide, g.D), BF), V((g.wide, g.D), BF),
        dma((3,)), dma((3,)),
    ]
    counts = [
        YC, Z - 1, X - 1, (Z - 1) * X, Z - 1, 3 * Z, Z, Z, Z - 1, YC, 2, 1,
        (Z - 1) * X, X - 1, 3 * Z, Z - 1, YC,
    ]
    for n in counts:
        scratch += pair(n)
    vm = pl.BlockSpec(memory_space=pltpu.VMEM)
    anyw = pl.BlockSpec(memory_space=pl.ANY)
    wide_shape = jax.ShapeDtypeStruct((g.wide, g.D), BF)
    tok_shape = jax.ShapeDtypeStruct(tokens.shape, BF)
    macs = 6 * g.T * g.src * g.D + 3 * g.T * g.wide * g.D
    results = pl.pallas_call(
        functools.partial(kernel, g),
        out_shape=(tok_shape, tok_shape, wide_shape, wide_shape, wide_shape),
        in_specs=[vm, vm, anyw, anyw, anyw, vm, vm],
        out_specs=(vm, vm, anyw, anyw, anyw),
        scratch_shapes=scratch,
        compiler_params=pltpu.CompilerParams(
            collective_id=0, has_side_effects=True, vmem_limit_bytes=56 * 1024 * 1024
        ),
        cost_estimate=pl.CostEstimate(
            flops=2 * macs, bytes_accessed=3 * 2 * g.D * (g.src + g.wide), transcendentals=g.T * g.src
        ),
        name="widened_layer",
    )(
        tokens, grad_out, gate_src, up_src, down_src,
        unit_map.reshape(1, -1), copy_flag.reshape(1, -1),
    )
    return pl.pallas_call(
        functools.partial(hand_over, len(results)),
        out_shape=tuple(jax.ShapeDtypeStruct(r.shape, r.dtype) for r in results),
        in_specs=[anyw] * len(results),
        out_specs=(anyw,) * len(results),
        scratch_shapes=[V(r.shape, r.dtype) for r in results] + [dma((len(results) * PARTS,))] * 2,
        cost_estimate=pl.CostEstimate(flops=0, bytes_accessed=12 * g.wide * g.D, transcendentals=0),
        name="hand_over",
    )(*results)


def solution(mesh):
    in_specs = (
        P("dp", "mp"),
        P("dp", "mp"),
        P(("dp", "mp"), None),
        P(("dp", "mp"), None),
        P(("dp", "mp"), None),
        P(("dp", "mp")),
        P(("dp", "mp")),
    )
    out_specs = (
        P("dp", "mp"),
        P("dp", "mp"),
        P(("dp", "mp"), None),
        P(("dp", "mp"), None),
        P(("dp", "mp"), None),
    )
    return jax.shard_map(
        per_device, mesh=mesh, in_specs=in_specs, out_specs=out_specs, check_vma=False
    )
```

```python
import functools

import jax
import jax.numpy as jnp
from jax import lax
from jax.experimental import pallas as pl
from jax.experimental.pallas import tpu as pltpu
from jax.sharding import PartitionSpec as P

MESH = pl.DeviceIdType.MESH
BF = jnp.bfloat16
F32 = jnp.float32
I32 = jnp.int32

CORES = 2
CHIPS_Y = 4
SLOTS = 3
LANES = 128


def _mod(v, n):
    return lax.rem(v + n, n)


class Geometry:
    def __init__(self, n_dp, n_mp, tokens_dev, cols, src, wide):
        self.Y = CHIPS_Y
        self.YC = CHIPS_Y * CORES
        self.Z = n_dp // self.YC
        self.X = n_mp
        self.dp = n_dp
        self.t = tokens_dev
        self.T = n_dp * tokens_dev
        self.G = self.YC * tokens_dev
        self.cols = cols
        tiles = cols // LANES
        self.a = (tiles // 2) * LANES
        self.b = cols - self.a
        self.ra = (tiles // 2 + 1) * LANES
        self.rb = cols - self.ra
        self.D = cols * n_mp
        self.src = src
        self.R = -(-src // 16) * 16
        self.wide = wide
        self.W8 = -(-wide // 8) * 8
        self.long = self.Z // 2
        self.short = self.Z - 1 - self.long
        self.M = -(-(self.YC * 3 * SLOTS) // 16) * 16


def kernel(g, *refs):
    (tok, gro, gate_h, up_h, down_h, umap, flag, o_out, o_in, gg_h, gu_h, gd_h) = refs[:12]
    (
        s1_src, s1_rcv, asm, codes, own_code,
        buf_a, buf_b,
        w_own, w_out, ws,
        pre_s, pre_r, lf, lb, lt,
        ss, spread, regroup, sel, msg, r1, m2, r2,
        pa, pb,
        ring_sl, ring_rl, ring_ss, ring_rs, ax_s, ax_r,
        b1_s, b1_r, b2_s, b2_r, bd_s, bd_r, bz_s, bz_r,
        fin_s, fin_r,
        g_gate, g_up, g_down,
        w_sem, o_sem,
        s1_ss, s1_rs, cz_ss, cz_rs, ga_xs, ga_xr, ga_zs, ga_zr, gb_zs, gb_zr, gb_xs, gb_xr,
        sa_s, sa_r, sb_s, sb_r,
        m1_s, m1_r, m2_s, m2_r,
        wx_s, wx_r, px_s, px_r,
        rz_s, rz_r, axx_s, axx_r, bxx_s, bxx_r, bzz_s, bzz_r, f_s, f_r,
    ) = refs[12:]
    X, Y, Z, YC = g.X, g.Y, g.Z, g.YC
    dp = lax.axis_index("dp")
    x = lax.axis_index("mp")
    z = lax.div(dp, YC)
    yc = lax.rem(dp, YC)
    y = lax.div(yc, CORES)
    c = lax.rem(yc, CORES)
    other = 1 - c
    step = 1 - 2 * c

    def at_z(zz):
        return (zz * YC + yc, x)

    def at_x(xx):
        return (dp, xx)

    def at_yc(k):
        return (z * YC + k, x)

    sibling = at_yc(y * CORES + other)
    yc_peers = []
    for dy in range(Y):
        for dc in range(CORES):
            if dy or dc:
                py = _mod(y + dy, Y)
                pc = _mod(c + dc, CORES)
                qy = _mod(y - dy, Y)
                yc_peers.append((dy * CORES + dc, py * CORES + pc, pc, qy * CORES + pc))

    sent = []

    def copy(src, dst, s_sem, r_sem, device):
        return pltpu.make_async_remote_copy(
            src_ref=src, dst_ref=dst, send_sem=s_sem, recv_sem=r_sem,
            device_id=device, device_id_type=MESH,
        )

    def send(src, dst, s_sem, r_sem, device):
        op = copy(src, dst, s_sem, r_sem, device)
        op.start()
        sent.append(op)

    def arrive(dst, s_sem, r_sem, device):
        copy(dst, dst, s_sem, r_sem, device).wait_recv()

    bar = pltpu.get_barrier_semaphore()
    for k in range(1, X):
        pl.semaphore_signal(bar, inc=1, device_id=at_x(_mod(x + k, X)), device_id_type=MESH)
    for k in range(1, Z):
        pl.semaphore_signal(bar, inc=1, device_id=at_z(_mod(z + k, Z)), device_id_type=MESH)
    for _, peer, _, _ in yc_peers:
        pl.semaphore_signal(bar, inc=1, device_id=at_yc(peer), device_id_type=MESH)

    loads = [
        pltpu.make_async_copy(h, w_own.at[i], w_sem.at[i])
        for i, h in enumerate((gate_h, up_h, down_h))
    ]
    for op in loads:
        op.start()

    code = umap[...] * 2 + flag[...]
    own_code[...] = jnp.full(own_code.shape, -1, I32)
    own_code[:, 0:g.wide] = code
    code_row = own_code[...]
    s1_src[0, :, 0:g.cols] = tok[...].astype(F32)
    s1_src[1, :, 0:g.cols] = gro[...].astype(F32)
    for k in range(2):
        s1_src[k, :, g.cols:g.cols + LANES] = jnp.broadcast_to(code_row.astype(F32), (g.t, LANES))
    s1_rcv[yc] = s1_src[c]

    pl.semaphore_wait(bar, (X - 1) + (Z - 1) + len(yc_peers))

    for i, peer, pc, _ in yc_peers:
        send(s1_src.at[pc], s1_rcv.at[yc], s1_ss.at[i], s1_rs.at[i], at_yc(peer))
    for i, _, _, origin in yc_peers:
        arrive(s1_rcv.at[origin], s1_ss.at[i], s1_rs.at[i], sibling)
    for k in range(YC):
        asm[k * g.t:(k + 1) * g.t, :] = s1_rcv[k, :, 0:g.cols]
        codes[z, k:k + 1, :] = s1_rcv[k, 0:1, g.cols:g.cols + LANES]
    block = asm[...].astype(BF)
    buf_a[c, z, x] = block[:, 0:g.a]
    buf_b[c, x, z] = block[:, g.a:g.cols]

    right, left = at_z(_mod(z + step, Z)), at_z(_mod(z - step, Z))
    a_cols = [x] + [_mod(x - k, X) for k in range(1, X)]

    def slots_at(hop):
        out = [(hop, _mod(z - hop * step, Z))]
        if 1 <= hop <= g.short:
            out.append((g.long + hop, _mod(z + hop * step, Z)))
        return out

    def a_forward(hop, j):
        if hop < g.long:
            ref = buf_a.at[c, _mod(z - hop * step, Z), a_cols[j]]
            i = hop * X + j
            send(ref, ref, ga_zs.at[i], ga_zr.at[i], right)
        if hop < g.short:
            ref = buf_a.at[c, _mod(z + hop * step, Z), a_cols[j]]
            i = (g.long + hop) * X + j
            send(ref, ref, ga_zs.at[i], ga_zr.at[i], left)

    def a_arrive(hop, j):
        i = (hop - 1) * X + j
        arrive(buf_a.at[c, _mod(z - hop * step, Z), a_cols[j]], ga_zs.at[i], ga_zr.at[i], sibling)
        if hop <= g.short:
            i = (g.long + hop - 1) * X + j
            arrive(buf_a.at[c, _mod(z + hop * step, Z), a_cols[j]], ga_zs.at[i], ga_zr.at[i], sibling)

    def b_forward(hop):
        if hop < g.long:
            ref = buf_b.at[c, x, _mod(z - hop * step, Z)]
            send(ref, ref, gb_zs.at[hop], gb_zr.at[hop], right)
        if hop < g.short:
            ref = buf_b.at[c, x, _mod(z + hop * step, Z)]
            i = g.long + hop
            send(ref, ref, gb_zs.at[i], gb_zr.at[i], left)

    def b_arrive(hop):
        arrive(buf_b.at[c, x, _mod(z - hop * step, Z)], gb_zs.at[hop - 1], gb_zr.at[hop - 1], sibling)
        if hop <= g.short:
            i = g.long + hop - 1
            arrive(buf_b.at[c, x, _mod(z + hop * step, Z)], gb_zs.at[i], gb_zr.at[i], sibling)

    x_up, x_down, x_far = _mod(x + 1, X), _mod(x - 1, X), _mod(x + 2, X)

    def b_across(i, b, last=False):
        ref = buf_b.at[c, x, b]
        if last:
            send(ref, ref, gb_xs.at[3 * i + 2], gb_xr.at[3 * i + 2], at_x(x_far))
        send(ref, ref, gb_xs.at[3 * i], gb_xr.at[3 * i], at_x(x_up))
        send(ref, ref, gb_xs.at[3 * i + 1], gb_xr.at[3 * i + 1], at_x(x_down))

    def b_beside(i, b):
        arrive(buf_b.at[c, x_down, b], gb_xs.at[3 * i], gb_xr.at[3 * i], sibling)
        arrive(buf_b.at[c, x_up, b], gb_xs.at[3 * i + 1], gb_xr.at[3 * i + 1], sibling)

    def b_pass_on(i, b):
        b_beside(i, b)
        way = 1 - 2 * lax.rem(b, 2)
        ref = buf_b.at[c, _mod(x - way, X), b]
        send(ref, ref, gb_xs.at[3 * i + 2], gb_xr.at[3 * i + 2], at_x(_mod(x + way, X)))

    def b_share(i, b):
        arrive(buf_b.at[c, x_far, b], gb_xs.at[3 * i + 2], gb_xr.at[3 * i + 2], sibling)
        ref = buf_b.at[c, :, b]
        send(ref, ref, sb_s.at[i], sb_r.at[i], sibling)

    def a_share(i, b):
        ref = buf_a.at[c, b]
        send(ref, ref, sa_s.at[i], sa_r.at[i], sibling)

    b_forward(0)
    for k in range(1, X):
        ref = buf_a.at[c, z, x]
        send(ref, ref, ga_xs.at[k - 1], ga_xr.at[k - 1], at_x(_mod(x + k, X)))
    a_forward(0, 0)
    b_across(0, z)
    for k in range(1, Z):
        send(codes.at[z], codes.at[z], cz_ss.at[k - 1], cz_rs.at[k - 1], at_z(_mod(z + k, Z)))

    for op in loads:
        op.wait()
    if g.R > g.src:
        pad = jnp.zeros((16, g.D), BF)
        w_out[0, g.R - 16:g.R, :] = pad
        w_out[1, g.R - 16:g.R, :] = pad
        ws[g.R - 16:g.R, :] = pad
        ws[3 * g.R - 16:3 * g.R, :] = pad
    w_out[0, 0:g.src, :] = w_own[2 * other]
    w_out[1, 0:g.src, :] = w_own[1]
    for k in range(2):
        rows = ws.at[pl.ds((2 * k + 1) * g.R, g.R)]
        send(w_out.at[k], rows, wx_s.at[k], wx_r.at[k], sibling)
    ws[0:g.src, :] = w_own[2 * c]
    ws[2 * g.R:2 * g.R + g.src, :] = w_own[1]
    spread_rows(g, spread)

    for k in (1, X - 1, *range(2, X - 1)):
        arrive(buf_a.at[c, z, _mod(x - k, X)], ga_xs.at[k - 1], ga_xr.at[k - 1], sibling)
        a_forward(0, k)
    a_share(0, z)
    for hop in range(1, g.long + 1):
        b_arrive(hop)
        b_forward(hop)
        for i, b in slots_at(hop):
            b_across(i, b, last=hop == g.long)
        for i, b in slots_at(hop - 1):
            b_pass_on(i, b)
        for j in (0, 1, X - 1, *range(2, X - 1)):
            a_arrive(hop, j)
            a_forward(hop, j)
        for i, b in slots_at(hop):
            a_share(i, b)
        if hop > 1:
            for i, b in slots_at(hop - 2):
                b_share(i, b)
    for k in range(1, Z):
        arrive(codes.at[_mod(z - k, Z)], cz_ss.at[k - 1], cz_rs.at[k - 1], sibling)
    routing(g, codes, ss, dp * X + x)
    for i, b in slots_at(g.long):
        b_beside(i, b)
    for hop in (g.long - 1, g.long):
        for i, b in slots_at(hop):
            b_share(i, b)
    sel[...] = jnp.dot(spread[...], ss[...], preferred_element_type=F32).astype(BF)
    regroup_rows(g, regroup)

    nt = (((1,), (1,)), ((), ()))

    def rows_a(array, xx):
        return buf_a[array, :, xx].reshape(g.T, g.a)

    def rows_b(array, xx):
        return buf_b[array, xx].reshape(g.T, g.b)

    for k in range(2):
        rows = ws.at[pl.ds((2 * k + 1) * g.R, g.R)]
        arrive(rows, wx_s.at[k], wx_r.at[k], sibling)
    pre = jnp.zeros((4 * g.R, g.T), F32)
    for xx in range(X):
        lo, mid, hi = xx * g.cols, xx * g.cols + g.a, (xx + 1) * g.cols
        pre += lax.dot_general(ws[:, lo:mid], rows_a(c, xx), nt, preferred_element_type=F32)
        pre += lax.dot_general(ws[:, mid:hi], rows_b(c, xx), nt, preferred_element_type=F32)
    pre_s[...] = pre
    send(pre_s, pre_r, px_s.at[0], px_r.at[0], sibling)
    arrive(pre_r, px_s.at[0], px_r.at[0], sibling)

    def turned(lo):
        return jnp.concatenate([pre_r[lo + g.R:lo + 2 * g.R], pre_r[lo:lo + g.R]], axis=0)

    first = c == 0
    pre_gate = jnp.where(first, pre_s[0:2 * g.R], turned(0))
    pre_up = jnp.where(first, pre_s[2 * g.R:4 * g.R], turned(2 * g.R))
    gh = jnp.where(first, turned(0), pre_s[0:2 * g.R])
    sigma = jax.nn.sigmoid(pre_gate)
    active = pre_gate * sigma
    hidden = active * pre_up
    d_gate = gh * pre_up * (sigma + active * (1.0 - sigma))
    d_up = gh * active
    lf[...] = jnp.zeros(lf.shape, F32)
    lf[0:2 * g.R, :] = jnp.where(first, d_gate, hidden)
    lf[2 * g.R:4 * g.R, :] = jnp.where(first, d_up, 0.0)
    for k in range(2):
        lt[:, k * LANES:(k + 1) * LANES] = lf[k * LANES:(k + 1) * LANES, :].T.astype(BF)
    lf[...] = jnp.zeros(lf.shape, F32)
    lf[0:g.R, :] = hidden[0:g.R]
    lf[LANES:LANES + g.R, :] = d_gate[0:g.R]
    lf[LANES + g.R:LANES + 2 * g.R, :] = d_up[0:g.R]
    lb[...] = lf[...].astype(BF)

    def partial(lo, width):
        return jnp.dot(lt[:, 0:4 * g.R], ws[:, pl.ds(lo, width)], preferred_element_type=F32)

    def own_a(b, xx):
        return pa[xx, b]

    def reduce_a(hop, xx):
        if hop < g.long:
            v = own_a(_mod(z + (g.long - hop) * step, Z), xx)
            if hop:
                i = (hop - 1) * X + xx
                arrive(ring_rl.at[hop - 1, xx], rz_s.at[i], rz_r.at[i], sibling)
                v = v + ring_rl[hop - 1, xx].astype(F32)
            ring_sl[hop, xx] = v.astype(BF)
            i = hop * X + xx
            send(ring_sl.at[hop, xx], ring_rl.at[hop, xx], rz_s.at[i], rz_r.at[i], right)
        if hop < g.short:
            v = own_a(_mod(z - (g.short - hop) * step, Z), xx)
            if hop:
                i = (g.long + hop - 1) * X + xx
                arrive(ring_rs.at[hop - 1, xx], rz_s.at[i], rz_r.at[i], sibling)
                v = v + ring_rs[hop - 1, xx].astype(F32)
            ring_ss[hop, xx] = v.astype(BF)
            i = (g.long + hop) * X + xx
            send(ring_ss.at[hop, xx], ring_rs.at[hop, xx], rz_s.at[i], rz_r.at[i], left)

    b_long = [(h, _mod(z + (g.long - h) * step, Z)) for h in range(g.long)]
    b_short = [(g.long + h, _mod(z - (g.short - h) * step, Z)) for h in range(g.short)]
    b_own = (Z - 1, z)
    b_order = []
    for h in range(g.long):
        b_order.append(b_long[h])
        if h < g.short:
            b_order.append(b_short[h])
    b_order.append(b_own)

    def way_of(b):
        return 1 - 2 * lax.rem(b, 2)

    def b_first(i, b):
        b1_s[i] = pb[x_far, b].astype(BF)
        send(b1_s.at[i], b1_r.at[i], bxx_s.at[3 * i], bxx_r.at[3 * i], at_x(_mod(x + way_of(b), X)))

    def b_direct(i, b):
        to = _mod(x - way_of(b), X)
        bd_s[i] = pb[to, b].astype(BF)
        send(bd_s.at[i], bd_r.at[i], bxx_s.at[3 * i + 1], bxx_r.at[3 * i + 1], at_x(to))

    def b_second(i, b):
        to = _mod(x + way_of(b), X)
        arrive(b1_r.at[i], bxx_s.at[3 * i], bxx_r.at[3 * i], sibling)
        b2_s[i] = (pb[to, b] + b1_r[i].astype(F32)).astype(BF)
        send(b2_s.at[i], b2_r.at[i], bxx_s.at[3 * i + 2], bxx_r.at[3 * i + 2], at_x(to))

    def b_sum(i, b):
        arrive(bd_r.at[i], bxx_s.at[3 * i + 1], bxx_r.at[3 * i + 1], sibling)
        arrive(b2_r.at[i], bxx_s.at[3 * i + 2], bxx_r.at[3 * i + 2], sibling)
        return pb[x, b] + bd_r[i].astype(F32) + b2_r[i].astype(F32)

    def reduce_b(hop):
        for chain, to, n in ((b_long, right, g.long), (b_short, left, g.short)):
            if hop < n:
                i, b = chain[hop]
                v = b_sum(i, b)
                if hop:
                    arrive(bz_r.at[i - 1], bzz_s.at[i - 1], bzz_r.at[i - 1], sibling)
                    v = v + bz_r[i - 1].astype(F32)
                bz_s[i] = v.astype(BF)
                send(bz_s.at[i], bz_r.at[i], bzz_s.at[i], bzz_r.at[i], to)

    order = [x_far, x_up, x_down, x]

    def chip_b(k):
        lo = pl.multiple_of(order[k] * g.cols + g.ra, LANES)
        pb[order[k]] = partial(lo, g.rb).reshape(Z, g.G, g.rb)

    picked = jnp.dot(sel[...], lb[...], preferred_element_type=F32).astype(BF)
    msg[...] = picked.reshape(Z, g.M, g.T)
    r1[z] = msg[z]
    for k in range(1, Z):
        zz = _mod(z + k, Z)
        send(msg.at[zz], r1.at[z], m1_s.at[k - 1], m1_r.at[k - 1], at_z(zz))
    chip_b(0)
    for i, b in b_order:
        b_first(i, b)
    chip_b(1)
    chip_b(2)
    for i, b in b_order:
        b_direct(i, b)
    for xx in range(X):
        pa[xx] = partial(xx * g.cols, g.ra).reshape(Z, g.G, g.ra)
        reduce_a(0, xx)
    half = Z // 2
    for i, b in b_order[0:half]:
        b_second(i, b)
    for xx in range(X):
        reduce_a(1, xx)
    chip_b(3)
    for i, b in b_order[half:]:
        b_second(i, b)
    reduce_b(0)

    for xx in range(X):
        reduce_a(2, xx)
    reduce_b(1)
    for xx in range(X):
        reduce_a(3, xx)
    reduce_b(2)
    for k in range(1, Z):
        arrive(r1.at[_mod(z - k, Z)], m1_s.at[k - 1], m1_r.at[k - 1], sibling)
    m2[...] = jnp.dot(
        regroup[...], r1[...].reshape(Z * g.M, g.T), preferred_element_type=F32
    ).astype(BF).reshape(YC, g.M, g.T)
    r2[yc] = m2[yc]
    for i, peer, _, _ in yc_peers:
        send(m2.at[peer], r2.at[yc], m2_s.at[i], m2_r.at[i], at_yc(peer))

    for xx in range(X):
        v = own_a(z, xx)
        i = (g.long - 1) * X + xx
        arrive(ring_rl.at[g.long - 1, xx], rz_s.at[i], rz_r.at[i], sibling)
        v = v + ring_rl[g.long - 1, xx].astype(F32)
        i = (g.long + g.short - 1) * X + xx
        arrive(ring_rs.at[g.short - 1, xx], rz_s.at[i], rz_r.at[i], sibling)
        v = v + ring_rs[g.short - 1, xx].astype(F32)
        pa[xx, z] = v
        ax_s[xx] = v.astype(BF)
    for k in range(1, X):
        xx = _mod(x + k, X)
        send(ax_s.at[xx], ax_r.at[k - 1], axx_s.at[k - 1], axx_r.at[k - 1], at_x(xx))
    reduce_b(3)

    va = pa[x, z]
    for k in range(1, X):
        arrive(ax_r.at[k - 1], axx_s.at[k - 1], axx_r.at[k - 1], sibling)
        va = va + ax_r[k - 1].astype(F32)
    vb = b_sum(*b_own)
    for i in (g.long - 1, g.long + g.short - 1):
        arrive(bz_r.at[i], bzz_s.at[i], bzz_r.at[i], sibling)
        vb = vb + bz_r[i].astype(F32)
    for k in range(YC):
        fin_s[k, :, 0:g.ra] = va[k * g.t:(k + 1) * g.t]
        fin_s[k, :, g.ra:g.cols] = vb[k * g.t:(k + 1) * g.t]
    fin_r[yc] = fin_s[yc]
    for i, peer, _, _ in yc_peers:
        send(fin_s.at[peer], fin_r.at[yc], f_s.at[i], f_r.at[i], at_yc(peer))

    for i in range(Z):
        hop = i if i <= g.long else g.long - i
        b = _mod(z + hop * step, Z)
        arrive(buf_a.at[other, b], sa_s.at[i], sa_r.at[i], sibling)
        arrive(buf_b.at[other, :, b], sb_s.at[i], sb_r.at[i], sibling)

    for i, _, _, origin in yc_peers:
        arrive(r2.at[origin], m2_s.at[i], m2_r.at[i], sibling)
    wide = widened(g, own_code[...], r2)
    g_rows = jnp.concatenate([wide[1], wide[2]], axis=0)
    for xx in range(X):
        for lo, width, rows in (
            (xx * g.cols, g.a, rows_a),
            (xx * g.cols + g.a, g.b, rows_b),
        ):
            both = jnp.dot(g_rows, rows(0, xx), preferred_element_type=F32).astype(BF)
            g_gate[:, lo:lo + width] = both[0:g.wide]
            g_up[:, lo:lo + width] = both[g.W8:g.W8 + g.wide]
            down = jnp.dot(wide[0], rows(1, xx), preferred_element_type=F32).astype(BF)
            g_down[:, lo:lo + width] = down[0:g.wide]
    stores = [
        pltpu.make_async_copy(v, h, o_sem.at[i])
        for i, (v, h) in enumerate(((g_gate, gg_h), (g_up, gu_h), (g_down, gd_h)))
    ]
    for op in stores:
        op.start()

    for op in sent:
        op.wait_send()
    for i, _, _, origin in yc_peers:
        arrive(fin_r.at[origin], f_s.at[i], f_r.at[i], sibling)
    for k, out in enumerate((o_in, o_out)):
        total = fin_r[k]
        for yy in range(1, Y):
            total = total + fin_r[yy * CORES + k]
        out[...] = total.astype(BF)

    for op in stores:
        op.wait()


def routing(g, codes, ss, flat):
    n, Z, YC = g.dp, g.Z, g.YC
    c = codes[...].reshape(n, LANES).astype(I32)
    local = (c >> 1) - flat * g.src
    owned = (local >= 0) & (local < g.src)
    loc = local.astype(F32)
    flg = (c & 1).astype(F32)
    ownf = jnp.where(owned, 1.0, 0.0)
    before = lax.broadcasted_iota(I32, (LANES, LANES), 0) < lax.broadcasted_iota(I32, (LANES, LANES), 1)
    rank = jnp.dot(ownf.astype(BF), jnp.where(before, 1.0, 0.0).astype(BF), preferred_element_type=F32)
    lane = lax.broadcasted_iota(I32, (n, LANES), 1).astype(F32)
    wide_lane = lax.broadcasted_iota(I32, (n, 2 * LANES), 1).astype(F32)
    picks = []
    share = jnp.zeros((1, LANES), F32)
    for k in range(SLOTS):
        chosen = jnp.where(rank == float(k), ownf, 0.0)
        idx = jnp.sum(chosen * loc, axis=1, keepdims=True)
        has = jnp.sum(chosen, axis=1, keepdims=True)
        fl = jnp.sum(chosen * flg, axis=1, keepdims=True)
        one = jnp.where(lane == idx, has, 0.0)
        share = share + jnp.sum(one * fl, axis=0, keepdims=True)
        picks.append((idx, has, fl, one))
    for k, (idx, has, fl, one) in enumerate(picks):
        total = jnp.sum(one * share, axis=1, keepdims=True)
        scale = jnp.where(has > 0.0, fl / jnp.where(has > 0.0, total, 1.0), 0.0)
        for kind, (offset, factor) in enumerate(
            ((0.0, has), (float(LANES), scale), (float(LANES + g.R), scale))
        ):
            q = k * 3 + kind
            ss[q * n:(q + 1) * n, :] = jnp.where(wide_lane == idx + offset, factor, 0.0).astype(BF)


def row_parts(g, groups):
    per = 3 * SLOTS
    row = lax.broadcasted_iota(I32, (g.Z * g.M, 1), 0).astype(F32)
    block = jnp.floor((row + 0.5) * (1.0 / g.M))
    rest = row - block * g.M
    inner = jnp.floor((rest + 0.5) * (1.0 / per))
    return block, inner, rest - inner * per, rest < float(groups * per)


def spread_rows(g, spread):
    block, inner, q, valid = row_parts(g, g.YC)
    want = jnp.where(valid, q * g.dp + block * g.YC + inner, -1.0)
    col = lax.broadcasted_iota(I32, spread.shape, 1).astype(F32)
    spread[...] = jnp.where(col == want, 1.0, 0.0).astype(BF)


def regroup_rows(g, regroup):
    block, inner, q, valid = row_parts(g, g.Z)
    want = jnp.where(valid, inner * g.M + block * (3.0 * SLOTS) + q, -1.0)
    col = lax.broadcasted_iota(I32, regroup.shape, 1).astype(F32)
    regroup[...] = jnp.where(col == want, 1.0, 0.0).astype(BF)


def widened(g, code_row, r2):
    src = (code_row >> 1).astype(F32)
    owner = jnp.floor((src + 0.5) * (1.0 / (g.src * g.X)))
    zz = jnp.floor((owner + 0.5) * (1.0 / g.YC))
    first = (owner - zz * g.YC) * g.M + zz * (3.0 * SLOTS)
    sub = lax.broadcasted_iota(I32, (LANES, LANES), 0)
    lane = lax.broadcasted_iota(I32, (LANES, LANES), 1)
    owners = jnp.broadcast_to(owner, (LANES, LANES))
    own_col = jnp.sum(jnp.where(sub == lane, owners, 0.0), axis=1, keepdims=True)
    first_col = jnp.sum(
        jnp.where(sub == lane, jnp.broadcast_to(first, (LANES, LANES)), 0.0), axis=1, keepdims=True
    )
    earlier = jnp.sum(
        jnp.where((owners == own_col) & (lane < sub), 1.0, 0.0), axis=1, keepdims=True
    )
    target = (first_col + 3.0 * earlier)[0:g.W8]
    n = g.YC * g.M
    pos = lax.broadcasted_iota(I32, (g.W8, n), 1).astype(F32)
    columns = r2[...].reshape(n, g.T)
    return [
        jnp.dot(
            jnp.where(pos == target + float(kind), 1.0, 0.0).astype(BF),
            columns, preferred_element_type=F32,
        ).astype(BF)
        for kind in range(3)
    ]


PARTS = 2


def hand_over(n, *refs):
    ins, outs, bufs, (sem_in, sem_out) = refs[:n], refs[n:2 * n], refs[2 * n:3 * n], refs[3 * n:]
    steps = []
    for i in range(n):
        cols = ins[i].shape[1]
        width = cols // PARTS if cols % (PARTS * LANES) == 0 else cols
        for lo in range(0, cols, width):
            k, part = len(steps), (slice(None), pl.ds(lo, width))
            steps.append((
                pltpu.make_async_copy(ins[i].at[part], bufs[i].at[part], sem_in.at[k]),
                pltpu.make_async_copy(bufs[i].at[part], outs[i].at[part], sem_out.at[k]),
            ))
    for fetch, _ in steps:
        fetch.start()
    for fetch, store in steps:
        fetch.wait()
        store.start()
    for _, store in steps:
        store.wait()


def per_device(tokens, grad_out, gate_src, up_src, down_src, unit_map, copy_flag):
    g = Geometry(
        lax.axis_size("dp"), lax.axis_size("mp"), tokens.shape[0], tokens.shape[1],
        gate_src.shape[0], unit_map.shape[0],
    )
    X, Z, YC = g.X, g.Z, g.YC
    V = pltpu.VMEM
    dma = pltpu.SemaphoreType.DMA

    def pair(n):
        return [dma((max(n, 1),)), dma((max(n, 1),))]

    scratch = [
        V((2, g.t, g.cols + LANES), F32), V((YC, g.t, g.cols + LANES), F32), V((g.G, g.cols), F32),
        V((Z, YC, LANES), F32), V((1, LANES), I32),
        V((2, Z, X, g.G, g.a), BF), V((2, X, Z, g.G, g.b), BF),
        V((3, *gate_src.shape), BF), V((2, g.R, g.D), BF), V((4 * g.R, g.D), BF),
        V((4 * g.R, g.T), F32), V((4 * g.R, g.T), F32),
        V((2 * LANES, g.T), F32), V((2 * LANES, g.T), BF), V((g.T, 2 * LANES), BF),
        V((3 * SLOTS * g.dp, 2 * LANES), BF), V((Z * g.M, 3 * SLOTS * g.dp), BF), V((Z * g.M, Z * g.M), BF),
        V((Z * g.M, 2 * LANES), BF),
        V((Z, g.M, g.T), BF), V((Z, g.M, g.T), BF), V((YC, g.M, g.T), BF), V((YC, g.M, g.T), BF),
        V((X, Z, g.G, g.ra), F32), V((X, Z, g.G, g.rb), F32),
        V((g.long, X, g.G, g.ra), BF), V((g.long, X, g.G, g.ra), BF),
        V((g.short, X, g.G, g.ra), BF), V((g.short, X, g.G, g.ra), BF),
        V((X, g.G, g.ra), BF), V((X - 1, g.G, g.ra), BF),
        *[V((Z, g.G, g.rb), BF) for _ in range(6)],
        V((Z - 1, g.G, g.rb), BF), V((Z - 1, g.G, g.rb), BF),
        V((YC, g.t, g.cols), F32), V((YC, g.t, g.cols), F32),
        V((g.wide, g.D), BF), V((g.wide, g.D), BF), V((g.wide, g.D), BF),
        dma((3,)), dma((3,)),
    ]
    counts = [
        YC, Z - 1, X - 1, (Z - 1) * X, Z - 1, 3 * Z, Z, Z, Z - 1, YC, 2, 1,
        (Z - 1) * X, X - 1, 3 * Z, Z - 1, YC,
    ]
    for n in counts:
        scratch += pair(n)
    vm = pl.BlockSpec(memory_space=pltpu.VMEM)
    anyw = pl.BlockSpec(memory_space=pl.ANY)
    wide_shape = jax.ShapeDtypeStruct((g.wide, g.D), BF)
    tok_shape = jax.ShapeDtypeStruct(tokens.shape, BF)
    macs = 6 * g.T * g.src * g.D + 3 * g.T * g.wide * g.D
    results = pl.pallas_call(
        functools.partial(kernel, g),
        out_shape=(tok_shape, tok_shape, wide_shape, wide_shape, wide_shape),
        in_specs=[vm, vm, anyw, anyw, anyw, vm, vm],
        out_specs=(vm, vm, anyw, anyw, anyw),
        scratch_shapes=scratch,
        compiler_params=pltpu.CompilerParams(
            collective_id=0, has_side_effects=True, vmem_limit_bytes=56 * 1024 * 1024
        ),
        cost_estimate=pl.CostEstimate(
            flops=2 * macs, bytes_accessed=3 * 2 * g.D * (g.src + g.wide), transcendentals=g.T * g.src
        ),
        name="widened_layer",
    )(
        tokens, grad_out, gate_src, up_src, down_src,
        unit_map.reshape(1, -1), copy_flag.reshape(1, -1),
    )
    return pl.pallas_call(
        functools.partial(hand_over, len(results)),
        out_shape=tuple(jax.ShapeDtypeStruct(r.shape, r.dtype) for r in results),
        in_specs=[anyw] * len(results),
        out_specs=(anyw,) * len(results),
        scratch_shapes=[V(r.shape, r.dtype) for r in results] + [dma((len(results) * PARTS,))] * 2,
        cost_estimate=pl.CostEstimate(flops=0, bytes_accessed=12 * g.wide * g.D, transcendentals=0),
        name="hand_over",
    )(*results)


def solution(mesh):
    in_specs = (
        P("dp", "mp"),
        P("dp", "mp"),
        P(("dp", "mp"), None),
        P(("dp", "mp"), None),
        P(("dp", "mp"), None),
        P(("dp", "mp")),
        P(("dp", "mp")),
    )
    out_specs = (
        P("dp", "mp"),
        P("dp", "mp"),
        P(("dp", "mp"), None),
        P(("dp", "mp"), None),
        P(("dp", "mp"), None),
    )
    return jax.shard_map(
        per_device, mesh=mesh, in_specs=in_specs, out_specs=out_specs, check_vma=False
    )
```

```python
import functools

import jax
import jax.numpy as jnp
from jax import lax
from jax.experimental import pallas as pl
from jax.experimental.pallas import tpu as pltpu
from jax.sharding import PartitionSpec as P

MESH = pl.DeviceIdType.MESH
BF = jnp.bfloat16
F32 = jnp.float32
I32 = jnp.int32

CORES = 2
CHIPS_Y = 4
SLOTS = 3
LANES = 128


def _mod(v, n):
    return lax.rem(v + n, n)


class Geometry:
    def __init__(self, n_dp, n_mp, tokens_dev, cols, src, wide):
        self.Y = CHIPS_Y
        self.YC = CHIPS_Y * CORES
        self.Z = n_dp // self.YC
        self.X = n_mp
        self.dp = n_dp
        self.t = tokens_dev
        self.T = n_dp * tokens_dev
        self.G = self.YC * tokens_dev
        self.cols = cols
        tiles = cols // LANES
        self.a = (tiles // 2) * LANES
        self.b = cols - self.a
        self.ra = (tiles // 2 + 1) * LANES
        self.rb = cols - self.ra
        self.D = cols * n_mp
        self.src = src
        self.R = -(-src // 16) * 16
        self.wide = wide
        self.W8 = -(-wide // 8) * 8
        self.long = self.Z // 2
        self.short = self.Z - 1 - self.long
        self.M = -(-(self.YC * 3 * SLOTS) // 16) * 16


def kernel(g, *refs):
    (tok, gro, gate_h, up_h, down_h, umap, flag, o_out, o_in, gg_h, gu_h, gd_h) = refs[:12]
    (
        s1_src, s1_rcv, asm, codes, own_code,
        buf_a, buf_b,
        w_own, w_out, ws,
        pre_s, pre_r, lf, lb, lt,
        ss, spread, regroup, sel, msg, r1, m2, r2,
        pa, pb,
        ring_sl, ring_rl, ring_ss, ring_rs, ax_s, ax_r,
        b1_s, b1_r, b2_s, b2_r, bd_s, bd_r, bz_s, bz_r,
        fin_s, fin_r,
        g_gate, g_up, g_down,
        w_sem, o_sem,
        s1_ss, s1_rs, cz_ss, cz_rs, ga_xs, ga_xr, ga_zs, ga_zr, gb_zs, gb_zr, gb_xs, gb_xr,
        sa_s, sa_r, sb_s, sb_r,
        m1_s, m1_r, m2_s, m2_r,
        wx_s, wx_r, px_s, px_r,
        rz_s, rz_r, axx_s, axx_r, bxx_s, bxx_r, bzz_s, bzz_r, f_s, f_r,
    ) = refs[12:]
    X, Y, Z, YC = g.X, g.Y, g.Z, g.YC
    dp = lax.axis_index("dp")
    x = lax.axis_index("mp")
    z = lax.div(dp, YC)
    yc = lax.rem(dp, YC)
    y = lax.div(yc, CORES)
    c = lax.rem(yc, CORES)
    other = 1 - c
    step = 1 - 2 * c

    def at_z(zz):
        return (zz * YC + yc, x)

    def at_x(xx):
        return (dp, xx)

    def at_yc(k):
        return (z * YC + k, x)

    sibling = at_yc(y * CORES + other)
    yc_peers = []
    for dy in range(Y):
        for dc in range(CORES):
            if dy or dc:
                py = _mod(y + dy, Y)
                pc = _mod(c + dc, CORES)
                qy = _mod(y - dy, Y)
                yc_peers.append((dy * CORES + dc, py * CORES + pc, pc, qy * CORES + pc))

    sent = []

    def copy(src, dst, s_sem, r_sem, device):
        return pltpu.make_async_remote_copy(
            src_ref=src, dst_ref=dst, send_sem=s_sem, recv_sem=r_sem,
            device_id=device, device_id_type=MESH,
        )

    def send(src, dst, s_sem, r_sem, device):
        op = copy(src, dst, s_sem, r_sem, device)
        op.start()
        sent.append(op)

    def arrive(dst, s_sem, r_sem, device):
        copy(dst, dst, s_sem, r_sem, device).wait_recv()

    bar = pltpu.get_barrier_semaphore()
    for k in range(1, X):
        pl.semaphore_signal(bar, inc=1, device_id=at_x(_mod(x + k, X)), device_id_type=MESH)
    for k in range(1, Z):
        pl.semaphore_signal(bar, inc=1, device_id=at_z(_mod(z + k, Z)), device_id_type=MESH)
    for _, peer, _, _ in yc_peers:
        pl.semaphore_signal(bar, inc=1, device_id=at_yc(peer), device_id_type=MESH)

    loads = [
        pltpu.make_async_copy(h, w_own.at[i], w_sem.at[i])
        for i, h in enumerate((gate_h, up_h, down_h))
    ]
    for op in loads:
        op.start()

    code = umap[...] * 2 + flag[...]
    own_code[...] = jnp.full(own_code.shape, -1, I32)
    own_code[:, 0:g.wide] = code
    code_row = own_code[...]
    s1_src[0, :, 0:g.cols] = tok[...].astype(F32)
    s1_src[1, :, 0:g.cols] = gro[...].astype(F32)
    for k in range(2):
        s1_src[k, :, g.cols:g.cols + LANES] = jnp.broadcast_to(code_row.astype(F32), (g.t, LANES))
    s1_rcv[yc] = s1_src[c]

    pl.semaphore_wait(bar, (X - 1) + (Z - 1) + len(yc_peers))

    for i, peer, pc, _ in yc_peers:
        send(s1_src.at[pc], s1_rcv.at[yc], s1_ss.at[i], s1_rs.at[i], at_yc(peer))
    for i, _, _, origin in yc_peers:
        arrive(s1_rcv.at[origin], s1_ss.at[i], s1_rs.at[i], sibling)
    for k in range(YC):
        asm[k * g.t:(k + 1) * g.t, :] = s1_rcv[k, :, 0:g.cols]
        codes[z, k:k + 1, :] = s1_rcv[k, 0:1, g.cols:g.cols + LANES]
    block = asm[...].astype(BF)
    buf_a[c, z, x] = block[:, 0:g.a]
    buf_b[c, x, z] = block[:, g.a:g.cols]

    right, left = at_z(_mod(z + step, Z)), at_z(_mod(z - step, Z))
    a_cols = [x] + [_mod(x - k, X) for k in range(1, X)]

    def slots_at(hop):
        out = [(hop, _mod(z - hop * step, Z))]
        if 1 <= hop <= g.short:
            out.append((g.long + hop, _mod(z + hop * step, Z)))
        return out

    def a_forward(hop, j):
        if hop < g.long:
            ref = buf_a.at[c, _mod(z - hop * step, Z), a_cols[j]]
            i = hop * X + j
            send(ref, ref, ga_zs.at[i], ga_zr.at[i], right)
        if hop < g.short:
            ref = buf_a.at[c, _mod(z + hop * step, Z), a_cols[j]]
            i = (g.long + hop) * X + j
            send(ref, ref, ga_zs.at[i], ga_zr.at[i], left)

    def a_arrive(hop, j):
        i = (hop - 1) * X + j
        arrive(buf_a.at[c, _mod(z - hop * step, Z), a_cols[j]], ga_zs.at[i], ga_zr.at[i], sibling)
        if hop <= g.short:
            i = (g.long + hop - 1) * X + j
            arrive(buf_a.at[c, _mod(z + hop * step, Z), a_cols[j]], ga_zs.at[i], ga_zr.at[i], sibling)

    def b_forward(hop):
        if hop < g.long:
            ref = buf_b.at[c, x, _mod(z - hop * step, Z)]
            send(ref, ref, gb_zs.at[hop], gb_zr.at[hop], right)
        if hop < g.short:
            ref = buf_b.at[c, x, _mod(z + hop * step, Z)]
            i = g.long + hop
            send(ref, ref, gb_zs.at[i], gb_zr.at[i], left)

    def b_arrive(hop):
        arrive(buf_b.at[c, x, _mod(z - hop * step, Z)], gb_zs.at[hop - 1], gb_zr.at[hop - 1], sibling)
        if hop <= g.short:
            i = g.long + hop - 1
            arrive(buf_b.at[c, x, _mod(z + hop * step, Z)], gb_zs.at[i], gb_zr.at[i], sibling)

    x_up, x_down, x_far = _mod(x + 1, X), _mod(x - 1, X), _mod(x + 2, X)

    def b_across(i, b, last=False):
        ref = buf_b.at[c, x, b]
        if last:
            send(ref, ref, gb_xs.at[3 * i + 2], gb_xr.at[3 * i + 2], at_x(x_far))
        send(ref, ref, gb_xs.at[3 * i], gb_xr.at[3 * i], at_x(x_up))
        send(ref, ref, gb_xs.at[3 * i + 1], gb_xr.at[3 * i + 1], at_x(x_down))

    def b_beside(i, b):
        arrive(buf_b.at[c, x_down, b], gb_xs.at[3 * i], gb_xr.at[3 * i], sibling)
        arrive(buf_b.at[c, x_up, b], gb_xs.at[3 * i + 1], gb_xr.at[3 * i + 1], sibling)

    def b_pass_on(i, b):
        b_beside(i, b)
        way = 1 - 2 * lax.rem(b, 2)
        ref = buf_b.at[c, _mod(x - way, X), b]
        send(ref, ref, gb_xs.at[3 * i + 2], gb_xr.at[3 * i + 2], at_x(_mod(x + way, X)))

    def b_share(i, b):
        arrive(buf_b.at[c, x_far, b], gb_xs.at[3 * i + 2], gb_xr.at[3 * i + 2], sibling)
        ref = buf_b.at[c, :, b]
        send(ref, ref, sb_s.at[i], sb_r.at[i], sibling)

    def a_share(i, b):
        ref = buf_a.at[c, b]
        send(ref, ref, sa_s.at[i], sa_r.at[i], sibling)

    b_forward(0)
    for k in range(1, X):
        ref = buf_a.at[c, z, x]
        send(ref, ref, ga_xs.at[k - 1], ga_xr.at[k - 1], at_x(_mod(x + k, X)))
    a_forward(0, 0)
    b_across(0, z)
    for k in range(1, Z):
        send(codes.at[z], codes.at[z], cz_ss.at[k - 1], cz_rs.at[k - 1], at_z(_mod(z + k, Z)))

    for op in loads:
        op.wait()
    if g.R > g.src:
        pad = jnp.zeros((16, g.D), BF)
        w_out[0, g.R - 16:g.R, :] = pad
        w_out[1, g.R - 16:g.R, :] = pad
        ws[g.R - 16:g.R, :] = pad
        ws[3 * g.R - 16:3 * g.R, :] = pad
    w_out[0, 0:g.src, :] = w_own[2 * other]
    w_out[1, 0:g.src, :] = w_own[1]
    for k in range(2):
        rows = ws.at[pl.ds((2 * k + 1) * g.R, g.R)]
        send(w_out.at[k], rows, wx_s.at[k], wx_r.at[k], sibling)
    ws[0:g.src, :] = w_own[2 * c]
    ws[2 * g.R:2 * g.R + g.src, :] = w_own[1]
    spread_rows(g, spread)

    for k in (1, X - 1, *range(2, X - 1)):
        arrive(buf_a.at[c, z, _mod(x - k, X)], ga_xs.at[k - 1], ga_xr.at[k - 1], sibling)
        a_forward(0, k)
    a_share(0, z)
    for hop in range(1, g.long + 1):
        b_arrive(hop)
        b_forward(hop)
        for i, b in slots_at(hop):
            b_across(i, b, last=hop == g.long)
        for i, b in slots_at(hop - 1):
            b_pass_on(i, b)
        for j in (0, 1, X - 1, *range(2, X - 1)):
            a_arrive(hop, j)
            a_forward(hop, j)
        for i, b in slots_at(hop):
            a_share(i, b)
        if hop > 1:
            for i, b in slots_at(hop - 2):
                b_share(i, b)
    for k in range(1, Z):
        arrive(codes.at[_mod(z - k, Z)], cz_ss.at[k - 1], cz_rs.at[k - 1], sibling)
    routing(g, codes, ss, dp * X + x)
    for i, b in slots_at(g.long):
        b_beside(i, b)
    for hop in (g.long - 1, g.long):
        for i, b in slots_at(hop):
            b_share(i, b)
    sel[...] = jnp.dot(spread[...], ss[...], preferred_element_type=F32).astype(BF)
    regroup_rows(g, regroup)

    nt = (((1,), (1,)), ((), ()))

    def rows_a(array, xx):
        return buf_a[array, :, xx].reshape(g.T, g.a)

    def rows_b(array, xx):
        return buf_b[array, xx].reshape(g.T, g.b)

    for k in range(2):
        rows = ws.at[pl.ds((2 * k + 1) * g.R, g.R)]
        arrive(rows, wx_s.at[k], wx_r.at[k], sibling)
    pre = jnp.zeros((4 * g.R, g.T), F32)
    for xx in range(X):
        lo, mid, hi = xx * g.cols, xx * g.cols + g.a, (xx + 1) * g.cols
        pre += lax.dot_general(ws[:, lo:mid], rows_a(c, xx), nt, preferred_element_type=F32)
        pre += lax.dot_general(ws[:, mid:hi], rows_b(c, xx), nt, preferred_element_type=F32)
    pre_s[...] = pre
    send(pre_s, pre_r, px_s.at[0], px_r.at[0], sibling)
    arrive(pre_r, px_s.at[0], px_r.at[0], sibling)

    def turned(lo):
        return jnp.concatenate([pre_r[lo + g.R:lo + 2 * g.R], pre_r[lo:lo + g.R]], axis=0)

    first = c == 0
    pre_gate = jnp.where(first, pre_s[0:2 * g.R], turned(0))
    pre_up = jnp.where(first, pre_s[2 * g.R:4 * g.R], turned(2 * g.R))
    gh = jnp.where(first, turned(0), pre_s[0:2 * g.R])
    sigma = jax.nn.sigmoid(pre_gate)
    active = pre_gate * sigma
    hidden = active * pre_up
    d_gate = gh * pre_up * (sigma + active * (1.0 - sigma))
    d_up = gh * active
    lf[...] = jnp.zeros(lf.shape, F32)
    lf[0:2 * g.R, :] = jnp.where(first, d_gate, hidden)
    lf[2 * g.R:4 * g.R, :] = jnp.where(first, d_up, 0.0)
    for k in range(2):
        lt[:, k * LANES:(k + 1) * LANES] = lf[k * LANES:(k + 1) * LANES, :].T.astype(BF)
    lf[...] = jnp.zeros(lf.shape, F32)
    lf[0:g.R, :] = hidden[0:g.R]
    lf[LANES:LANES + g.R, :] = d_gate[0:g.R]
    lf[LANES + g.R:LANES + 2 * g.R, :] = d_up[0:g.R]
    lb[...] = lf[...].astype(BF)

    def partial(lo, width):
        return jnp.dot(lt[:, 0:4 * g.R], ws[:, pl.ds(lo, width)], preferred_element_type=F32)

    def own_a(b, xx):
        return pa[xx, b]

    def reduce_a(hop, xx):
        if hop < g.long:
            v = own_a(_mod(z + (g.long - hop) * step, Z), xx)
            if hop:
                i = (hop - 1) * X + xx
                arrive(ring_rl.at[hop - 1, xx], rz_s.at[i], rz_r.at[i], sibling)
                v = v + ring_rl[hop - 1, xx].astype(F32)
            ring_sl[hop, xx] = v.astype(BF)
            i = hop * X + xx
            send(ring_sl.at[hop, xx], ring_rl.at[hop, xx], rz_s.at[i], rz_r.at[i], right)
        if hop < g.short:
            v = own_a(_mod(z - (g.short - hop) * step, Z), xx)
            if hop:
                i = (g.long + hop - 1) * X + xx
                arrive(ring_rs.at[hop - 1, xx], rz_s.at[i], rz_r.at[i], sibling)
                v = v + ring_rs[hop - 1, xx].astype(F32)
            ring_ss[hop, xx] = v.astype(BF)
            i = (g.long + hop) * X + xx
            send(ring_ss.at[hop, xx], ring_rs.at[hop, xx], rz_s.at[i], rz_r.at[i], left)

    b_long = [(h, _mod(z + (g.long - h) * step, Z)) for h in range(g.long)]
    b_short = [(g.long + h, _mod(z - (g.short - h) * step, Z)) for h in range(g.short)]
    b_own = (Z - 1, z)
    b_order = []
    for h in range(g.long):
        b_order.append(b_long[h])
        if h < g.short:
            b_order.append(b_short[h])
    b_order.append(b_own)

    def way_of(b):
        return 1 - 2 * lax.rem(b, 2)

    def b_first(i, b):
        b1_s[i] = pb[x_far, b].astype(BF)
        send(b1_s.at[i], b1_r.at[i], bxx_s.at[3 * i], bxx_r.at[3 * i], at_x(_mod(x + way_of(b), X)))

    def b_direct(i, b):
        to = _mod(x - way_of(b), X)
        bd_s[i] = pb[to, b].astype(BF)
        send(bd_s.at[i], bd_r.at[i], bxx_s.at[3 * i + 1], bxx_r.at[3 * i + 1], at_x(to))

    def b_second(i, b):
        to = _mod(x + way_of(b), X)
        arrive(b1_r.at[i], bxx_s.at[3 * i], bxx_r.at[3 * i], sibling)
        b2_s[i] = (pb[to, b] + b1_r[i].astype(F32)).astype(BF)
        send(b2_s.at[i], b2_r.at[i], bxx_s.at[3 * i + 2], bxx_r.at[3 * i + 2], at_x(to))

    def b_sum(i, b):
        arrive(bd_r.at[i], bxx_s.at[3 * i + 1], bxx_r.at[3 * i + 1], sibling)
        arrive(b2_r.at[i], bxx_s.at[3 * i + 2], bxx_r.at[3 * i + 2], sibling)
        return pb[x, b] + bd_r[i].astype(F32) + b2_r[i].astype(F32)

    def reduce_b(hop):
        for chain, to, n in ((b_long, right, g.long), (b_short, left, g.short)):
            if hop < n:
                i, b = chain[hop]
                v = b_sum(i, b)
                if hop:
                    arrive(bz_r.at[i - 1], bzz_s.at[i - 1], bzz_r.at[i - 1], sibling)
                    v = v + bz_r[i - 1].astype(F32)
                bz_s[i] = v.astype(BF)
                send(bz_s.at[i], bz_r.at[i], bzz_s.at[i], bzz_r.at[i], to)

    order = [x_far, x_up, x_down, x]

    def chip_b(k):
        lo = pl.multiple_of(order[k] * g.cols + g.ra, LANES)
        pb[order[k]] = partial(lo, g.rb).reshape(Z, g.G, g.rb)

    picked = jnp.dot(sel[...], lb[...], preferred_element_type=F32).astype(BF)
    msg[...] = picked.reshape(Z, g.M, g.T)
    r1[z] = msg[z]
    for k in range(1, Z):
        zz = _mod(z + k, Z)
        send(msg.at[zz], r1.at[z], m1_s.at[k - 1], m1_r.at[k - 1], at_z(zz))
    chip_b(0)
    for i, b in b_order:
        b_first(i, b)
    chip_b(1)
    chip_b(2)
    for i, b in b_order:
        b_direct(i, b)
    for xx in range(X):
        pa[xx] = partial(xx * g.cols, g.ra).reshape(Z, g.G, g.ra)
        reduce_a(0, xx)
    chip_b(3)
    half = Z // 2
    for i, b in b_order[0:half]:
        b_second(i, b)
    for xx in range(X):
        reduce_a(1, xx)
    for i, b in b_order[half:]:
        b_second(i, b)
    reduce_b(0)

    for xx in range(X):
        reduce_a(2, xx)
    reduce_b(1)
    for xx in range(X):
        reduce_a(3, xx)
    reduce_b(2)
    for k in range(1, Z):
        arrive(r1.at[_mod(z - k, Z)], m1_s.at[k - 1], m1_r.at[k - 1], sibling)
    m2[...] = jnp.dot(
        regroup[...], r1[...].reshape(Z * g.M, g.T), preferred_element_type=F32
    ).astype(BF).reshape(YC, g.M, g.T)
    r2[yc] = m2[yc]
    for i, peer, _, _ in yc_peers:
        send(m2.at[peer], r2.at[yc], m2_s.at[i], m2_r.at[i], at_yc(peer))

    for xx in range(X):
        v = own_a(z, xx)
        i = (g.long - 1) * X + xx
        arrive(ring_rl.at[g.long - 1, xx], rz_s.at[i], rz_r.at[i], sibling)
        v = v + ring_rl[g.long - 1, xx].astype(F32)
        i = (g.long + g.short - 1) * X + xx
        arrive(ring_rs.at[g.short - 1, xx], rz_s.at[i], rz_r.at[i], sibling)
        v = v + ring_rs[g.short - 1, xx].astype(F32)
        pa[xx, z] = v
        ax_s[xx] = v.astype(BF)
    for k in range(1, X):
        xx = _mod(x + k, X)
        send(ax_s.at[xx], ax_r.at[k - 1], axx_s.at[k - 1], axx_r.at[k - 1], at_x(xx))
    reduce_b(3)

    va = pa[x, z]
    for k in range(1, X):
        arrive(ax_r.at[k - 1], axx_s.at[k - 1], axx_r.at[k - 1], sibling)
        va = va + ax_r[k - 1].astype(F32)
    vb = b_sum(*b_own)
    for i in (g.long - 1, g.long + g.short - 1):
        arrive(bz_r.at[i], bzz_s.at[i], bzz_r.at[i], sibling)
        vb = vb + bz_r[i].astype(F32)
    for k in range(YC):
        fin_s[k, :, 0:g.ra] = va[k * g.t:(k + 1) * g.t]
        fin_s[k, :, g.ra:g.cols] = vb[k * g.t:(k + 1) * g.t]
    fin_r[yc] = fin_s[yc]
    for i, peer, _, _ in yc_peers:
        send(fin_s.at[peer], fin_r.at[yc], f_s.at[i], f_r.at[i], at_yc(peer))

    for i in range(Z):
        hop = i if i <= g.long else g.long - i
        b = _mod(z + hop * step, Z)
        arrive(buf_a.at[other, b], sa_s.at[i], sa_r.at[i], sibling)
        arrive(buf_b.at[other, :, b], sb_s.at[i], sb_r.at[i], sibling)

    for i, _, _, origin in yc_peers:
        arrive(r2.at[origin], m2_s.at[i], m2_r.at[i], sibling)
    wide = widened(g, own_code[...], r2)
    g_rows = jnp.concatenate([wide[1], wide[2]], axis=0)
    for xx in range(X):
        for lo, width, rows in (
            (xx * g.cols, g.a, rows_a),
            (xx * g.cols + g.a, g.b, rows_b),
        ):
            both = jnp.dot(g_rows, rows(0, xx), preferred_element_type=F32).astype(BF)
            g_gate[:, lo:lo + width] = both[0:g.wide]
            g_up[:, lo:lo + width] = both[g.W8:g.W8 + g.wide]
            down = jnp.dot(wide[0], rows(1, xx), preferred_element_type=F32).astype(BF)
            g_down[:, lo:lo + width] = down[0:g.wide]
    stores = [
        pltpu.make_async_copy(v, h, o_sem.at[i])
        for i, (v, h) in enumerate(((g_gate, gg_h), (g_up, gu_h), (g_down, gd_h)))
    ]
    for op in stores:
        op.start()

    for op in sent:
        op.wait_send()
    for i, _, _, origin in yc_peers:
        arrive(fin_r.at[origin], f_s.at[i], f_r.at[i], sibling)
    for k, out in enumerate((o_in, o_out)):
        total = fin_r[k]
        for yy in range(1, Y):
            total = total + fin_r[yy * CORES + k]
        out[...] = total.astype(BF)

    for op in stores:
        op.wait()


def routing(g, codes, ss, flat):
    n, Z, YC = g.dp, g.Z, g.YC
    c = codes[...].reshape(n, LANES).astype(I32)
    local = (c >> 1) - flat * g.src
    owned = (local >= 0) & (local < g.src)
    loc = local.astype(F32)
    flg = (c & 1).astype(F32)
    ownf = jnp.where(owned, 1.0, 0.0)
    before = lax.broadcasted_iota(I32, (LANES, LANES), 0) < lax.broadcasted_iota(I32, (LANES, LANES), 1)
    rank = jnp.dot(ownf.astype(BF), jnp.where(before, 1.0, 0.0).astype(BF), preferred_element_type=F32)
    lane = lax.broadcasted_iota(I32, (n, LANES), 1).astype(F32)
    wide_lane = lax.broadcasted_iota(I32, (n, 2 * LANES), 1).astype(F32)
    picks = []
    share = jnp.zeros((1, LANES), F32)
    for k in range(SLOTS):
        chosen = jnp.where(rank == float(k), ownf, 0.0)
        idx = jnp.sum(chosen * loc, axis=1, keepdims=True)
        has = jnp.sum(chosen, axis=1, keepdims=True)
        fl = jnp.sum(chosen * flg, axis=1, keepdims=True)
        one = jnp.where(lane == idx, has, 0.0)
        share = share + jnp.sum(one * fl, axis=0, keepdims=True)
        picks.append((idx, has, fl, one))
    for k, (idx, has, fl, one) in enumerate(picks):
        total = jnp.sum(one * share, axis=1, keepdims=True)
        scale = jnp.where(has > 0.0, fl / jnp.where(has > 0.0, total, 1.0), 0.0)
        for kind, (offset, factor) in enumerate(
            ((0.0, has), (float(LANES), scale), (float(LANES + g.R), scale))
        ):
            q = k * 3 + kind
            ss[q * n:(q + 1) * n, :] = jnp.where(wide_lane == idx + offset, factor, 0.0).astype(BF)


def row_parts(g, groups):
    per = 3 * SLOTS
    row = lax.broadcasted_iota(I32, (g.Z * g.M, 1), 0).astype(F32)
    block = jnp.floor((row + 0.5) * (1.0 / g.M))
    rest = row - block * g.M
    inner = jnp.floor((rest + 0.5) * (1.0 / per))
    return block, inner, rest - inner * per, rest < float(groups * per)


def spread_rows(g, spread):
    block, inner, q, valid = row_parts(g, g.YC)
    want = jnp.where(valid, q * g.dp + block * g.YC + inner, -1.0)
    col = lax.broadcasted_iota(I32, spread.shape, 1).astype(F32)
    spread[...] = jnp.where(col == want, 1.0, 0.0).astype(BF)


def regroup_rows(g, regroup):
    block, inner, q, valid = row_parts(g, g.Z)
    want = jnp.where(valid, inner * g.M + block * (3.0 * SLOTS) + q, -1.0)
    col = lax.broadcasted_iota(I32, regroup.shape, 1).astype(F32)
    regroup[...] = jnp.where(col == want, 1.0, 0.0).astype(BF)


def widened(g, code_row, r2):
    src = (code_row >> 1).astype(F32)
    owner = jnp.floor((src + 0.5) * (1.0 / (g.src * g.X)))
    zz = jnp.floor((owner + 0.5) * (1.0 / g.YC))
    first = (owner - zz * g.YC) * g.M + zz * (3.0 * SLOTS)
    sub = lax.broadcasted_iota(I32, (LANES, LANES), 0)
    lane = lax.broadcasted_iota(I32, (LANES, LANES), 1)
    owners = jnp.broadcast_to(owner, (LANES, LANES))
    own_col = jnp.sum(jnp.where(sub == lane, owners, 0.0), axis=1, keepdims=True)
    first_col = jnp.sum(
        jnp.where(sub == lane, jnp.broadcast_to(first, (LANES, LANES)), 0.0), axis=1, keepdims=True
    )
    earlier = jnp.sum(
        jnp.where((owners == own_col) & (lane < sub), 1.0, 0.0), axis=1, keepdims=True
    )
    target = (first_col + 3.0 * earlier)[0:g.W8]
    n = g.YC * g.M
    pos = lax.broadcasted_iota(I32, (g.W8, n), 1).astype(F32)
    columns = r2[...].reshape(n, g.T)
    return [
        jnp.dot(
            jnp.where(pos == target + float(kind), 1.0, 0.0).astype(BF),
            columns, preferred_element_type=F32,
        ).astype(BF)
        for kind in range(3)
    ]


PARTS = 2


def hand_over(n, *refs):
    ins, outs, bufs, (sem_in, sem_out) = refs[:n], refs[n:2 * n], refs[2 * n:3 * n], refs[3 * n:]
    steps = []
    for i in range(n):
        cols = ins[i].shape[1]
        width = cols // PARTS if cols % (PARTS * LANES) == 0 else cols
        for lo in range(0, cols, width):
            k, part = len(steps), (slice(None), pl.ds(lo, width))
            steps.append((
                pltpu.make_async_copy(ins[i].at[part], bufs[i].at[part], sem_in.at[k]),
                pltpu.make_async_copy(bufs[i].at[part], outs[i].at[part], sem_out.at[k]),
            ))
    for fetch, _ in steps:
        fetch.start()
    for fetch, store in steps:
        fetch.wait()
        store.start()
    for _, store in steps:
        store.wait()


def per_device(tokens, grad_out, gate_src, up_src, down_src, unit_map, copy_flag):
    g = Geometry(
        lax.axis_size("dp"), lax.axis_size("mp"), tokens.shape[0], tokens.shape[1],
        gate_src.shape[0], unit_map.shape[0],
    )
    X, Z, YC = g.X, g.Z, g.YC
    V = pltpu.VMEM
    dma = pltpu.SemaphoreType.DMA

    def pair(n):
        return [dma((max(n, 1),)), dma((max(n, 1),))]

    scratch = [
        V((2, g.t, g.cols + LANES), F32), V((YC, g.t, g.cols + LANES), F32), V((g.G, g.cols), F32),
        V((Z, YC, LANES), F32), V((1, LANES), I32),
        V((2, Z, X, g.G, g.a), BF), V((2, X, Z, g.G, g.b), BF),
        V((3, *gate_src.shape), BF), V((2, g.R, g.D), BF), V((4 * g.R, g.D), BF),
        V((4 * g.R, g.T), F32), V((4 * g.R, g.T), F32),
        V((2 * LANES, g.T), F32), V((2 * LANES, g.T), BF), V((g.T, 2 * LANES), BF),
        V((3 * SLOTS * g.dp, 2 * LANES), BF), V((Z * g.M, 3 * SLOTS * g.dp), BF), V((Z * g.M, Z * g.M), BF),
        V((Z * g.M, 2 * LANES), BF),
        V((Z, g.M, g.T), BF), V((Z, g.M, g.T), BF), V((YC, g.M, g.T), BF), V((YC, g.M, g.T), BF),
        V((X, Z, g.G, g.ra), F32), V((X, Z, g.G, g.rb), F32),
        V((g.long, X, g.G, g.ra), BF), V((g.long, X, g.G, g.ra), BF),
        V((g.short, X, g.G, g.ra), BF), V((g.short, X, g.G, g.ra), BF),
        V((X, g.G, g.ra), BF), V((X - 1, g.G, g.ra), BF),
        *[V((Z, g.G, g.rb), BF) for _ in range(6)],
        V((Z - 1, g.G, g.rb), BF), V((Z - 1, g.G, g.rb), BF),
        V((YC, g.t, g.cols), F32), V((YC, g.t, g.cols), F32),
        V((g.wide, g.D), BF), V((g.wide, g.D), BF), V((g.wide, g.D), BF),
        dma((3,)), dma((3,)),
    ]
    counts = [
        YC, Z - 1, X - 1, (Z - 1) * X, Z - 1, 3 * Z, Z, Z, Z - 1, YC, 2, 1,
        (Z - 1) * X, X - 1, 3 * Z, Z - 1, YC,
    ]
    for n in counts:
        scratch += pair(n)
    vm = pl.BlockSpec(memory_space=pltpu.VMEM)
    anyw = pl.BlockSpec(memory_space=pl.ANY)
    wide_shape = jax.ShapeDtypeStruct((g.wide, g.D), BF)
    tok_shape = jax.ShapeDtypeStruct(tokens.shape, BF)
    macs = 6 * g.T * g.src * g.D + 3 * g.T * g.wide * g.D
    results = pl.pallas_call(
        functools.partial(kernel, g),
        out_shape=(tok_shape, tok_shape, wide_shape, wide_shape, wide_shape),
        in_specs=[vm, vm, anyw, anyw, anyw, vm, vm],
        out_specs=(vm, vm, anyw, anyw, anyw),
        scratch_shapes=scratch,
        compiler_params=pltpu.CompilerParams(
            collective_id=0, has_side_effects=True, vmem_limit_bytes=56 * 1024 * 1024
        ),
        cost_estimate=pl.CostEstimate(
            flops=2 * macs, bytes_accessed=3 * 2 * g.D * (g.src + g.wide), transcendentals=g.T * g.src
        ),
        name="widened_layer",
    )(
        tokens, grad_out, gate_src, up_src, down_src,
        unit_map.reshape(1, -1), copy_flag.reshape(1, -1),
    )
    return pl.pallas_call(
        functools.partial(hand_over, len(results)),
        out_shape=tuple(jax.ShapeDtypeStruct(r.shape, r.dtype) for r in results),
        in_specs=[anyw] * len(results),
        out_specs=(anyw,) * len(results),
        scratch_shapes=[V(r.shape, r.dtype) for r in results] + [dma((len(results) * PARTS,))] * 2,
        cost_estimate=pl.CostEstimate(flops=0, bytes_accessed=12 * g.wide * g.D, transcendentals=0),
        name="hand_over",
    )(*results)


def solution(mesh):
    in_specs = (
        P("dp", "mp"),
        P("dp", "mp"),
        P(("dp", "mp"), None),
        P(("dp", "mp"), None),
        P(("dp", "mp"), None),
        P(("dp", "mp")),
        P(("dp", "mp")),
    )
    out_specs = (
        P("dp", "mp"),
        P("dp", "mp"),
        P(("dp", "mp"), None),
        P(("dp", "mp"), None),
        P(("dp", "mp"), None),
    )
    return jax.shard_map(
        per_device, mesh=mesh, in_specs=in_specs, out_specs=out_specs, check_vma=False
    )
```
